32 devices in a mesh: tm: 8 (over y, x, core), bl: 4 (over z).
Axes of the slice: x: 2, y: 2, z: 4, core: 2. Of those that a mesh axis runs over, the one named last changes fastest.
Arguments:
- visibilities: bfloat16 [16384, 2, 240], P(('tm', 'bl')), may hold values from -12 to 12
- noise_weight: float32 [16384], P(('tm', 'bl')), may hold values from 0.005 to 0.05
- keep_flag: int32 [16384], P(('tm', 'bl')), may hold values 0 or 1
- station_pairs: int32 [2, 16384], P(None, ('tm', 'bl')), may hold values from 0 to 63, as said below
- tile_owner: int32 [16384, 1], P(('tm', 'bl')), may hold values from 0 to 31; in each aligned block of 512 rows (0 to 511, 512 to 1023, ...) at most 32 rows name the same one
- tile_offset: int32 [16384], P(('tm', 'bl')), may hold values from 0 to 131064
- kernel_taps: float32 [8, 16384], P(None, ('tm', 'bl')), may hold values from 0.1 to 1
- gain_field: float32 [8, 64, 8, 2, 240], P('tm', 'bl'), may hold values from 0.25 to 1.75
- sky_grid: float32 [2, 8, 2, 4194304], P(None, None, None, ('tm', 'bl')), may hold values from -4 to 4
Outputs:
- gain_gradient: float32 [8, 64, 8, 2, 240], P('tm', 'bl')
- grid_gradient: float32 [2, 8, 2, 4194304], P(None, None, None, ('tm', 'bl'))
The draws below stay inside these ranges and needn't reach their ends.
Inputs may be any that keep to these rules, and one draw needn't show every extreme that they name: `station_pairs`: the two stations of a row differ. `tile_owner`: among the rows of one device no value appears more than 32 times, and in some device one appears exactly 32 times.
All inputs are finite; a program needn't handle non-finite values. No bound on the sum of `keep_flag` on one device may be relied on, other than what follows from the above.
Results may differ from the reference program's by a relative error of at most 0.0003.
Values sent between devices are 32-bit elements; how exact they have to be, the bound alone decides.
No kernel may reach another device: no remote copies, remote signals or barrier semaphores. Data moves between devices by JAX's collectives and lax.ppermute only.
A program may use at most 192 MiB of HBM per device.

```python
import math
import jax
import jax.numpy as jnp
import numpy as np
from jax import lax

S = 64
F = 8
C = 240
NT = 2
KT = 8
GRID = 4194304
ROWS_DEV = 512
NSOL = 8
ROWS_SOL = 2048
ROWS = 16384
GRID_DEV = 131072
CAP = 32
N_TM = 8
DEVICES = 32


def draw_station_pairs(key, part):
    first_key, second_key = jax.random.split(jax.random.fold_in(key, 11))
    first_station = jax.random.randint(first_key, (ROWS,), 0, S)
    offset = jax.random.randint(second_key, (ROWS,), 1, S)
    second_station = (first_station + offset) % S
    return jnp.stack([first_station, second_station]).astype(jnp.int32)


def plant(drawn, key, least, top_value):
    shape = drawn.shape
    spot = [jax.random.randint(jax.random.fold_in(key, axis), (), 0, shape[axis]) for axis in range(len(shape))]
    drawn = drawn.at[tuple(spot)].set(least)
    longest = shape.index(max(shape))
    spot[longest] = (spot[longest] + 1) % shape[longest]
    return drawn.at[tuple(spot)].set(top_value)


def level_of(own_key, shape, pieces, low, top_value):
    def one(dim, parts):
        steps = jax.random.uniform(jax.random.fold_in(jax.random.fold_in(own_key, 6), dim), (parts,), jnp.float32, low / len(pieces), top_value / len(pieces))
        return jnp.repeat(jnp.exp(steps), shape[dim] // parts).reshape((-1,) + (1,) * (len(shape) - dim - 1))

    factor_of = one(*pieces[0])
    for cut in pieces[1:]:
        factor_of = factor_of * one(*cut)
    return factor_of


def deal_out(key, own, number, rows, amount, top, most, skew):
    sequence = jax.random.permutation(key, amount)
    packed, usual = load_shares(amount, rows * top, most, skew, True), load_shares(amount, rows * top, most, skew, False)
    places = jnp.arange(amount)

    def named(sizes, turn):
        used = int((sizes > 0).sum())
        fixed = max(1, used // 4)
        passed = fixed + (places - fixed + turn * (used - fixed)) % max(1, amount - fixed)
        return jnp.zeros((amount,), jnp.int32).at[sequence[jnp.where(places < fixed, places, passed)]].set(jnp.asarray(sizes, jnp.int32))

    sizes = jnp.where(number % 4 == 0, named(packed, number // 4), named(usual, number - number // 4 - 1))
    mixed = jax.random.permutation(jax.random.fold_in(own, 3), amount)
    source_of, taker = mixed[0:amount // 2 * 2:2], mixed[1:amount // 2 * 2:2]
    slack = jnp.minimum(sizes[source_of] - 1, most - sizes[taker]) // 2
    slack = jnp.where((source_of == sequence[0]) | (taker == sequence[0]) | (sizes[taker] == 0), 0, jnp.maximum(slack, 0))
    passed = jax.random.randint(jax.random.fold_in(own, 4), (amount // 2,), 0, 1 << 20) % (slack + 1)
    sizes = sizes.at[source_of].add(-passed).at[taker].add(passed)
    items = jnp.searchsorted(jnp.cumsum(sizes), jnp.arange(rows * top), side="right").astype(jnp.int32)
    table = items.reshape(top, rows).T
    table = table[jax.random.permutation(jax.random.fold_in(own, 1), rows)]
    turn = jax.random.randint(jax.random.fold_in(own, 2), (rows, 1), 0, top)
    return jnp.take_along_axis(table, (jnp.arange(top)[None, :] + turn) % top, axis=1)


def load_shares(number_of, total, limit, lean, full):
    portions = [(1 << 20) // math.isqrt(rank ** lean) + 1 for rank in range(1, number_of + 1)]
    largest = limit if full else min(limit, max(-(-total // number_of), total * portions[0] // sum(portions)))
    least = 1 if total - largest >= number_of - 1 else 0
    counts, surplus = [largest] + [least] * (number_of - 1), total - largest - least * (number_of - 1)
    while surplus > 0:
        free = [i for i in range(1, number_of) if counts[i] < largest] or [i for i in range(1, number_of) if counts[i] < limit]
        pool, left = sum([portions[i] for i in free]), surplus
        for i in free:
            addition = min(limit - counts[i], max(1, left * portions[i] // pool), surplus)
            counts[i] = counts[i] + addition
            surplus = surplus - addition
    return np.array(counts)


def bell_draw(own_key, shape, width, bound, cuts=(), held_as=jnp.bfloat16):
    values = jax.random.normal(own_key, shape, jnp.float32) * width
    if len(cuts) > 0:
        values = level_of(own_key, shape, cuts, -0.22, 0.18) * values
    return jnp.clip(values, min=-bound, max=bound).astype(held_as)


def setup_inputs(seed: int = 0) -> dict:
    key_of = jax.random.split(jax.random.key(seed), 10)
    visibilities = bell_draw(key_of[0], (ROWS, 2, C), 2.0, 12.0, ((0, 32),))
    noise_weight = jnp.clip(jnp.exp(math.log(0.05) - 2.3025851 * jax.random.uniform(key_of[1], (ROWS,), jnp.float32) ** level_of(key_of[1], (ROWS,), ((0, 32),), -0.2, 0.2)), 0.005, 0.05)
    keep_flag = plant((jax.random.randint(key_of[2], (ROWS,), 0, 10) < 9).astype(jnp.int32), jax.random.fold_in(key_of[2], 1), 0, 1)
    station_pairs = draw_station_pairs(jax.random.fold_in(key_of[9], 71), 0)
    tile_owner_keys = jax.random.split(jax.random.fold_in(key_of[4], 1), ROWS // ROWS_DEV)
    tile_owner_turns = jax.random.permutation(jax.random.fold_in(key_of[4], 3), ROWS // ROWS_DEV)
    tile_owner = jax.vmap(lambda own, number: deal_out(jax.random.fold_in(key_of[4], 2), own, number, ROWS_DEV, DEVICES, 1, CAP, 2))(tile_owner_keys, tile_owner_turns).reshape((ROWS, 1))
    tile_offset = plant(jax.random.randint(key_of[5], (ROWS,), 0, GRID_DEV - KT + 1), jax.random.fold_in(key_of[5], 1), 0, GRID_DEV - KT).astype(jnp.int32)
    kernel_taps = jnp.clip(0.1 + 0.9 * jax.random.uniform(key_of[6], (KT, ROWS), jnp.float32) ** level_of(key_of[6], (KT, ROWS), ((1, 32),), -0.2, 0.2), 0.1, 1.0)
    gain_field = jnp.clip(1.0 + 0.15 * jax.random.normal(key_of[7], (NSOL, S, F, 2, C), jnp.float32), 0.25, 1.75)
    sky_grid = bell_draw(key_of[8], (2, F, NT, GRID), 0.5, 4.0, ((3, 32),), jnp.float32)
    return dict(visibilities=visibilities, noise_weight=noise_weight, keep_flag=keep_flag, station_pairs=station_pairs, tile_owner=tile_owner, tile_offset=tile_offset, kernel_taps=kernel_taps, gain_field=gain_field, sky_grid=sky_grid)


smoothness = 4.0

def spectral_table(channels, spectral_terms):
    channel_ramp = 2.0 * jnp.arange(channels, dtype=jnp.float32) / (channels - 1) - 1.0
    powers = jnp.arange(spectral_terms, dtype=jnp.float32)
    return channel_ramp[None, :] ** powers[:, None]

def complex_mul(x_re, x_im, y_re, y_im):
    return (x_re * y_re - x_im * y_im, x_re * y_im + x_im * y_re)

def row_grads(visibilities, noise_weight, keep_flag, station_pairs, gains_all, degrid):
    row_count = visibilities.shape[0]
    stations = gains_all.shape[0]
    facets = gains_all.shape[1]
    channels = gains_all.shape[3]
    spectral_terms = degrid.shape[2]
    spectrum = spectral_table(channels, spectral_terms)
    first_station = station_pairs[0]
    second_station = station_pairs[1]
    observed = visibilities.astype(jnp.float32)
    scaling = (noise_weight * keep_flag.astype(jnp.float32))[:, None, None]
    onehot_first = (jnp.arange(stations, dtype=jnp.int32)[:, None] == first_station[None, :]).astype(jnp.float32)
    onehot_second = (jnp.arange(stations, dtype=jnp.int32)[:, None] == second_station[None, :]).astype(jnp.float32)

    def facet_parts(facet_index):
        gain_slab = lax.dynamic_index_in_dim(gains_all, facet_index, 1, keepdims=False)
        left_gain = jnp.take(gain_slab, first_station, axis=0)
        right_gain = jnp.take(gain_slab, second_station, axis=0)
        degrid_slab = lax.dynamic_index_in_dim(degrid, facet_index, 1, keepdims=False)
        facet_model = jnp.einsum('xtr,tc->xrc', degrid_slab, spectrum, precision=lax.Precision.HIGHEST)
        return (left_gain, right_gain, facet_model)

    def add_model(facet_index, running):
        left_gain, right_gain, facet_model = facet_parts(facet_index)
        pair_re, pair_im = complex_mul(left_gain[:, 0], left_gain[:, 1], right_gain[:, 0], -right_gain[:, 1])
        vis_re, vis_im = complex_mul(pair_re, pair_im, facet_model[0], facet_model[1])
        return running + jnp.stack([vis_re, vis_im], axis=1)
    predicted = lax.fori_loop(0, facets, add_model, jnp.zeros((row_count, 2, channels), jnp.float32))
    error = scaling * (observed - predicted)
    err_re = error[:, 0]
    err_im = error[:, 1]

    def add_grads(facet_index, accums):
        gain_acc, degrid_acc = accums
        left_gain, right_gain, facet_model = facet_parts(facet_index)
        left_re, left_im = (left_gain[:, 0], left_gain[:, 1])
        right_re, right_im = (right_gain[:, 0], right_gain[:, 1])
        model_re, model_im = (facet_model[0], facet_model[1])
        first_re, first_im = complex_mul(err_re, err_im, right_re, right_im)
        grad_are, grad_aim = complex_mul(first_re, first_im, model_re, -model_im)
        second_re, second_im = complex_mul(err_re, -err_im, left_re, left_im)
        grad_bre, grad_bim = complex_mul(second_re, second_im, model_re, model_im)
        third_re, third_im = complex_mul(err_re, err_im, left_re, -left_im)
        grad_mre, grad_mim = complex_mul(third_re, third_im, right_re, right_im)
        grad_left = -jnp.stack([grad_are, grad_aim], axis=1).reshape(row_count, 2 * channels)
        grad_right = -jnp.stack([grad_bre, grad_bim], axis=1).reshape(row_count, 2 * channels)
        per_station = jnp.dot(onehot_first, grad_left, precision=lax.Precision.HIGHEST)
        per_station = per_station + jnp.dot(onehot_second, grad_right, precision=lax.Precision.HIGHEST)
        gain_acc = lax.dynamic_update_index_in_dim(gain_acc, per_station.reshape(stations, 2, channels), facet_index, 1)
        grad_model = -jnp.stack([grad_mre, grad_mim], axis=0)
        grad_degrid = jnp.einsum('xrc,tc->xtr', grad_model, spectrum, precision=lax.Precision.HIGHEST)
        degrid_acc = lax.dynamic_update_index_in_dim(degrid_acc, grad_degrid, facet_index, 1)
        return (gain_acc, degrid_acc)
    initial = (jnp.zeros((stations, facets, 2, channels), jnp.float32), jnp.zeros((2, facets, spectral_terms, row_count), jnp.float32))
    return lax.fori_loop(0, facets, add_grads, initial)

def smooth_grad(gain_block):
    step_diff = gain_block[1:] - gain_block[:-1]
    from_below = jnp.pad(step_diff, ((1, 0), (0, 0), (0, 0), (0, 0), (0, 0)))
    from_above = jnp.pad(step_diff, ((0, 1), (0, 0), (0, 0), (0, 0), (0, 0)))
    return smoothness * (from_below - from_above)

def reference(visibilities, noise_weight, keep_flag, station_pairs, tile_owner, tile_offset, kernel_taps, gain_field, sky_grid):
    rows_block = ROWS_SOL
    taps_count = kernel_taps.shape[0]
    tile_start = (tile_owner[:, 0] * GRID_DEV + tile_offset).astype(jnp.int32)

    def per_time(grid_sum, block_index):
        begin = (block_index * rows_block).astype(jnp.int32)
        vis_rows = lax.dynamic_slice_in_dim(visibilities, begin, rows_block, 0)
        weight_rows = lax.dynamic_slice_in_dim(noise_weight, begin, rows_block, 0)
        keep_rows = lax.dynamic_slice_in_dim(keep_flag, begin, rows_block, 0)
        pair_rows = lax.dynamic_slice_in_dim(station_pairs, begin, rows_block, 1)
        start_rows = lax.dynamic_slice_in_dim(tile_start, begin, rows_block, 0)
        tap_rows = lax.dynamic_slice_in_dim(kernel_taps, begin, rows_block, 1).T
        gains_here = lax.dynamic_index_in_dim(gain_field, block_index, 0, keepdims=False)
        cell_index = start_rows[:, None] + jnp.arange(taps_count, dtype=jnp.int32)[None, :]
        tiles = sky_grid[:, :, :, cell_index]
        degrid = lax.optimization_barrier(jnp.sum(tiles * tap_rows[None, None, None], axis=4))
        gain_part, grad_degrid = row_grads(vis_rows, weight_rows, keep_rows, pair_rows, gains_here, degrid)
        spread = grad_degrid[..., None] * tap_rows[None, None, None]
        grid_sum = grid_sum.at[:, :, :, cell_index].add(spread)
        return (grid_sum, gain_part)
    grid_gradient, data_gain = lax.scan(per_time, jnp.zeros(sky_grid.shape, jnp.float32), jnp.arange(N_TM, dtype=jnp.int32))
    gain_gradient = data_gain + smooth_grad(gain_field)
    return (gain_gradient, grid_gradient)
```

```python
import functools

import jax
import jax.numpy as jnp
from jax import lax
from jax.experimental import pallas as pl
from jax.experimental.pallas import tpu as pltpu
from jax.sharding import PartitionSpec as P

smoothness = 4.0
LANES = 128
f32 = jnp.float32
bf16 = jnp.bfloat16
i32 = jnp.int32
VMEM = pl.BlockSpec(memory_space=pltpu.VMEM)
SMEM = pl.BlockSpec(memory_space=pltpu.SMEM)
ANY = pl.BlockSpec(memory_space=pl.ANY)
CHUNK = 16


def iota(shape, dim):
    return lax.broadcasted_iota(i32, shape, dim)


def as_bf16(mask):
    return jnp.where(mask, 1.0, 0.0).astype(bf16)


def split(x, pieces):
    out = []
    for _ in range(pieces - 1):
        head = x.astype(bf16)
        out.append(head)
        x = x - head.astype(f32)
    out.append(x.astype(bf16))
    return out


def mm(a, b):
    return jnp.dot(a, b, preferred_element_type=f32)


def mm_nt(a, b):
    return lax.dot_general(a, b, (((1,), (1,)), ((), ())), preferred_element_type=f32)


def params(mib=48):
    return pltpu.CompilerParams(vmem_limit_bytes=mib << 20)


def cost(flops, byte_count):
    return pl.CostEstimate(flops=flops, bytes_accessed=byte_count, transcendentals=0)


def read_wide(ref, count):
    per = ref.shape[0] // count
    return jnp.concatenate(
        [ref[pl.ds(i, count, stride=per), :] for i in range(per)], axis=1
    )


def write_wide(ref, value):
    count = value.shape[0]
    per = ref.shape[0] // count
    for i in range(per):
        ref[pl.ds(i, count, stride=per), :] = value[:, i * LANES : (i + 1) * LANES]


def slots_kernel(
    n, cap, tiles, group, group_count,
    shift_ref, owner_ref, offset_ref, taps_ref, pairs_ref, noise_ref, keep_ref,
    send_ref, rows_ref, cols_ref,
):
    rows = owner_ref.shape[1]
    taps = taps_ref.shape[0]
    width = send_ref.shape[0] // n * LANES
    owner = owner_ref[...]
    hit = iota((n, rows), 0) == owner
    onehot = as_bf16(hit)
    earlier = as_bf16(iota((rows, rows), 0) < iota((rows, rows), 1))
    before = mm(onehot, earlier)
    rank = jnp.sum(jnp.where(hit, before, 0.0), axis=0, keepdims=True)
    at_rank = iota((cap, rows), 0) == rank.astype(i32)
    offset = offset_ref[...]
    base = jnp.minimum(offset // LANES, tiles - 2)
    low = offset - base * LANES
    fields = [taps_ref[k : k + 1, :] for k in range(taps)]
    fields += [low.astype(f32), base.astype(f32)]
    parts = [jnp.where(at_rank, v, 0.0) for v in fields]
    spare = width - len(parts) * cap
    if spare:
        parts.append(jnp.zeros((spare, rows), f32))
    total = None
    for piece in split(jnp.concatenate(parts, axis=0), 3):
        term = mm_nt(onehot, piece)
        total = term if total is None else total + term
    write_wide(send_ref, total)
    station = pairs_ref[...]
    turn = shift_ref[0] - station // group + group_count
    turn = jnp.where(turn >= group_count, turn - group_count, turn)
    local = (turn * group + (station - station // group * group)).astype(f32)
    scale = noise_ref[...] * keep_ref[...].astype(f32)
    table = jnp.concatenate(
        [owner.astype(f32), rank, local, scale, jnp.zeros((3, rows), f32)], axis=0
    )
    rows_ref[...] = table
    cols_ref[...] = table.T


def degrid_kernel(
    n, cap, taps,
    base_ref, recv_ref, sky_ref, out_ref, w_ref, held, blocks, sem,
):
    pairs = sky_ref.shape[0]
    copies = []
    for i in range(pairs):
        copy = pltpu.make_async_copy(sky_ref.at[i], held.at[:, i], sem.at[i])
        copy.start()
        copies.append(copy)
    recv = read_wide(recv_ref, n)
    lane = iota((n, 2 * LANES), 1).astype(f32)
    for j in range(cap):
        place = lane - recv[:, taps * cap + j : taps * cap + j + 1]
        w = jnp.zeros((n, 2 * LANES), f32)
        for k in range(taps):
            w = jnp.where(place == float(k), recv[:, k * cap + j : k * cap + j + 1], w)
        w_ref[j * n : (j + 1) * n, :] = w
    for copy in copies:
        copy.wait()
    block_count = n * cap // LANES
    per_block = LANES // n
    unroll = min(n, 16)
    lane3 = iota((2, pairs, LANES), 2)

    def block(jb, carry):
        def step(g, acc):
            for u in range(unroll):
                at = g * unroll + u
                j = jb * per_block + at // n
                start = base_ref[at % n, j] * 2
                w = w_ref[pl.ds(jb * LANES + at, 1), :]
                window = held[pl.ds(start, 4)]
                prod = window[0:2] * w[:, :LANES] + window[2:4] * w[:, LANES:]
                acc = jnp.where(lane3 == at, jnp.sum(prod, axis=2, keepdims=True), acc)
            return acc

        acc = lax.fori_loop(
            0, LANES // unroll, step, jnp.zeros((2, pairs, LANES), f32)
        )
        blocks[jb] = acc.reshape(2 * pairs, LANES)
        return carry

    lax.fori_loop(0, block_count, block, 0)
    planes = 2 * pairs
    turned = [blocks[jb].T for jb in range(block_count)]
    pieces = []
    for j in range(cap):
        jb, lo = j * n // LANES, j * n % LANES
        pieces.append(turned[jb][lo : lo + n, :planes])
    per_line = LANES // planes
    per = cap // per_line
    for i in range(per):
        line = jnp.concatenate(pieces[i * per_line : (i + 1) * per_line], axis=1)
        out_ref[pl.ds(i, n, stride=per), :] = line


def rows_kernel(
    n, cap, group_count,
    rows_ref, cols_ref, vis_ref, back_ref, *rest,
):
    gain_refs = rest[:group_count]
    out_refs = rest[group_count : 2 * group_count]
    send_ref = rest[2 * group_count]
    gains, g3, spec, a_s, b_s, m_s, e_s, glr_hi, glr_lo, gm_hi, gm_lo = rest[
        2 * group_count + 1 :
    ]
    facets, _, group, channels = gain_refs[0].shape
    rows = cols_ref.shape[0]
    stations = group * group_count
    planes = 4 * facets
    pairs = 2 * facets
    half = m_s.shape[2] // 2
    wide = 2 * half
    cols = cols_ref[...]
    owner_col, rank_col = cols[:, 0:1].astype(i32), cols[:, 1:2].astype(i32)
    first_col, second_col = cols[:, 2:3].astype(i32), cols[:, 3:4].astype(i32)

    gains[...] = jnp.zeros(gains.shape, f32)
    for k in range(group_count):
        for f in range(facets):
            for x in range(2):
                gains[f, k * group : (k + 1) * group, x * half : x * half + channels] = (
                    gain_refs[k][f, x]
                )

    back = jnp.concatenate(split(read_wide(back_ref, n), 3), axis=0)
    lane_n = iota((rows, 3 * n), 1)
    owner3 = as_bf16(
        (lane_n == owner_col) | (lane_n == owner_col + n) | (lane_n == owner_col + 2 * n)
    )
    picked = mm(owner3, back)
    slot_width = cap * planes
    lane_s = iota((rows, slot_width), 1)
    in_slot = lane_s // planes == rank_col
    picked = jnp.where(in_slot, picked, 0.0)
    fold = as_bf16(iota((slot_width, planes), 0) % planes == iota((slot_width, planes), 1))
    degrid = None
    for piece in split(picked, 3):
        term = mm(piece, fold)
        degrid = term if degrid is None else degrid + term
    term_scale = jnp.where(
        iota((1, planes), 1) >= pairs, 1.0 / (channels - 1), 1.0
    )
    d3 = jnp.concatenate(split(degrid * term_scale, 3), axis=1)

    lane_st = iota((rows, 3 * stations), 1)
    first3 = as_bf16(
        (lane_st == first_col)
        | (lane_st == first_col + stations)
        | (lane_st == first_col + 2 * stations)
    )
    second3 = as_bf16(
        (lane_st == second_col)
        | (lane_st == second_col + stations)
        | (lane_st == second_col + 2 * stations)
    )
    plane = iota((3 * planes, wide), 0) % planes
    lane_w = iota((3 * planes, wide), 1)
    chan = jnp.where(lane_w >= half, lane_w - half, lane_w)
    side = jnp.where(lane_w >= half, 1, 0)
    value = jnp.where(plane >= pairs, 2 * chan - (channels - 1), 1).astype(f32)
    live = (chan < channels) & ((plane % pairs) // facets == side)
    value = jnp.where(live, value, 0.0)
    facet_of = plane % facets

    def gather(f, carry):
        for q, piece in enumerate(split(gains[f], 3)):
            g3[q * stations : (q + 1) * stations, :] = piece
        spec[f] = jnp.where(facet_of == f, value, 0.0).astype(bf16)
        table = g3[...]
        a_s[f] = mm(first3, table)
        b_s[f] = mm(second3, table)
        m_s[f] = mm(d3, spec[f])
        return carry

    lax.fori_loop(0, facets, gather, 0)

    def predict(rc, carry):
        at = pl.ds(rc * CHUNK, CHUNK)
        re = jnp.zeros((CHUNK, half), f32)
        im = jnp.zeros((CHUNK, half), f32)
        for f in range(facets):
            a_re, a_im = a_s[f, at, :half], a_s[f, at, half:]
            b_re, b_im = b_s[f, at, :half], b_s[f, at, half:]
            m_re, m_im = m_s[f, at, :half], m_s[f, at, half:]
            p_re = a_re * b_re + a_im * b_im
            p_im = a_im * b_re - a_re * b_im
            re = re + (p_re * m_re - p_im * m_im)
            im = im + (p_re * m_im + p_im * m_re)
        scale = cols_ref[at, 4:5]
        e_s[at, :half] = scale * (re - vis_ref[at, :half].astype(f32))
        e_s[at, half:] = scale * (im - vis_ref[at, half:].astype(f32))
        return carry

    lax.fori_loop(0, rows // CHUNK, predict, 0)

    station_row = iota((stations, rows), 0)
    to_station = jnp.concatenate(
        [
            as_bf16(station_row == rows_ref[2:3, :].astype(i32)),
            as_bf16(station_row == rows_ref[3:4, :].astype(i32)),
        ],
        axis=1,
    )

    def put(hi_ref, lo_ref, at, lanes, value):
        hi = value.astype(bf16)
        hi_ref[at, lanes] = hi
        lo_ref[at, lanes] = (value - hi.astype(f32)).astype(bf16)

    re_lanes, im_lanes = slice(0, half), slice(half, wide)

    def grads(f, grad_degrid):
        def chunk(rc, carry):
            at = pl.ds(rc * CHUNK, CHUNK)
            later = pl.ds(rows + rc * CHUNK, CHUNK)
            e_re, e_im = e_s[at, :half], e_s[at, half:]
            a_re, a_im = a_s[f, at, :half], a_s[f, at, half:]
            b_re, b_im = b_s[f, at, :half], b_s[f, at, half:]
            m_re, m_im = m_s[f, at, :half], m_s[f, at, half:]
            t_re = e_re * m_re + e_im * m_im
            t_im = e_im * m_re - e_re * m_im
            p_re = a_re * b_re + a_im * b_im
            p_im = a_im * b_re - a_re * b_im
            put(glr_hi, glr_lo, at, re_lanes, t_re * b_re - t_im * b_im)
            put(glr_hi, glr_lo, at, im_lanes, t_re * b_im + t_im * b_re)
            put(glr_hi, glr_lo, later, re_lanes, t_re * a_re + t_im * a_im)
            put(glr_hi, glr_lo, later, im_lanes, t_re * a_im - t_im * a_re)
            put(gm_hi, gm_lo, at, re_lanes, e_re * p_re + e_im * p_im)
            put(gm_hi, gm_lo, at, im_lanes, e_im * p_re - e_re * p_im)
            return carry

        lax.fori_loop(0, rows // CHUNK, chunk, 0)
        summed = mm(to_station, glr_hi[...]) + mm(to_station, glr_lo[...])
        for k in range(group_count):
            for x in range(2):
                out_refs[k][f, x] = summed[
                    k * group : (k + 1) * group, x * half : x * half + channels
                ]
        table = spec[f, :planes, :]
        return grad_degrid + (mm_nt(gm_hi[...], table) + mm_nt(gm_lo[...], table))

    grad_degrid = lax.fori_loop(0, facets, grads, jnp.zeros((rows, planes), f32))
    grad3 = jnp.concatenate(split(grad_degrid * term_scale, 3), axis=1)
    spread = as_bf16(
        iota((3 * planes, slot_width), 0) % planes
        == iota((3 * planes, slot_width), 1) % planes
    )
    placed = jnp.where(in_slot, mm(grad3, spread), 0.0)
    owner_rows = as_bf16(iota((n, rows), 0) == rows_ref[0:1, :].astype(i32))
    total = None
    for piece in split(placed, 3):
        term = mm(owner_rows, piece)
        total = term if total is None else total + term
    write_wide(send_ref, total)


def scatter_kernel(n, cap, base_ref, grad_ref, w_ref, out_ref, held, blocks, sem):
    pairs = out_ref.shape[0]
    planes = 2 * pairs
    lines = held.shape[0]
    fill = 32

    def clear(i, carry):
        held[pl.ds(i * fill, fill)] = jnp.zeros((fill, pairs, LANES), f32)
        return carry

    lax.fori_loop(0, lines // fill, clear, 0)
    per_line = LANES // planes
    per = cap // per_line
    pieces = []
    for i in range(per):
        line = grad_ref[pl.ds(i, n, stride=per), :]
        for q in range(per_line):
            pieces.append(line[:, q * planes : (q + 1) * planes])
    per_block = LANES // n
    block_count = cap // per_block
    for jb in range(block_count):
        mine = pieces[jb * per_block : (jb + 1) * per_block]
        joined = mine[0] if per_block == 1 else jnp.concatenate(mine, axis=0)
        blocks[jb] = joined.T
    unroll = min(n, 16)
    lane3 = iota((2, pairs, LANES), 2)

    def block(jb, carry):
        values = blocks[jb].reshape(2, pairs, LANES)

        def step(g, inner):
            for u in range(unroll):
                at = g * unroll + u
                start = base_ref[at % n, jb * per_block + at // n] * 2
                w = w_ref[pl.ds(jb * LANES + at, 1), :]
                value = jnp.sum(
                    jnp.where(lane3 == at, values, 0.0), axis=2, keepdims=True
                )
                held[pl.ds(start, 2)] += value * w[:, :LANES]
                held[pl.ds(start + 2, 2)] += value * w[:, LANES:]
            return inner

        return lax.fori_loop(0, LANES // unroll, step, carry)

    lax.fori_loop(0, block_count, block, 0)
    copies = []
    for i in range(pairs):
        copy = pltpu.make_async_copy(held.at[:, i], out_ref.at[i], sem.at[i])
        copy.start()
        copies.append(copy)
    for copy in copies:
        copy.wait()


def body(
    visibilities,
    noise_weight,
    keep_flag,
    station_pairs,
    tile_owner,
    tile_offset,
    kernel_taps,
    gain_field,
    sky_grid,
):
    rows, _, channels = visibilities.shape
    taps = kernel_taps.shape[0]
    time_count = lax.axis_size("tm")
    group_count = lax.axis_size("bl")
    n = time_count * group_count
    cap = max(2, 2 * rows // n)
    _, facets, terms, cells = sky_grid.shape
    pairs = 2 * facets
    planes = pairs * terms
    tiles = cells // LANES
    group = gain_field.shape[1]
    stations = group * group_count
    both = ("tm", "bl")
    half = -(-channels // LANES) * LANES
    wide = 2 * half

    gain_turned = gain_field[0].transpose(1, 2, 0, 3)
    gathered = [gain_turned]
    for k in range(1, group_count):
        gathered.append(
            lax.ppermute(
                gain_turned, "bl", [(i, (i + k) % group_count) for i in range(group_count)]
            )
        )
    below = lax.ppermute(gain_field, "tm", [(i, i + 1) for i in range(time_count - 1)])
    above = lax.ppermute(gain_field, "tm", [(i + 1, i) for i in range(time_count - 1)])

    fields = taps + 2
    lines = -(-fields * cap // LANES)
    shift = jnp.full((1,), lax.axis_index("bl"), i32)
    send, row_table, col_table = pl.pallas_call(
        functools.partial(slots_kernel, n, cap, tiles, group, group_count),
        out_shape=(
            jax.ShapeDtypeStruct((n * lines, LANES), f32),
            jax.ShapeDtypeStruct((8, rows), f32),
            jax.ShapeDtypeStruct((rows, 8), f32),
        ),
        in_specs=[SMEM] + [VMEM] * 6,
        out_specs=(VMEM,) * 3,
        compiler_params=params(),
        cost_estimate=cost(10**9, 10**6),
        name="slots",
    )(
        shift,
        tile_owner.reshape(1, rows),
        tile_offset.reshape(1, rows),
        kernel_taps,
        station_pairs,
        noise_weight.reshape(1, rows),
        keep_flag.reshape(1, rows),
    )

    def exchange(x):
        x = x.reshape(n, -1, LANES)
        x = lax.all_to_all(x, both, split_axis=0, concat_axis=0, tiled=True)
        return x.reshape(-1, LANES)

    received = exchange(send)
    base = received.reshape(n, lines * LANES)[:, (taps + 1) * cap : (taps + 2) * cap]
    base = jnp.clip(base.astype(i32), 0, tiles - 2)
    sky = (
        sky_grid.reshape(pairs, terms, tiles, LANES)
        .transpose(0, 2, 1, 3)
        .reshape(pairs, terms * tiles, LANES)
    )
    slot_lines = n * cap * planes // LANES
    block_count = n * cap // LANES
    values, weights = pl.pallas_call(
        functools.partial(degrid_kernel, n, cap, taps),
        out_shape=(
            jax.ShapeDtypeStruct((slot_lines, LANES), f32),
            jax.ShapeDtypeStruct((n * cap, 2 * LANES), f32),
        ),
        in_specs=[SMEM, VMEM, ANY],
        out_specs=(VMEM, VMEM),
        scratch_shapes=[
            pltpu.VMEM((terms * tiles, pairs, LANES), f32),
            pltpu.VMEM((block_count, planes, LANES), f32),
            pltpu.SemaphoreType.DMA((pairs,)),
        ],
        compiler_params=params(),
        cost_estimate=cost(10**8, 7 * 10**7),
        name="degrid",
    )(base, received, sky)
    back = exchange(values)

    vis_wide = jnp.pad(visibilities, ((0, 0), (0, 0), (0, half - channels))).reshape(
        rows, wide
    )
    partial_shape = jax.ShapeDtypeStruct((facets, 2, group, channels), f32)
    outs = pl.pallas_call(
        functools.partial(rows_kernel, n, cap, group_count),
        out_shape=(partial_shape,) * group_count
        + (jax.ShapeDtypeStruct((slot_lines, LANES), f32),),
        in_specs=[VMEM] * (4 + group_count),
        out_specs=(VMEM,) * (group_count + 1),
        scratch_shapes=[
            pltpu.VMEM((facets, stations, wide), f32),
            pltpu.VMEM((3 * stations, wide), bf16),
            pltpu.VMEM((facets, 3 * planes, wide), bf16),
            pltpu.VMEM((facets, rows, wide), f32),
            pltpu.VMEM((facets, rows, wide), f32),
            pltpu.VMEM((facets, rows, wide), f32),
            pltpu.VMEM((rows, wide), f32),
            pltpu.VMEM((2 * rows, wide), bf16),
            pltpu.VMEM((2 * rows, wide), bf16),
            pltpu.VMEM((rows, wide), bf16),
            pltpu.VMEM((rows, wide), bf16),
        ],
        compiler_params=params(),
        cost_estimate=cost(2 * 10**10, 10**7),
        name="rowgrads",
    )(row_table, col_table, vis_wide, back, *gathered)

    got = exchange(outs[group_count])
    total = outs[0]
    for k in range(1, group_count):
        total = total + lax.ppermute(
            outs[k], "bl", [(i, (i - k) % group_count) for i in range(group_count)]
        )
    grid = pl.pallas_call(
        functools.partial(scatter_kernel, n, cap),
        out_shape=jax.ShapeDtypeStruct((pairs, terms * tiles, LANES), f32),
        in_specs=[SMEM, VMEM, VMEM],
        out_specs=ANY,
        scratch_shapes=[
            pltpu.VMEM((terms * tiles, pairs, LANES), f32),
            pltpu.VMEM((block_count, planes, LANES), f32),
            pltpu.SemaphoreType.DMA((pairs,)),
        ],
        compiler_params=params(),
        cost_estimate=cost(10**8, 10**8),
        name="scatter",
    )(base, got, weights)
    grid_gradient = (
        grid.reshape(pairs, tiles, terms, LANES)
        .transpose(0, 2, 1, 3)
        .reshape(sky_grid.shape)
    )
    when = lax.axis_index("tm")
    prior = jnp.where(when > 0, gain_field - below, 0.0)
    prior = prior - jnp.where(when < time_count - 1, above - gain_field, 0.0)
    gain_gradient = total.transpose(2, 0, 1, 3)[None] + smoothness * prior
    return (gain_gradient, grid_gradient)


def solution(mesh):
    return jax.shard_map(
        body,
        mesh=mesh,
        in_specs=(
            P(("tm", "bl"), None, None),
            P(("tm", "bl")),
            P(("tm", "bl")),
            P(None, ("tm", "bl")),
            P(("tm", "bl"), None),
            P(("tm", "bl")),
            P(None, ("tm", "bl")),
            P("tm", "bl", None, None, None),
            P(None, None, None, ("tm", "bl")),
        ),
        out_specs=(P("tm", "bl", None, None, None), P(None, None, None, ("tm", "bl"))),
        check_vma=False,
    )
```

```python
import functools

import jax
import jax.numpy as jnp
from jax import lax
from jax.experimental import pallas as pl
from jax.experimental.pallas import tpu as pltpu
from jax.sharding import PartitionSpec as P

smoothness = 4.0
LANES = 128
f32 = jnp.float32
bf16 = jnp.bfloat16
i32 = jnp.int32
VMEM = pl.BlockSpec(memory_space=pltpu.VMEM)
SMEM = pl.BlockSpec(memory_space=pltpu.SMEM)
ANY = pl.BlockSpec(memory_space=pl.ANY)
CHUNK = 16


def iota(shape, dim):
    return lax.broadcasted_iota(i32, shape, dim)


def as_bf16(mask):
    return jnp.where(mask, 1.0, 0.0).astype(bf16)


def split(x, pieces):
    out = []
    for _ in range(pieces - 1):
        head = x.astype(bf16)
        out.append(head)
        x = x - head.astype(f32)
    out.append(x.astype(bf16))
    return out


def mm(a, b):
    return jnp.dot(a, b, preferred_element_type=f32)


def mm_nt(a, b):
    return lax.dot_general(a, b, (((1,), (1,)), ((), ())), preferred_element_type=f32)


def params(mib=60):
    return pltpu.CompilerParams(vmem_limit_bytes=mib << 20)


def cost(flops, byte_count):
    return pl.CostEstimate(flops=flops, bytes_accessed=byte_count, transcendentals=0)


def read_wide(ref, count):
    per = ref.shape[0] // count
    return jnp.concatenate(
        [ref[pl.ds(i, count, stride=per), :] for i in range(per)], axis=1
    )


def write_wide(ref, value):
    count = value.shape[0]
    per = ref.shape[0] // count
    for i in range(per):
        ref[pl.ds(i, count, stride=per), :] = value[:, i * LANES : (i + 1) * LANES]


def slots_kernel(
    n, cap, tiles, group, group_count,
    shift_ref, owner_ref, offset_ref, taps_ref, pairs_ref, noise_ref, keep_ref,
    send_ref, rows_ref, cols_ref,
):
    rows = owner_ref.shape[1]
    taps = taps_ref.shape[0]
    width = send_ref.shape[0] // n * LANES
    owner = owner_ref[...]
    hit = iota((n, rows), 0) == owner
    onehot = as_bf16(hit)
    earlier = as_bf16(iota((rows, rows), 0) < iota((rows, rows), 1))
    before = mm(onehot, earlier)
    rank = jnp.sum(jnp.where(hit, before, 0.0), axis=0, keepdims=True)
    at_rank = iota((cap, rows), 0) == rank.astype(i32)
    offset = offset_ref[...]
    base = jnp.minimum(offset // LANES, tiles - 2)
    low = offset - base * LANES
    fields = [taps_ref[k : k + 1, :] for k in range(taps)]
    fields += [low.astype(f32), base.astype(f32)]
    parts = [jnp.where(at_rank, v, 0.0) for v in fields]
    spare = width - len(parts) * cap
    if spare:
        parts.append(jnp.zeros((spare, rows), f32))
    total = None
    for piece in split(jnp.concatenate(parts, axis=0), 3):
        term = mm_nt(onehot, piece)
        total = term if total is None else total + term
    write_wide(send_ref, total)
    station = pairs_ref[...]
    turn = shift_ref[0] - station // group + group_count
    turn = jnp.where(turn >= group_count, turn - group_count, turn)
    local = (turn * group + (station - station // group * group)).astype(f32)
    scale = noise_ref[...] * keep_ref[...].astype(f32)
    table = jnp.concatenate(
        [owner.astype(f32), rank, local, scale, jnp.zeros((3, rows), f32)], axis=0
    )
    rows_ref[...] = table
    cols_ref[...] = table.T


def degrid_kernel(
    n, cap, taps,
    base_ref, recv_ref, sky_ref, out_ref, w_ref, held, blocks, sem,
):
    pairs = sky_ref.shape[0]
    copies = []
    for i in range(pairs):
        copy = pltpu.make_async_copy(sky_ref.at[i], held.at[:, i], sem.at[i])
        copy.start()
        copies.append(copy)
    recv = read_wide(recv_ref, n)
    lane = iota((n, 2 * LANES), 1).astype(f32)
    for j in range(cap):
        place = lane - recv[:, taps * cap + j : taps * cap + j + 1]
        w = jnp.zeros((n, 2 * LANES), f32)
        for k in range(taps):
            w = jnp.where(place == float(k), recv[:, k * cap + j : k * cap + j + 1], w)
        w_ref[j * n : (j + 1) * n, :] = w
    for copy in copies:
        copy.wait()
    block_count = n * cap // LANES
    per_block = LANES // n
    unroll = min(n, 16)
    lane3 = iota((2, pairs, LANES), 2)

    def block(jb, carry):
        def step(g, acc):
            for u in range(unroll):
                at = g * unroll + u
                j = jb * per_block + at // n
                start = base_ref[at % n, j] * 2
                w = w_ref[pl.ds(jb * LANES + at, 1), :]
                window = held[pl.ds(start, 4)]
                prod = window[0:2] * w[:, :LANES] + window[2:4] * w[:, LANES:]
                acc = jnp.where(lane3 == at, jnp.sum(prod, axis=2, keepdims=True), acc)
            return acc

        acc = lax.fori_loop(
            0, LANES // unroll, step, jnp.zeros((2, pairs, LANES), f32)
        )
        blocks[jb] = acc.reshape(2 * pairs, LANES)
        return carry

    lax.fori_loop(0, block_count, block, 0)
    planes = 2 * pairs
    turned = [blocks[jb].T for jb in range(block_count)]
    pieces = []
    for j in range(cap):
        jb, lo = j * n // LANES, j * n % LANES
        pieces.append(turned[jb][lo : lo + n, :planes])
    per_line = LANES // planes
    per = cap // per_line
    for i in range(per):
        line = jnp.concatenate(pieces[i * per_line : (i + 1) * per_line], axis=1)
        out_ref[pl.ds(i, n, stride=per), :] = line


def rows_kernel(
    n, cap, group_count,
    rows_ref, cols_ref, vis_ref, back_ref, *rest,
):
    gain_refs = rest[:group_count]
    out_refs = rest[group_count : 2 * group_count]
    send_ref = rest[2 * group_count]
    gains, g3, spec, a_s, b_s, m_s, e_s, glr_hi, glr_lo, gm_hi, gm_lo = rest[
        2 * group_count + 1 :
    ]
    facets, _, group, channels = gain_refs[0].shape
    rows = cols_ref.shape[0]
    stations = group * group_count
    planes = 4 * facets
    pairs = 2 * facets
    half = m_s.shape[2] // 2
    wide = 2 * half
    cols = cols_ref[...]
    owner_col, rank_col = cols[:, 0:1].astype(i32), cols[:, 1:2].astype(i32)
    first_col, second_col = cols[:, 2:3].astype(i32), cols[:, 3:4].astype(i32)

    gains[...] = jnp.zeros(gains.shape, f32)
    for k in range(group_count):
        for f in range(facets):
            for x in range(2):
                gains[f, k * group : (k + 1) * group, x * half : x * half + channels] = (
                    gain_refs[k][f, x]
                )

    back = jnp.concatenate(split(read_wide(back_ref, n), 3), axis=0)
    lane_n = iota((rows, 3 * n), 1)
    owner3 = as_bf16(
        (lane_n == owner_col) | (lane_n == owner_col + n) | (lane_n == owner_col + 2 * n)
    )
    picked = mm(owner3, back)
    slot_width = cap * planes
    lane_s = iota((rows, slot_width), 1)
    in_slot = lane_s // planes == rank_col
    picked = jnp.where(in_slot, picked, 0.0)
    fold = as_bf16(iota((slot_width, planes), 0) % planes == iota((slot_width, planes), 1))
    degrid = None
    for piece in split(picked, 3):
        term = mm(piece, fold)
        degrid = term if degrid is None else degrid + term
    term_scale = jnp.where(
        iota((1, planes), 1) >= pairs, 1.0 / (channels - 1), 1.0
    )
    d3 = jnp.concatenate(split(degrid * term_scale, 3), axis=1)

    lane_st = iota((rows, 3 * stations), 1)
    first3 = as_bf16(
        (lane_st == first_col)
        | (lane_st == first_col + stations)
        | (lane_st == first_col + 2 * stations)
    )
    second3 = as_bf16(
        (lane_st == second_col)
        | (lane_st == second_col + stations)
        | (lane_st == second_col + 2 * stations)
    )
    plane = iota((3 * planes, wide), 0) % planes
    lane_w = iota((3 * planes, wide), 1)
    chan = jnp.where(lane_w >= half, lane_w - half, lane_w)
    side = jnp.where(lane_w >= half, 1, 0)
    value = jnp.where(plane >= pairs, 2 * chan - (channels - 1), 1).astype(f32)
    live = (chan < channels) & ((plane % pairs) // facets == side)
    value = jnp.where(live, value, 0.0)
    facet_of = plane % facets

    def gather(f, carry):
        for q, piece in enumerate(split(gains[f], 3)):
            g3[q * stations : (q + 1) * stations, :] = piece
        spec[f] = jnp.where(facet_of == f, value, 0.0).astype(bf16)
        table = g3[...]
        a_s[f] = mm(first3, table)
        b_s[f] = mm(second3, table)
        m_s[f] = mm(d3, spec[f])
        return carry

    lax.fori_loop(0, facets, gather, 0)

    def predict(rc, carry):
        at = pl.ds(rc * CHUNK, CHUNK)
        re = jnp.zeros((CHUNK, half), f32)
        im = jnp.zeros((CHUNK, half), f32)
        for f in range(facets):
            a_re, a_im = a_s[f, at, :half], a_s[f, at, half:]
            b_re, b_im = b_s[f, at, :half], b_s[f, at, half:]
            m_re, m_im = m_s[f, at, :half], m_s[f, at, half:]
            p_re = a_re * b_re + a_im * b_im
            p_im = a_im * b_re - a_re * b_im
            re = re + (p_re * m_re - p_im * m_im)
            im = im + (p_re * m_im + p_im * m_re)
        scale = cols_ref[at, 4:5]
        e_s[at, :half] = scale * (re - vis_ref[at, :half].astype(f32))
        e_s[at, half:] = scale * (im - vis_ref[at, half:].astype(f32))
        return carry

    lax.fori_loop(0, rows // CHUNK, predict, 0)

    station_row = iota((stations, rows), 0)
    to_station = jnp.concatenate(
        [
            as_bf16(station_row == rows_ref[2:3, :].astype(i32)),
            as_bf16(station_row == rows_ref[3:4, :].astype(i32)),
        ],
        axis=1,
    )

    def put(hi_ref, lo_ref, at, lanes, value):
        hi = value.astype(bf16)
        hi_ref[at, lanes] = hi
        lo_ref[at, lanes] = (value - hi.astype(f32)).astype(bf16)

    re_lanes, im_lanes = slice(0, half), slice(half, wide)

    def grads(f, grad_degrid):
        def chunk(rc, carry):
            at = pl.ds(rc * CHUNK, CHUNK)
            later = pl.ds(rows + rc * CHUNK, CHUNK)
            e_re, e_im = e_s[at, :half], e_s[at, half:]
            a_re, a_im = a_s[f, at, :half], a_s[f, at, half:]
            b_re, b_im = b_s[f, at, :half], b_s[f, at, half:]
            m_re, m_im = m_s[f, at, :half], m_s[f, at, half:]
            t_re = e_re * m_re + e_im * m_im
            t_im = e_im * m_re - e_re * m_im
            p_re = a_re * b_re + a_im * b_im
            p_im = a_im * b_re - a_re * b_im
            put(glr_hi, glr_lo, at, re_lanes, t_re * b_re - t_im * b_im)
            put(glr_hi, glr_lo, at, im_lanes, t_re * b_im + t_im * b_re)
            put(glr_hi, glr_lo, later, re_lanes, t_re * a_re + t_im * a_im)
            put(glr_hi, glr_lo, later, im_lanes, t_re * a_im - t_im * a_re)
            put(gm_hi, gm_lo, at, re_lanes, e_re * p_re + e_im * p_im)
            put(gm_hi, gm_lo, at, im_lanes, e_im * p_re - e_re * p_im)
            return carry

        lax.fori_loop(0, rows // CHUNK, chunk, 0)
        summed = mm(to_station, glr_hi[...]) + mm(to_station, glr_lo[...])
        for k in range(group_count):
            for x in range(2):
                out_refs[k][f, x] = summed[
                    k * group : (k + 1) * group, x * half : x * half + channels
                ]
        table = spec[f, :planes, :]
        return grad_degrid + (mm_nt(gm_hi[...], table) + mm_nt(gm_lo[...], table))

    grad_degrid = lax.fori_loop(0, facets, grads, jnp.zeros((rows, planes), f32))
    grad3 = jnp.concatenate(split(grad_degrid * term_scale, 3), axis=1)
    spread = as_bf16(
        iota((3 * planes, slot_width), 0) % planes
        == iota((3 * planes, slot_width), 1) % planes
    )
    placed = jnp.where(in_slot, mm(grad3, spread), 0.0)
    owner_rows = as_bf16(iota((n, rows), 0) == rows_ref[0:1, :].astype(i32))
    total = None
    for piece in split(placed, 3):
        term = mm(owner_rows, piece)
        total = term if total is None else total + term
    write_wide(send_ref, total)


def scatter_kernel(n, cap, base_ref, grad_ref, w_ref, out_ref, held, blocks, sem):
    pairs = out_ref.shape[0]
    planes = 2 * pairs
    lines = held.shape[0]
    fill = 32

    def clear(i, carry):
        held[pl.ds(i * fill, fill)] = jnp.zeros((fill, pairs, LANES), f32)
        return carry

    lax.fori_loop(0, lines // fill, clear, 0)
    per_line = LANES // planes
    per = cap // per_line
    pieces = []
    for i in range(per):
        line = grad_ref[pl.ds(i, n, stride=per), :]
        for q in range(per_line):
            pieces.append(line[:, q * planes : (q + 1) * planes])
    per_block = LANES // n
    block_count = cap // per_block
    for jb in range(block_count):
        mine = pieces[jb * per_block : (jb + 1) * per_block]
        joined = mine[0] if per_block == 1 else jnp.concatenate(mine, axis=0)
        blocks[jb] = joined.T
    unroll = min(n, 16)
    lane3 = iota((2, pairs, LANES), 2)

    def block(jb, carry):
        values = blocks[jb].reshape(2, pairs, LANES)

        def step(g, inner):
            for u in range(unroll):
                at = g * unroll + u
                start = base_ref[at % n, jb * per_block + at // n] * 2
                w = w_ref[pl.ds(jb * LANES + at, 1), :]
                value = jnp.sum(
                    jnp.where(lane3 == at, values, 0.0), axis=2, keepdims=True
                )
                held[pl.ds(start, 2)] += value * w[:, :LANES]
                held[pl.ds(start + 2, 2)] += value * w[:, LANES:]
            return inner

        return lax.fori_loop(0, LANES // unroll, step, carry)

    lax.fori_loop(0, block_count, block, 0)
    copies = []
    for i in range(pairs):
        copy = pltpu.make_async_copy(held.at[:, i], out_ref.at[i], sem.at[i])
        copy.start()
        copies.append(copy)
    for copy in copies:
        copy.wait()


def body(
    visibilities,
    noise_weight,
    keep_flag,
    station_pairs,
    tile_owner,
    tile_offset,
    kernel_taps,
    gain_field,
    sky_grid,
):
    rows, _, channels = visibilities.shape
    taps = kernel_taps.shape[0]
    time_count = lax.axis_size("tm")
    group_count = lax.axis_size("bl")
    n = time_count * group_count
    cap = max(2, 2 * rows // n)
    _, facets, terms, cells = sky_grid.shape
    pairs = 2 * facets
    planes = pairs * terms
    tiles = cells // LANES
    group = gain_field.shape[1]
    stations = group * group_count
    both = ("tm", "bl")
    half = -(-channels // LANES) * LANES
    wide = 2 * half

    gain_turned = gain_field[0].transpose(1, 2, 0, 3)
    fields = taps + 2
    lines = -(-fields * cap // LANES)
    shift = jnp.full((1,), lax.axis_index("bl"), i32)
    send, row_table, col_table = pl.pallas_call(
        functools.partial(slots_kernel, n, cap, tiles, group, group_count),
        out_shape=(
            jax.ShapeDtypeStruct((n * lines, LANES), f32),
            jax.ShapeDtypeStruct((8, rows), f32),
            jax.ShapeDtypeStruct((rows, 8), f32),
        ),
        in_specs=[SMEM] + [VMEM] * 6,
        out_specs=(VMEM,) * 3,
        compiler_params=params(),
        cost_estimate=cost(10**9, 10**6),
        name="slots",
    )(
        shift,
        tile_owner.reshape(1, rows),
        tile_offset.reshape(1, rows),
        kernel_taps,
        station_pairs,
        noise_weight.reshape(1, rows),
        keep_flag.reshape(1, rows),
    )

    def exchange(x):
        x = x.reshape(n, -1, LANES)
        x = lax.all_to_all(x, both, split_axis=0, concat_axis=0, tiled=True)
        return x.reshape(-1, LANES)

    received, gain_turned = lax.optimization_barrier((exchange(send), gain_turned))
    gathered = [gain_turned]
    for k in range(1, group_count):
        gathered.append(
            lax.ppermute(
                gain_turned, "bl", [(i, (i + k) % group_count) for i in range(group_count)]
            )
        )
    base = received.reshape(n, lines * LANES)[:, (taps + 1) * cap : (taps + 2) * cap]
    base = jnp.clip(base.astype(i32), 0, tiles - 2)
    sky = (
        sky_grid.reshape(pairs, terms, tiles, LANES)
        .transpose(0, 2, 1, 3)
        .reshape(pairs, terms * tiles, LANES)
    )
    slot_lines = n * cap * planes // LANES
    block_count = n * cap // LANES
    values, weights = pl.pallas_call(
        functools.partial(degrid_kernel, n, cap, taps),
        out_shape=(
            jax.ShapeDtypeStruct((slot_lines, LANES), f32),
            jax.ShapeDtypeStruct((n * cap, 2 * LANES), f32),
        ),
        in_specs=[SMEM, VMEM, ANY],
        out_specs=(VMEM, VMEM),
        scratch_shapes=[
            pltpu.VMEM((terms * tiles, pairs, LANES), f32),
            pltpu.VMEM((block_count, planes, LANES), f32),
            pltpu.SemaphoreType.DMA((pairs,)),
        ],
        compiler_params=params(),
        cost_estimate=cost(10**8, 7 * 10**7),
        name="degrid",
    )(base, received, sky)
    values, *gathered = lax.optimization_barrier((values, *gathered))
    back, gain_here = lax.optimization_barrier((exchange(values), gain_field))
    below = lax.ppermute(gain_here, "tm", [(i, i + 1) for i in range(time_count - 1)])
    above = lax.ppermute(gain_here, "tm", [(i + 1, i) for i in range(time_count - 1)])

    vis_wide = jnp.pad(visibilities, ((0, 0), (0, 0), (0, half - channels))).reshape(
        rows, wide
    )
    partial_shape = jax.ShapeDtypeStruct((facets, 2, group, channels), f32)
    outs = pl.pallas_call(
        functools.partial(rows_kernel, n, cap, group_count),
        out_shape=(partial_shape,) * group_count
        + (jax.ShapeDtypeStruct((slot_lines, LANES), f32),),
        in_specs=[VMEM] * (4 + group_count),
        out_specs=(VMEM,) * (group_count + 1),
        scratch_shapes=[
            pltpu.VMEM((facets, stations, wide), f32),
            pltpu.VMEM((3 * stations, wide), bf16),
            pltpu.VMEM((facets, 3 * planes, wide), bf16),
            pltpu.VMEM((facets, rows, wide), f32),
            pltpu.VMEM((facets, rows, wide), f32),
            pltpu.VMEM((facets, rows, wide), f32),
            pltpu.VMEM((rows, wide), f32),
            pltpu.VMEM((2 * rows, wide), bf16),
            pltpu.VMEM((2 * rows, wide), bf16),
            pltpu.VMEM((rows, wide), bf16),
            pltpu.VMEM((rows, wide), bf16),
        ],
        compiler_params=params(),
        cost_estimate=cost(2 * 10**10, 10**7),
        name="rowgrads",
    )(row_table, col_table, vis_wide, back, *gathered)

    *parts, send_grad = outs
    send_grad, below, above = lax.optimization_barrier((send_grad, below, above))
    got, *parts = lax.optimization_barrier((exchange(send_grad), *parts))
    for k in range(1, group_count):
        parts[k] = lax.ppermute(
            parts[k], "bl", [(i, (i - k) % group_count) for i in range(group_count)]
        )
    grid = pl.pallas_call(
        functools.partial(scatter_kernel, n, cap),
        out_shape=jax.ShapeDtypeStruct((pairs, terms * tiles, LANES), f32),
        in_specs=[SMEM, VMEM, VMEM],
        out_specs=ANY,
        scratch_shapes=[
            pltpu.VMEM((terms * tiles, pairs, LANES), f32),
            pltpu.VMEM((block_count, planes, LANES), f32),
            pltpu.SemaphoreType.DMA((pairs,)),
        ],
        compiler_params=params(),
        cost_estimate=cost(10**8, 10**8),
        name="scatter",
    )(base, got, weights)
    grid, *parts = lax.optimization_barrier((grid, *parts))
    total = parts[0]
    for part in parts[1:]:
        total = total + part
    grid_gradient = (
        grid.reshape(pairs, tiles, terms, LANES)
        .transpose(0, 2, 1, 3)
        .reshape(sky_grid.shape)
    )
    when = lax.axis_index("tm")
    prior = jnp.where(when > 0, gain_field - below, 0.0)
    prior = prior - jnp.where(when < time_count - 1, above - gain_field, 0.0)
    gain_gradient = total.transpose(2, 0, 1, 3)[None] + smoothness * prior
    return (gain_gradient, grid_gradient)


def solution(mesh):
    return jax.shard_map(
        body,
        mesh=mesh,
        in_specs=(
            P(("tm", "bl"), None, None),
            P(("tm", "bl")),
            P(("tm", "bl")),
            P(None, ("tm", "bl")),
            P(("tm", "bl"), None),
            P(("tm", "bl")),
            P(None, ("tm", "bl")),
            P("tm", "bl", None, None, None),
            P(None, None, None, ("tm", "bl")),
        ),
        out_specs=(P("tm", "bl", None, None, None), P(None, None, None, ("tm", "bl"))),
        check_vma=False,
    )
```

```python
import functools

import jax
import jax.numpy as jnp
from jax import lax
from jax.experimental import pallas as pl
from jax.experimental.pallas import tpu as pltpu
from jax.sharding import PartitionSpec as P

smoothness = 4.0
LANES = 128
f32 = jnp.float32
bf16 = jnp.bfloat16
i32 = jnp.int32
VMEM = pl.BlockSpec(memory_space=pltpu.VMEM)
SMEM = pl.BlockSpec(memory_space=pltpu.SMEM)
ANY = pl.BlockSpec(memory_space=pl.ANY)
CHUNK = 16


def iota(shape, dim):
    return lax.broadcasted_iota(i32, shape, dim)


def as_bf16(mask):
    return jnp.where(mask, 1.0, 0.0).astype(bf16)


def split(x, pieces):
    out = []
    for _ in range(pieces - 1):
        head = x.astype(bf16)
        out.append(head)
        x = x - head.astype(f32)
    out.append(x.astype(bf16))
    return out


def mm(a, b):
    return jnp.dot(a, b, preferred_element_type=f32)


def mm_nt(a, b):
    return lax.dot_general(a, b, (((1,), (1,)), ((), ())), preferred_element_type=f32)


def div(x, k):
    return x >> (k.bit_length() - 1) if k & (k - 1) == 0 else x // k


def mod(x, k):
    return x & (k - 1) if k & (k - 1) == 0 else x - x // k * k


def params(mib=60):
    return pltpu.CompilerParams(vmem_limit_bytes=mib << 20)


def cost(flops, byte_count):
    return pl.CostEstimate(flops=flops, bytes_accessed=byte_count, transcendentals=0)


def read_wide(ref, count):
    per = ref.shape[0] // count
    return jnp.concatenate(
        [ref[pl.ds(i, count, stride=per), :] for i in range(per)], axis=1
    )


def write_wide(ref, value):
    count = value.shape[0]
    per = ref.shape[0] // count
    for i in range(per):
        ref[pl.ds(i, count, stride=per), :] = value[:, i * LANES : (i + 1) * LANES]


def slots_kernel(
    n, cap, tiles, group, group_count,
    shift_ref, owner_ref, offset_ref, taps_ref, pairs_ref, noise_ref, keep_ref,
    send_ref, rows_ref, cols_ref,
):
    rows = owner_ref.shape[1]
    taps = taps_ref.shape[0]
    width = send_ref.shape[0] // n * LANES
    owner = owner_ref[...]
    hit = iota((n, rows), 0) == owner
    onehot = as_bf16(hit)
    earlier = as_bf16(iota((rows, rows), 0) < iota((rows, rows), 1))
    before = mm(onehot, earlier)
    rank = jnp.sum(jnp.where(hit, before, 0.0), axis=0, keepdims=True)
    at_rank = iota((cap, rows), 0) == rank.astype(i32)
    offset = offset_ref[...]
    base = jnp.minimum(offset // LANES, tiles - 2)
    low = offset - base * LANES
    fields = [taps_ref[k : k + 1, :] for k in range(taps)]
    fields += [low.astype(f32), base.astype(f32)]
    parts = [jnp.where(at_rank, v, 0.0) for v in fields]
    spare = width - len(parts) * cap
    if spare:
        parts.append(jnp.zeros((spare, rows), f32))
    total = None
    for piece in split(jnp.concatenate(parts, axis=0), 3):
        term = mm_nt(onehot, piece)
        total = term if total is None else total + term
    write_wide(send_ref, total)
    station = pairs_ref[...]
    turn = shift_ref[0] - station // group + group_count
    turn = jnp.where(turn >= group_count, turn - group_count, turn)
    local = (turn * group + (station - station // group * group)).astype(f32)
    scale = noise_ref[...] * keep_ref[...].astype(f32)
    table = jnp.concatenate(
        [owner.astype(f32), rank, local, scale, jnp.zeros((3, rows), f32)], axis=0
    )
    rows_ref[...] = table
    cols_ref[...] = table.T


def load_kernel(sky_ref, held_ref, sem):
    copies = []
    for i in range(sky_ref.shape[0]):
        copy = pltpu.make_async_copy(sky_ref.at[i], held_ref.at[:, i], sem.at[i])
        copy.start()
        copies.append(copy)
    for copy in copies:
        copy.wait()


def degrid_kernel(
    n, cap, taps,
    base_ref, recv_ref, held, out_ref, w_ref, blocks,
):
    pairs = held.shape[1]
    planes = 2 * pairs
    recv = read_wide(recv_ref, n)
    lane = iota((n, 2 * LANES), 1).astype(f32)
    for j in range(cap):
        place = lane - recv[:, taps * cap + j : taps * cap + j + 1]
        w = jnp.zeros((n, 2 * LANES), f32)
        for k in range(taps):
            w = jnp.where(place == float(k), recv[:, k * cap + j : k * cap + j + 1], w)
        w_ref[j * n : (j + 1) * n, :] = w
    per_block = LANES // n
    block_count = cap // per_block
    unroll = min(n, 16)
    lane3 = iota((2, pairs, LANES), 2)

    def block(jb, carry):
        acc = jnp.zeros((2, pairs, LANES), f32)
        for q in range(per_block):
            j = jb * per_block + q

            def step(g, acc):
                first = g * unroll
                rel = lane3 - (q * n + first)
                for u in range(unroll):
                    start = base_ref[j, first + u]
                    w = w_ref[pl.ds(j * n + first + u, 1), :]
                    window = held[pl.ds(start, 4)]
                    prod = window[0:2] * w[:, :LANES] + window[2:4] * w[:, LANES:]
                    acc = jnp.where(rel == u, jnp.sum(prod, axis=2, keepdims=True), acc)
                return acc

            acc = lax.fori_loop(0, n // unroll, step, acc)
        blocks[jb] = acc.reshape(planes, LANES)
        return carry

    lax.fori_loop(0, block_count, block, 0)
    turned = [blocks[jb].T for jb in range(block_count)]
    pieces = []
    for j in range(cap):
        jb, lo = j * n // LANES, j * n % LANES
        pieces.append(turned[jb][lo : lo + n, :planes])
    per_line = LANES // planes
    per = cap // per_line
    for i in range(per):
        line = jnp.concatenate(pieces[i * per_line : (i + 1) * per_line], axis=1)
        out_ref[pl.ds(i, n, stride=per), :] = line


def rows_kernel(
    n, cap, group_count,
    rows_ref, cols_ref, vis_ref, back_ref, *rest,
):
    gain_refs = rest[:group_count]
    out_refs = rest[group_count : 2 * group_count]
    send_ref = rest[2 * group_count]
    gains, spec, a_s, b_s, m_s, e_s, glr_hi, glr_lo, gm_hi, gm_lo = rest[
        2 * group_count + 1 :
    ]
    facets, _, group, channels = gain_refs[0].shape
    rows = cols_ref.shape[0]
    stations = group * group_count
    planes = 4 * facets
    pairs = 2 * facets
    half = m_s.shape[2] // 2
    wide = 2 * half
    cols = cols_ref[...]
    owner_col, rank_col = cols[:, 0:1].astype(i32), cols[:, 1:2].astype(i32)
    first_col, second_col = cols[:, 2:3].astype(i32), cols[:, 3:4].astype(i32)

    gains[...] = jnp.zeros(gains.shape, f32)
    for k in range(group_count):
        for f in range(facets):
            for x in range(2):
                gains[f, k * group : (k + 1) * group, x * half : x * half + channels] = (
                    gain_refs[k][f, x]
                )

    owner3 = as_bf16(mod(iota((1, 3 * n), 1), n) == owner_col)
    per_line = LANES // planes
    line_count = cap // per_line
    slot_of = div(iota((1, LANES), 1), planes) - rank_col
    degrid = jnp.zeros((rows, LANES), f32)
    for i in range(line_count):
        line = jnp.concatenate(split(back_ref[pl.ds(i, n, stride=line_count), :], 3), axis=0)
        degrid = degrid + jnp.where(slot_of == -i * per_line, mm(owner3, line), 0.0)
    fold = as_bf16(mod(iota((3 * LANES, planes), 0), planes) == iota((3 * LANES, planes), 1))
    degrid = mm(jnp.concatenate(split(degrid, 3), axis=1), fold)
    term_scale = jnp.where(iota((1, planes), 1) >= pairs, 1.0 / (channels - 1), 1.0)
    d3 = jnp.concatenate(split(degrid * term_scale, 3), axis=1)

    lane_st = mod(iota((1, 3 * stations), 1), stations)
    first3 = as_bf16(lane_st == first_col)
    second3 = as_bf16(lane_st == second_col)
    plane = mod(iota((3 * planes, wide), 0), planes)
    lane_w = iota((3 * planes, wide), 1)
    chan = jnp.where(lane_w >= half, lane_w - half, lane_w)
    side = jnp.where(lane_w >= half, 1, 0)
    value = jnp.where(plane >= pairs, 2 * chan - (channels - 1), 1).astype(f32)
    live = (chan < channels) & (div(mod(plane, pairs), facets) == side)
    value = jnp.where(live, value, 0.0)
    facet_of = mod(plane, facets)
    chunks = [pl.ds(i * CHUNK, CHUNK) for i in range(rows // CHUNK)]

    def gather(f):
        table = jnp.concatenate(split(gains[f], 3), axis=0)
        spec[f] = jnp.where(facet_of == f, value, 0.0).astype(bf16)
        a_s[f] = mm(first3, table)
        b_s[f] = mm(second3, table)
        m_s[f] = mm(d3, spec[f])

    def load(f, at):
        return (
            a_s[f, at, :half], a_s[f, at, half:],
            b_s[f, at, :half], b_s[f, at, half:],
            m_s[f, at, :half], m_s[f, at, half:],
        )

    def predict(f):
        for at in chunks:
            a_re, a_im, b_re, b_im, m_re, m_im = load(f, at)
            p_re = a_re * b_re + a_im * b_im
            p_im = a_im * b_re - a_re * b_im
            e_s[at, :half] += p_re * m_re - p_im * m_im
            e_s[at, half:] += p_re * m_im + p_im * m_re

    e_s[...] = -vis_ref[...].astype(f32)
    gather(0)

    def forward(f, carry):
        gather(f + 1)
        predict(f)
        return carry

    lax.fori_loop(0, facets - 1, forward, 0)
    predict(facets - 1)
    e_s[...] = e_s[...] * cols[:, 4:5]

    block = min(rows, 128)
    block_count = rows // block
    station_row = iota((stations, rows), 0)
    to_first = as_bf16(station_row == rows_ref[2:3, :].astype(i32))
    to_second = as_bf16(station_row == rows_ref[3:4, :].astype(i32))
    to_station = []
    for c in range(block_count):
        part = slice(c * block, (c + 1) * block)
        to_station.append(jnp.concatenate([to_first[:, part], to_second[:, part]], axis=1))

    def put(hi_ref, lo_ref, at, lanes, value):
        hi = value.astype(bf16)
        hi_ref[at, lanes] = hi
        lo_ref[at, lanes] = (value - hi.astype(f32)).astype(bf16)

    re_lanes, im_lanes = slice(0, half), slice(half, wide)

    def grads(f, grad_degrid):
        summed = jnp.zeros((stations, wide), f32)
        table = spec[f, :planes, :]
        parts = []
        for c in range(block_count):
            for i in range(block // CHUNK):
                at = pl.ds(c * block + i * CHUNK, CHUNK)
                left = pl.ds(2 * c * block + i * CHUNK, CHUNK)
                right = pl.ds((2 * c + 1) * block + i * CHUNK, CHUNK)
                e_re, e_im = e_s[at, :half], e_s[at, half:]
                a_re, a_im, b_re, b_im, m_re, m_im = load(f, at)
                t_re = e_re * m_re + e_im * m_im
                t_im = e_im * m_re - e_re * m_im
                p_re = a_re * b_re + a_im * b_im
                p_im = a_im * b_re - a_re * b_im
                put(glr_hi, glr_lo, left, re_lanes, t_re * b_re - t_im * b_im)
                put(glr_hi, glr_lo, left, im_lanes, t_re * b_im + t_im * b_re)
                put(glr_hi, glr_lo, right, re_lanes, t_re * a_re + t_im * a_im)
                put(glr_hi, glr_lo, right, im_lanes, t_re * a_im - t_im * a_re)
                put(gm_hi, gm_lo, at, re_lanes, e_re * p_re + e_im * p_im)
                put(gm_hi, gm_lo, at, im_lanes, e_im * p_re - e_re * p_im)
            both = pl.ds(2 * c * block, 2 * block)
            here = pl.ds(c * block, block)
            summed = summed + (
                mm(to_station[c], glr_hi[both, :]) + mm(to_station[c], glr_lo[both, :])
            )
            parts.append(mm_nt(gm_hi[here, :], table) + mm_nt(gm_lo[here, :], table))
        for k in range(group_count):
            for x in range(2):
                out_refs[k][f, x] = summed[
                    k * group : (k + 1) * group, x * half : x * half + channels
                ]
        return grad_degrid + jnp.concatenate(parts, axis=0)

    grad_degrid = lax.fori_loop(0, facets, grads, jnp.zeros((rows, planes), f32))
    grad3 = jnp.concatenate(split(grad_degrid * term_scale, 3), axis=1)
    spread = as_bf16(
        mod(iota((3 * planes, LANES), 0), planes) == mod(iota((3 * planes, LANES), 1), planes)
    )
    heads = [h.astype(f32) for h in split(mm(grad3, spread), 2)]
    owner_rows = as_bf16(iota((n, rows), 0) == rows_ref[0:1, :].astype(i32))
    for i in range(line_count):
        here = slot_of == -i * per_line
        placed = jnp.concatenate(
            [jnp.where(here, h, 0.0).astype(bf16) for h in heads], axis=1
        )
        total = mm(owner_rows, placed)
        send_ref[pl.ds(i, n, stride=line_count), :] = total[:, :LANES] + total[:, LANES:]


def scatter_kernel(n, cap, base_ref, grad_ref, w_ref, out_ref, held, blocks, sem):
    pairs = out_ref.shape[0]
    planes = 2 * pairs
    lines = held.shape[0]
    fill = 32

    def clear(i, carry):
        held[pl.ds(i * fill, fill)] = jnp.zeros((fill, pairs, LANES), f32)
        return carry

    lax.fori_loop(0, lines // fill, clear, 0)
    per_line = LANES // planes
    per = cap // per_line
    pieces = []
    for i in range(per):
        line = grad_ref[pl.ds(i, n, stride=per), :]
        for q in range(per_line):
            pieces.append(line[:, q * planes : (q + 1) * planes])
    per_block = LANES // n
    block_count = cap // per_block
    for jb in range(block_count):
        mine = pieces[jb * per_block : (jb + 1) * per_block]
        joined = mine[0] if per_block == 1 else jnp.concatenate(mine, axis=0)
        blocks[jb] = joined.T
    unroll = min(n, 16)
    lane3 = iota((2, pairs, LANES), 2)

    def block(jb, carry):
        values = blocks[jb].reshape(2, pairs, LANES)
        for q in range(per_block):
            j = jb * per_block + q

            def step(g, inner):
                first = g * unroll
                rel = lane3 - (q * n + first)
                for u in range(unroll):
                    at = pl.ds(base_ref[j, first + u], 4)
                    w = w_ref[pl.ds(j * n + first + u, 1), :]
                    value = jnp.sum(
                        jnp.where(rel == u, values, 0.0), axis=2, keepdims=True
                    )
                    held[at] = held[at] + jnp.concatenate(
                        [value * w[:, :LANES], value * w[:, LANES:]], axis=0
                    )
                return inner

            carry = lax.fori_loop(0, n // unroll, step, carry)
        return carry

    lax.fori_loop(0, block_count, block, 0)
    copies = []
    for i in range(pairs):
        copy = pltpu.make_async_copy(held.at[:, i], out_ref.at[i], sem.at[i])
        copy.start()
        copies.append(copy)
    for copy in copies:
        copy.wait()


def body(
    visibilities,
    noise_weight,
    keep_flag,
    station_pairs,
    tile_owner,
    tile_offset,
    kernel_taps,
    gain_field,
    sky_grid,
):
    rows, _, channels = visibilities.shape
    taps = kernel_taps.shape[0]
    time_count = lax.axis_size("tm")
    group_count = lax.axis_size("bl")
    n = time_count * group_count
    cap = max(2, 2 * rows // n)
    _, facets, terms, cells = sky_grid.shape
    pairs = 2 * facets
    planes = pairs * terms
    tiles = cells // LANES
    group = gain_field.shape[1]
    stations = group * group_count
    both = ("tm", "bl")
    half = -(-channels // LANES) * LANES
    wide = 2 * half

    gain_turned = gain_field[0].transpose(1, 2, 0, 3)
    fields = taps + 2
    lines = 1 << (-(-fields * cap // LANES) - 1).bit_length()
    shift = jnp.full((1,), lax.axis_index("bl"), i32)
    send, row_table, col_table = pl.pallas_call(
        functools.partial(slots_kernel, n, cap, tiles, group, group_count),
        out_shape=(
            jax.ShapeDtypeStruct((n * lines, LANES), f32),
            jax.ShapeDtypeStruct((8, rows), f32),
            jax.ShapeDtypeStruct((rows, 8), f32),
        ),
        in_specs=[SMEM] + [VMEM] * 6,
        out_specs=(VMEM,) * 3,
        compiler_params=params(),
        cost_estimate=cost(10**9, 10**6),
        name="slots",
    )(
        shift,
        tile_owner.reshape(1, rows),
        tile_offset.reshape(1, rows),
        kernel_taps,
        station_pairs,
        noise_weight.reshape(1, rows),
        keep_flag.reshape(1, rows),
    )

    def exchange(x):
        x = x.reshape(n, -1, LANES)
        x = lax.all_to_all(x, both, split_axis=0, concat_axis=0, tiled=True)
        return x.reshape(-1, LANES)

    sky = (
        sky_grid.reshape(pairs, terms, tiles, LANES)
        .transpose(0, 2, 1, 3)
        .reshape(pairs, terms * tiles, LANES)
    )
    held = pl.pallas_call(
        load_kernel,
        out_shape=pltpu.VMEM((terms * tiles, pairs, LANES), f32),
        in_specs=[ANY],
        out_specs=VMEM,
        scratch_shapes=[pltpu.SemaphoreType.DMA((pairs,))],
        compiler_params=params(44),
        cost_estimate=cost(0, 2 * 10**7),
        name="load",
    )(sky)
    received, gain_turned, held = lax.optimization_barrier(
        (exchange(send), gain_turned, held)
    )
    gathered = [gain_turned]
    for k in range(1, group_count):
        gathered.append(
            lax.ppermute(
                gain_turned, "bl", [(i, (i + k) % group_count) for i in range(group_count)]
            )
        )
    base = received.reshape(n, lines * LANES)[:, (taps + 1) * cap : (taps + 2) * cap]
    base = jnp.clip(base.T.astype(i32), 0, tiles - 2) * terms
    slot_lines = n * cap * planes // LANES
    block_count = n * cap // LANES
    values, weights = pl.pallas_call(
        functools.partial(degrid_kernel, n, cap, taps),
        out_shape=(
            jax.ShapeDtypeStruct((slot_lines, LANES), f32),
            jax.ShapeDtypeStruct((n * cap, 2 * LANES), f32),
        ),
        in_specs=[SMEM, VMEM, VMEM],
        out_specs=(VMEM, VMEM),
        scratch_shapes=[pltpu.VMEM((block_count, planes, LANES), f32)],
        compiler_params=params(24),
        cost_estimate=cost(10**8, 5 * 10**7),
        name="degrid",
    )(base, received, held)
    values, *gathered = lax.optimization_barrier((values, *gathered))
    back, gain_here = lax.optimization_barrier((exchange(values), gain_field))
    below = lax.ppermute(gain_here, "tm", [(i, i + 1) for i in range(time_count - 1)])
    above = lax.ppermute(gain_here, "tm", [(i + 1, i) for i in range(time_count - 1)])

    vis_wide = jnp.pad(visibilities, ((0, 0), (0, 0), (0, half - channels))).reshape(
        rows, wide
    )
    partial_shape = jax.ShapeDtypeStruct((facets, 2, group, channels), f32)
    outs = pl.pallas_call(
        functools.partial(rows_kernel, n, cap, group_count),
        out_shape=(partial_shape,) * group_count
        + (jax.ShapeDtypeStruct((slot_lines, LANES), f32),),
        in_specs=[VMEM] * (4 + group_count),
        out_specs=(VMEM,) * (group_count + 1),
        scratch_shapes=[
            pltpu.VMEM((facets, stations, wide), f32),
            pltpu.VMEM((facets, 3 * planes, wide), bf16),
            pltpu.VMEM((facets, rows, wide), f32),
            pltpu.VMEM((facets, rows, wide), f32),
            pltpu.VMEM((facets, rows, wide), f32),
            pltpu.VMEM((rows, wide), f32),
            pltpu.VMEM((2 * rows, wide), bf16),
            pltpu.VMEM((2 * rows, wide), bf16),
            pltpu.VMEM((rows, wide), bf16),
            pltpu.VMEM((rows, wide), bf16),
        ],
        compiler_params=params(),
        cost_estimate=cost(2 * 10**10, 10**7),
        name="rowgrads",
    )(row_table, col_table, vis_wide, back, *gathered)

    *parts, send_grad = outs
    send_grad, below, above = lax.optimization_barrier((send_grad, below, above))
    got, *parts = lax.optimization_barrier((exchange(send_grad), *parts))
    for k in range(1, group_count):
        parts[k] = lax.ppermute(
            parts[k], "bl", [(i, (i - k) % group_count) for i in range(group_count)]
        )
    grid = pl.pallas_call(
        functools.partial(scatter_kernel, n, cap),
        out_shape=jax.ShapeDtypeStruct((pairs, terms * tiles, LANES), f32),
        in_specs=[SMEM, VMEM, VMEM],
        out_specs=ANY,
        scratch_shapes=[
            pltpu.VMEM((terms * tiles, pairs, LANES), f32),
            pltpu.VMEM((block_count, planes, LANES), f32),
            pltpu.SemaphoreType.DMA((pairs,)),
        ],
        compiler_params=params(),
        cost_estimate=cost(10**8, 10**8),
        name="scatter",
    )(base, got, weights)
    grid, *parts = lax.optimization_barrier((grid, *parts))
    total = parts[0]
    for part in parts[1:]:
        total = total + part
    grid_gradient = (
        grid.reshape(pairs, tiles, terms, LANES)
        .transpose(0, 2, 1, 3)
        .reshape(sky_grid.shape)
    )
    when = lax.axis_index("tm")
    prior = jnp.where(when > 0, gain_field - below, 0.0)
    prior = prior - jnp.where(when < time_count - 1, above - gain_field, 0.0)
    gain_gradient = total.transpose(2, 0, 1, 3)[None] + smoothness * prior
    return (gain_gradient, grid_gradient)


def solution(mesh):
    return jax.shard_map(
        body,
        mesh=mesh,
        in_specs=(
            P(("tm", "bl"), None, None),
            P(("tm", "bl")),
            P(("tm", "bl")),
            P(None, ("tm", "bl")),
            P(("tm", "bl"), None),
            P(("tm", "bl")),
            P(None, ("tm", "bl")),
            P("tm", "bl", None, None, None),
            P(None, None, None, ("tm", "bl")),
        ),
        out_specs=(P("tm", "bl", None, None, None), P(None, None, None, ("tm", "bl"))),
        check_vma=False,
    )
```

```python
import functools

import jax
import jax.numpy as jnp
from jax import lax
from jax.experimental import pallas as pl
from jax.experimental.pallas import tpu as pltpu
from jax.sharding import PartitionSpec as P

smoothness = 4.0
LANES = 128
f32 = jnp.float32
bf16 = jnp.bfloat16
i32 = jnp.int32
VMEM = pl.BlockSpec(memory_space=pltpu.VMEM)
SMEM = pl.BlockSpec(memory_space=pltpu.SMEM)
ANY = pl.BlockSpec(memory_space=pl.ANY)
CHUNK = 16


def iota(shape, dim):
    return lax.broadcasted_iota(i32, shape, dim)


def as_bf16(mask):
    return jnp.where(mask, 1.0, 0.0).astype(bf16)


def split(x, pieces):
    out = []
    for _ in range(pieces - 1):
        head = x.astype(bf16)
        out.append(head)
        x = x - head.astype(f32)
    out.append(x.astype(bf16))
    return out


def mm(a, b):
    return jnp.dot(a, b, preferred_element_type=f32)


def mm_nt(a, b):
    return lax.dot_general(a, b, (((1,), (1,)), ((), ())), preferred_element_type=f32)


def div(x, k):
    return x >> (k.bit_length() - 1) if k & (k - 1) == 0 else x // k


def mod(x, k):
    return x & (k - 1) if k & (k - 1) == 0 else x - x // k * k


def params(mib=60):
    return pltpu.CompilerParams(vmem_limit_bytes=mib << 20)


def cost(flops, byte_count):
    return pl.CostEstimate(flops=flops, bytes_accessed=byte_count, transcendentals=0)


def read_wide(ref, count):
    per = ref.shape[0] // count
    return jnp.concatenate(
        [ref[pl.ds(i, count, stride=per), :] for i in range(per)], axis=1
    )


def write_wide(ref, value):
    count = value.shape[0]
    per = ref.shape[0] // count
    for i in range(per):
        ref[pl.ds(i, count, stride=per), :] = value[:, i * LANES : (i + 1) * LANES]


def slots_kernel(
    n, cap, tiles, group, group_count,
    shift_ref, owner_ref, offset_ref, taps_ref, pairs_ref, noise_ref, keep_ref,
    send_ref, rows_ref, cols_ref,
):
    rows = owner_ref.shape[1]
    taps = taps_ref.shape[0]
    width = send_ref.shape[0] // n * LANES
    owner = owner_ref[...]
    hit = iota((n, rows), 0) == owner
    onehot = as_bf16(hit)
    earlier = as_bf16(iota((rows, rows), 0) < iota((rows, rows), 1))
    before = mm(onehot, earlier)
    rank = jnp.sum(jnp.where(hit, before, 0.0), axis=0, keepdims=True)
    at_rank = iota((cap, rows), 0) == rank.astype(i32)
    offset = offset_ref[...]
    base = jnp.minimum(offset // LANES, tiles - 2)
    low = offset - base * LANES
    fields = [taps_ref[k : k + 1, :] for k in range(taps)]
    fields += [low.astype(f32), base.astype(f32)]
    parts = [jnp.where(at_rank, v, 0.0) for v in fields]
    spare = width - len(parts) * cap
    if spare:
        parts.append(jnp.zeros((spare, rows), f32))
    total = None
    for piece in split(jnp.concatenate(parts, axis=0), 3):
        term = mm_nt(onehot, piece)
        total = term if total is None else total + term
    write_wide(send_ref, total)
    station = pairs_ref[...]
    turn = shift_ref[0] - station // group + group_count
    turn = jnp.where(turn >= group_count, turn - group_count, turn)
    local = (turn * group + (station - station // group * group)).astype(f32)
    scale = noise_ref[...] * keep_ref[...].astype(f32)
    table = jnp.concatenate(
        [owner.astype(f32), rank, local, scale, jnp.zeros((3, rows), f32)], axis=0
    )
    rows_ref[...] = table
    cols_ref[...] = table.T


def load_kernel(sky_ref, held_ref, token_ref, sem):
    token_ref[...] = jnp.zeros(token_ref.shape, f32)
    copies = []
    for i in range(sky_ref.shape[0]):
        copy = pltpu.make_async_copy(sky_ref.at[i], held_ref.at[:, i], sem.at[i])
        copy.start()
        copies.append(copy)
    for copy in copies:
        copy.wait()


def degrid_kernel(
    n, cap, taps,
    base_ref, recv_ref, held, out_ref, w_ref, w_s, turn_s, blocks, sem,
):
    pairs = held.shape[1]
    planes = 2 * pairs
    per_block = LANES // n
    block_count = cap // per_block
    turn_s[...] = read_wide(recv_ref, n).T
    fields = []
    for k in range(taps + 1):
        fields.append(
            jnp.concatenate(
                [
                    turn_s[pl.ds(k * cap + q, block_count, stride=per_block), :]
                    for q in range(per_block)
                ],
                axis=1,
            )
        )
    line = iota((2 * LANES, LANES), 0).astype(f32)
    for jb in range(block_count):
        place = line - fields[taps][jb : jb + 1, :]
        w = jnp.zeros((2 * LANES, LANES), f32)
        for k in range(taps):
            w = jnp.where(place == float(k), fields[k][jb : jb + 1, :], w)
        w_s[jb * LANES : (jb + 1) * LANES, :] = w.T
    save = pltpu.make_async_copy(w_s, w_ref, sem.at[0])
    save.start()
    unroll = min(n, 16)
    lane3 = iota((2, pairs, LANES), 2)
    ones = jnp.ones((2 * LANES, LANES), bf16)

    def block(jb, carry):
        acc = jnp.zeros((2, pairs, LANES), f32)
        for q in range(per_block):
            j = jb * per_block + q

            def step(g, acc):
                first = g * unroll
                rel = lane3 - (q * n + first)
                prods = []
                for u in range(unroll):
                    start = base_ref[j, first + u]
                    w = w_s[pl.ds(j * n + first + u, 1), :]
                    window = held[pl.ds(start, 4)]
                    prod = window[0:2] * w[:, :LANES] + window[2:4] * w[:, LANES:]
                    prods.append(prod.reshape(planes, LANES))
                halves = split(jnp.concatenate(prods, axis=0), 2)
                sums = mm(jnp.concatenate(halves, axis=1), ones)
                for u in range(unroll):
                    one = sums[u * planes : (u + 1) * planes, :].reshape(2, pairs, LANES)
                    acc = jnp.where(rel == u, one, acc)
                return acc

            acc = lax.fori_loop(0, n // unroll, step, acc)
        blocks[jb] = acc.reshape(planes, LANES)
        return carry

    lax.fori_loop(0, block_count, block, 0)
    turned = [blocks[jb].T for jb in range(block_count)]
    pieces = []
    for j in range(cap):
        jb, lo = j * n // LANES, j * n % LANES
        pieces.append(turned[jb][lo : lo + n, :planes])
    per_line = LANES // planes
    per = cap // per_line
    for i in range(per):
        line = jnp.concatenate(pieces[i * per_line : (i + 1) * per_line], axis=1)
        out_ref[pl.ds(i, n, stride=per), :] = line
    save.wait()


def rows_kernel(
    n, cap, group_count,
    rows_ref, cols_ref, vis_ref, back_ref, *rest,
):
    gain_refs = rest[:group_count]
    out_refs = rest[group_count : 2 * group_count]
    send_ref = rest[2 * group_count]
    gains, spec, a_s, b_s, m_s, e_s, glr_hi, glr_lo, gm_hi, gm_lo = rest[
        2 * group_count + 1 :
    ]
    facets, _, group, channels = gain_refs[0].shape
    rows = cols_ref.shape[0]
    stations = group * group_count
    planes = 4 * facets
    pairs = 2 * facets
    half = m_s.shape[2] // 2
    wide = 2 * half
    cols = cols_ref[...]
    owner_col, rank_col = cols[:, 0:1].astype(i32), cols[:, 1:2].astype(i32)
    first_col, second_col = cols[:, 2:3].astype(i32), cols[:, 3:4].astype(i32)

    gains[...] = jnp.zeros(gains.shape, f32)
    for k in range(group_count):
        for f in range(facets):
            for x in range(2):
                gains[f, k * group : (k + 1) * group, x * half : x * half + channels] = (
                    gain_refs[k][f, x]
                )

    owner3 = as_bf16(mod(iota((1, 3 * n), 1), n) == owner_col)
    per_line = LANES // planes
    line_count = cap // per_line
    slot_of = div(iota((1, LANES), 1), planes) - rank_col
    degrid = jnp.zeros((rows, LANES), f32)
    for i in range(line_count):
        line = jnp.concatenate(split(back_ref[pl.ds(i, n, stride=line_count), :], 3), axis=0)
        degrid = degrid + jnp.where(slot_of == -i * per_line, mm(owner3, line), 0.0)
    fold = as_bf16(mod(iota((3 * LANES, planes), 0), planes) == iota((3 * LANES, planes), 1))
    degrid = mm(jnp.concatenate(split(degrid, 3), axis=1), fold)
    term_scale = jnp.where(iota((1, planes), 1) >= pairs, 1.0 / (channels - 1), 1.0)
    d3 = jnp.concatenate(split(degrid * term_scale, 3), axis=1)

    lane_st = mod(iota((1, 3 * stations), 1), stations)
    first3 = as_bf16(lane_st == first_col)
    second3 = as_bf16(lane_st == second_col)
    plane = mod(iota((3 * planes, wide), 0), planes)
    lane_w = iota((3 * planes, wide), 1)
    chan = jnp.where(lane_w >= half, lane_w - half, lane_w)
    side = jnp.where(lane_w >= half, 1, 0)
    value = jnp.where(plane >= pairs, 2 * chan - (channels - 1), 1).astype(f32)
    live = (chan < channels) & (div(mod(plane, pairs), facets) == side)
    value = jnp.where(live, value, 0.0)
    facet_of = mod(plane, facets)
    chunks = [pl.ds(i * CHUNK, CHUNK) for i in range(rows // CHUNK)]

    def gather(f):
        table = jnp.concatenate(split(gains[f], 3), axis=0)
        spec[f] = jnp.where(facet_of == f, value, 0.0).astype(bf16)
        a_s[f] = mm(first3, table)
        b_s[f] = mm(second3, table)
        m_s[f] = mm(d3, spec[f])

    def load(f, at):
        return (
            a_s[f, at, :half], a_s[f, at, half:],
            b_s[f, at, :half], b_s[f, at, half:],
            m_s[f, at, :half], m_s[f, at, half:],
        )

    def predict(f):
        for at in chunks:
            a_re, a_im, b_re, b_im, m_re, m_im = load(f, at)
            p_re = a_re * b_re + a_im * b_im
            p_im = a_im * b_re - a_re * b_im
            e_s[at, :half] += p_re * m_re - p_im * m_im
            e_s[at, half:] += p_re * m_im + p_im * m_re

    e_s[...] = -vis_ref[...].astype(f32)
    gather(0)

    def forward(f, carry):
        gather(f + 1)
        predict(f)
        return carry

    lax.fori_loop(0, facets - 1, forward, 0)
    predict(facets - 1)
    e_s[...] = e_s[...] * cols[:, 4:5]

    block = min(rows, 128)
    block_count = rows // block
    station_row = iota((stations, rows), 0)
    to_first = as_bf16(station_row == rows_ref[2:3, :].astype(i32))
    to_second = as_bf16(station_row == rows_ref[3:4, :].astype(i32))
    to_station = []
    for c in range(block_count):
        part = slice(c * block, (c + 1) * block)
        to_station.append(jnp.concatenate([to_first[:, part], to_second[:, part]], axis=1))

    def put(hi_ref, lo_ref, at, lanes, value):
        hi = value.astype(bf16)
        hi_ref[at, lanes] = hi
        lo_ref[at, lanes] = (value - hi.astype(f32)).astype(bf16)

    re_lanes, im_lanes = slice(0, half), slice(half, wide)

    def grads(f, grad_degrid):
        summed = jnp.zeros((stations, wide), f32)
        table = spec[f, :planes, :]
        parts = []
        for c in range(block_count):
            for i in range(block // CHUNK):
                at = pl.ds(c * block + i * CHUNK, CHUNK)
                left = pl.ds(2 * c * block + i * CHUNK, CHUNK)
                right = pl.ds((2 * c + 1) * block + i * CHUNK, CHUNK)
                e_re, e_im = e_s[at, :half], e_s[at, half:]
                a_re, a_im, b_re, b_im, m_re, m_im = load(f, at)
                t_re = e_re * m_re + e_im * m_im
                t_im = e_im * m_re - e_re * m_im
                p_re = a_re * b_re + a_im * b_im
                p_im = a_im * b_re - a_re * b_im
                put(glr_hi, glr_lo, left, re_lanes, t_re * b_re - t_im * b_im)
                put(glr_hi, glr_lo, left, im_lanes, t_re * b_im + t_im * b_re)
                put(glr_hi, glr_lo, right, re_lanes, t_re * a_re + t_im * a_im)
                put(glr_hi, glr_lo, right, im_lanes, t_re * a_im - t_im * a_re)
                put(gm_hi, gm_lo, at, re_lanes, e_re * p_re + e_im * p_im)
                put(gm_hi, gm_lo, at, im_lanes, e_im * p_re - e_re * p_im)
            both = pl.ds(2 * c * block, 2 * block)
            here = pl.ds(c * block, block)
            summed = summed + (
                mm(to_station[c], glr_hi[both, :]) + mm(to_station[c], glr_lo[both, :])
            )
            parts.append(mm_nt(gm_hi[here, :], table) + mm_nt(gm_lo[here, :], table))
        for k in range(group_count):
            for x in range(2):
                out_refs[k][f, x] = summed[
                    k * group : (k + 1) * group, x * half : x * half + channels
                ]
        return grad_degrid + jnp.concatenate(parts, axis=0)

    grad_degrid = lax.fori_loop(0, facets, grads, jnp.zeros((rows, planes), f32))
    grad3 = jnp.concatenate(split(grad_degrid * term_scale, 3), axis=1)
    spread = as_bf16(
        mod(iota((3 * planes, LANES), 0), planes) == mod(iota((3 * planes, LANES), 1), planes)
    )
    heads = [h.astype(f32) for h in split(mm(grad3, spread), 2)]
    owner_rows = as_bf16(iota((n, rows), 0) == rows_ref[0:1, :].astype(i32))
    for i in range(line_count):
        here = slot_of == -i * per_line
        placed = jnp.concatenate(
            [jnp.where(here, h, 0.0).astype(bf16) for h in heads], axis=1
        )
        total = mm(owner_rows, placed)
        send_ref[pl.ds(i, n, stride=line_count), :] = total[:, :LANES] + total[:, LANES:]


def clear_kernel(after_ref, held):
    fill = 32

    def clear(i, carry):
        held[pl.ds(i * fill, fill)] = jnp.zeros((fill,) + held.shape[1:], f32)
        return carry

    lax.fori_loop(0, held.shape[0] // fill, clear, 0)


def scatter_kernel(n, cap, base_ref, grad_ref, w_ref, zero_ref, out_ref, held, sem):
    pairs = out_ref.shape[0]
    planes = 2 * pairs
    per_line = LANES // planes
    line_count = cap // per_line
    tall = 16
    eye = as_bf16(iota((LANES, LANES), 0) == iota((LANES, LANES), 1))
    ones = jnp.ones((2 * LANES, LANES), bf16)
    unroll = 4

    def line(i, carry):
        def step(g, inner):
            for u in range(unroll):
                src = g * unroll + u
                row = grad_ref[pl.ds(src * line_count + i, 1), :]
                spread = []
                for piece in split(jnp.broadcast_to(row, (tall, LANES)), 2):
                    spread.append(
                        jnp.concatenate(
                            [
                                eye[m * tall : (m + 1) * tall, :] * piece
                                for m in range(LANES // tall)
                            ],
                            axis=0,
                        )
                    )
                values = mm(jnp.concatenate(spread, axis=1), ones)
                for q in range(per_line):
                    j = i * per_line + q
                    at = pl.ds(base_ref[j, src], 4)
                    w = w_ref[pl.ds(j * n + src, 1), :]
                    value = values[q * planes : (q + 1) * planes, :]
                    value = value.reshape(2, pairs, LANES)
                    held[at] = held[at] + jnp.concatenate(
                        [value * w[:, :LANES], value * w[:, LANES:]], axis=0
                    )
            return inner

        return lax.fori_loop(0, n // unroll, step, carry)

    lax.fori_loop(0, line_count, line, 0)
    copies = []
    for i in range(pairs):
        copy = pltpu.make_async_copy(held.at[:, i], out_ref.at[i], sem.at[i])
        copy.start()
        copies.append(copy)
    for copy in copies:
        copy.wait()


def body(
    visibilities,
    noise_weight,
    keep_flag,
    station_pairs,
    tile_owner,
    tile_offset,
    kernel_taps,
    gain_field,
    sky_grid,
):
    rows, _, channels = visibilities.shape
    taps = kernel_taps.shape[0]
    time_count = lax.axis_size("tm")
    group_count = lax.axis_size("bl")
    n = time_count * group_count
    cap = max(2, 2 * rows // n)
    _, facets, terms, cells = sky_grid.shape
    pairs = 2 * facets
    planes = pairs * terms
    tiles = cells // LANES
    group = gain_field.shape[1]
    stations = group * group_count
    both = ("tm", "bl")
    half = -(-channels // LANES) * LANES
    wide = 2 * half

    gain_turned = gain_field[0].transpose(1, 2, 0, 3)
    fields = taps + 2
    lines = 1 << (-(-fields * cap // LANES) - 1).bit_length()
    shift = jnp.full((1,), lax.axis_index("bl"), i32)
    send, row_table, col_table = pl.pallas_call(
        functools.partial(slots_kernel, n, cap, tiles, group, group_count),
        out_shape=(
            jax.ShapeDtypeStruct((n * lines, LANES), f32),
            jax.ShapeDtypeStruct((8, rows), f32),
            jax.ShapeDtypeStruct((rows, 8), f32),
        ),
        in_specs=[SMEM] + [VMEM] * 6,
        out_specs=(VMEM,) * 3,
        compiler_params=params(),
        cost_estimate=cost(10**9, 10**6),
        name="slots",
    )(
        shift,
        tile_owner.reshape(1, rows),
        tile_offset.reshape(1, rows),
        kernel_taps,
        station_pairs,
        noise_weight.reshape(1, rows),
        keep_flag.reshape(1, rows),
    )

    def exchange(x):
        x = x.reshape(n, -1, LANES)
        x = lax.all_to_all(x, both, split_axis=0, concat_axis=0, tiled=True)
        return x.reshape(-1, LANES)

    sky = (
        sky_grid.reshape(pairs, terms, tiles, LANES)
        .transpose(0, 2, 1, 3)
        .reshape(pairs, terms * tiles, LANES)
    )
    grid_shape = (terms * tiles, pairs, LANES)
    held, token = pl.pallas_call(
        load_kernel,
        out_shape=(
            pltpu.VMEM(grid_shape, f32),
            jax.ShapeDtypeStruct((8, LANES), f32),
        ),
        in_specs=[ANY],
        out_specs=(VMEM, VMEM),
        scratch_shapes=[pltpu.SemaphoreType.DMA((pairs,))],
        compiler_params=params(40),
        cost_estimate=cost(0, 2 * 10**7),
        name="load",
    )(sky)
    received, gain_turned, token = lax.optimization_barrier(
        (exchange(send), gain_turned, token)
    )
    gathered = [gain_turned]
    for k in range(1, group_count):
        gathered.append(
            lax.ppermute(
                gain_turned, "bl", [(i, (i + k) % group_count) for i in range(group_count)]
            )
        )
    base = received.reshape(n, lines * LANES)[:, (taps + 1) * cap : (taps + 2) * cap]
    base = jnp.clip(base.T.astype(i32), 0, tiles - 2) * terms
    slot_lines = n * cap * planes // LANES
    block_count = n * cap // LANES
    values, weights = pl.pallas_call(
        functools.partial(degrid_kernel, n, cap, taps),
        out_shape=(
            jax.ShapeDtypeStruct((slot_lines, LANES), f32),
            jax.ShapeDtypeStruct((n * cap, 2 * LANES), f32),
        ),
        in_specs=[SMEM, VMEM, VMEM],
        out_specs=(VMEM, pl.BlockSpec(memory_space=pltpu.HBM)),
        scratch_shapes=[
            pltpu.VMEM((n * cap, 2 * LANES), f32),
            pltpu.VMEM((lines * LANES, n), f32),
            pltpu.VMEM((block_count, planes, LANES), f32),
            pltpu.SemaphoreType.DMA((1,)),
        ],
        compiler_params=params(30),
        cost_estimate=cost(10**8, 5 * 10**7),
        name="degrid",
    )(base, received, held)
    values, *gathered = lax.optimization_barrier((values, *gathered))
    values, gain_here = lax.optimization_barrier((values, gain_field))
    back = exchange(values)
    below = lax.ppermute(gain_here, "tm", [(i, i + 1) for i in range(time_count - 1)])
    above = lax.ppermute(gain_here, "tm", [(i + 1, i) for i in range(time_count - 1)])

    vis_wide = jnp.pad(visibilities, ((0, 0), (0, 0), (0, half - channels))).reshape(
        rows, wide
    )
    partial_shape = jax.ShapeDtypeStruct((facets, 2, group, channels), f32)
    outs = pl.pallas_call(
        functools.partial(rows_kernel, n, cap, group_count),
        out_shape=(partial_shape,) * group_count
        + (jax.ShapeDtypeStruct((slot_lines, LANES), f32),),
        in_specs=[VMEM] * (4 + group_count),
        out_specs=(VMEM,) * (group_count + 1),
        scratch_shapes=[
            pltpu.VMEM((facets, stations, wide), f32),
            pltpu.VMEM((facets, 3 * planes, wide), bf16),
            pltpu.VMEM((facets, rows, wide), f32),
            pltpu.VMEM((facets, rows, wide), f32),
            pltpu.VMEM((facets, rows, wide), f32),
            pltpu.VMEM((rows, wide), f32),
            pltpu.VMEM((2 * rows, wide), bf16),
            pltpu.VMEM((2 * rows, wide), bf16),
            pltpu.VMEM((rows, wide), bf16),
            pltpu.VMEM((rows, wide), bf16),
        ],
        compiler_params=params(),
        cost_estimate=cost(2 * 10**10, 10**7),
        name="rowgrads",
    )(row_table, col_table, vis_wide, back, *gathered)

    *parts, send_grad = outs
    send_grad, below, above = lax.optimization_barrier((send_grad, below, above))
    zero = pl.pallas_call(
        clear_kernel,
        out_shape=pltpu.VMEM(grid_shape, f32),
        in_specs=[ANY],
        out_specs=VMEM,
        compiler_params=params(24),
        cost_estimate=cost(0, 2 * 10**7),
        name="clear",
    )(send_grad)
    got = exchange(send_grad)
    for k in range(1, group_count):
        parts[k] = lax.ppermute(
            parts[k], "bl", [(i, (i - k) % group_count) for i in range(group_count)]
        )
    grid, _ = pl.pallas_call(
        functools.partial(scatter_kernel, n, cap),
        out_shape=(
            jax.ShapeDtypeStruct((pairs, terms * tiles, LANES), f32),
            pltpu.VMEM(grid_shape, f32),
        ),
        in_specs=[SMEM, VMEM, VMEM, VMEM],
        out_specs=(ANY, VMEM),
        scratch_shapes=[pltpu.SemaphoreType.DMA((pairs,))],
        input_output_aliases={3: 1},
        compiler_params=params(24),
        cost_estimate=cost(10**8, 10**8),
        name="scatter",
    )(base, got, weights, zero)
    grid, *parts = lax.optimization_barrier((grid, *parts))
    total = parts[0]
    for part in parts[1:]:
        total = total + part
    grid_gradient = (
        grid.reshape(pairs, tiles, terms, LANES)
        .transpose(0, 2, 1, 3)
        .reshape(sky_grid.shape)
    )
    when = lax.axis_index("tm")
    prior = jnp.where(when > 0, gain_field - below, 0.0)
    prior = prior - jnp.where(when < time_count - 1, above - gain_field, 0.0)
    gain_gradient = total.transpose(2, 0, 1, 3)[None] + smoothness * prior
    return (gain_gradient, grid_gradient)


def solution(mesh):
    return jax.shard_map(
        body,
        mesh=mesh,
        in_specs=(
            P(("tm", "bl"), None, None),
            P(("tm", "bl")),
            P(("tm", "bl")),
            P(None, ("tm", "bl")),
            P(("tm", "bl"), None),
            P(("tm", "bl")),
            P(None, ("tm", "bl")),
            P("tm", "bl", None, None, None),
            P(None, None, None, ("tm", "bl")),
        ),
        out_specs=(P("tm", "bl", None, None, None), P(None, None, None, ("tm", "bl"))),
        check_vma=False,
    )
```

```python
import functools

import jax
import jax.numpy as jnp
from jax import lax
from jax.experimental import pallas as pl
from jax.experimental.pallas import tpu as pltpu
from jax.sharding import PartitionSpec as P

smoothness = 4.0
LANES = 128
f32 = jnp.float32
bf16 = jnp.bfloat16
i32 = jnp.int32
VMEM = pl.BlockSpec(memory_space=pltpu.VMEM)
SMEM = pl.BlockSpec(memory_space=pltpu.SMEM)
ANY = pl.BlockSpec(memory_space=pl.ANY)
CHUNK = 16


def iota(shape, dim):
    return lax.broadcasted_iota(i32, shape, dim)


def as_bf16(mask):
    return jnp.where(mask, 1.0, 0.0).astype(bf16)


def split(x, pieces):
    out = []
    for _ in range(pieces - 1):
        head = x.astype(bf16)
        out.append(head)
        x = x - head.astype(f32)
    out.append(x.astype(bf16))
    return out


def mm(a, b):
    return jnp.dot(a, b, preferred_element_type=f32)


def mm_nt(a, b):
    return lax.dot_general(a, b, (((1,), (1,)), ((), ())), preferred_element_type=f32)


def div(x, k):
    return x >> (k.bit_length() - 1) if k & (k - 1) == 0 else x // k


def mod(x, k):
    return x & (k - 1) if k & (k - 1) == 0 else x - x // k * k


def params(mib=60):
    return pltpu.CompilerParams(vmem_limit_bytes=mib << 20)


def cost(flops, byte_count):
    return pl.CostEstimate(flops=flops, bytes_accessed=byte_count, transcendentals=0)


def read_wide(ref, count):
    per = ref.shape[0] // count
    return jnp.concatenate(
        [ref[pl.ds(i, count, stride=per), :] for i in range(per)], axis=1
    )


def write_wide(ref, value):
    count = value.shape[0]
    per = ref.shape[0] // count
    for i in range(per):
        ref[pl.ds(i, count, stride=per), :] = value[:, i * LANES : (i + 1) * LANES]


def slots_kernel(
    n, cap, tiles, group, group_count,
    shift_ref, owner_ref, offset_ref, taps_ref, pairs_ref, noise_ref, keep_ref,
    send_ref, rows_ref, cols_ref,
):
    rows = owner_ref.shape[1]
    taps = taps_ref.shape[0]
    width = send_ref.shape[0] // n * LANES
    owner = owner_ref[...]
    hit = iota((n, rows), 0) == owner
    onehot = as_bf16(hit)
    earlier = as_bf16(iota((rows, rows), 0) < iota((rows, rows), 1))
    before = mm(onehot, earlier)
    rank = jnp.sum(jnp.where(hit, before, 0.0), axis=0, keepdims=True)
    at_rank = iota((cap, rows), 0) == rank.astype(i32)
    offset = offset_ref[...]
    base = jnp.minimum(offset // LANES, tiles - 2)
    low = offset - base * LANES
    fields = [taps_ref[k : k + 1, :] for k in range(taps)]
    fields += [low.astype(f32), base.astype(f32)]
    parts = [jnp.where(at_rank, v, 0.0) for v in fields]
    spare = width - len(parts) * cap
    if spare:
        parts.append(jnp.zeros((spare, rows), f32))
    total = None
    for piece in split(jnp.concatenate(parts, axis=0), 3):
        term = mm_nt(onehot, piece)
        total = term if total is None else total + term
    write_wide(send_ref, total)
    station = pairs_ref[...]
    turn = shift_ref[0] - station // group + group_count
    turn = jnp.where(turn >= group_count, turn - group_count, turn)
    local = (turn * group + (station - station // group * group)).astype(f32)
    scale = noise_ref[...] * keep_ref[...].astype(f32)
    table = jnp.concatenate(
        [owner.astype(f32), rank, local, scale, jnp.zeros((3, rows), f32)], axis=0
    )
    rows_ref[...] = table
    cols_ref[...] = table.T


def turn_fields(n, cap, count, recv_ref, turn_s):
    per_block = LANES // n
    turn_s[...] = read_wide(recv_ref, n).T
    return [
        jnp.concatenate(
            [
                turn_s[pl.ds(k * cap + q, cap // per_block, stride=per_block), :]
                for q in range(per_block)
            ],
            axis=1,
        )
        for k in range(count)
    ]


def each_slot(n, visit, carry, jb):
    per_block = LANES // n
    unroll = min(n, 32)
    for q in range(per_block):
        j = jb * per_block + q

        def step(g, inner):
            first = g * unroll
            for u in range(unroll):
                inner = visit(inner, j, first + u, u, q * n + first)
            return inner

        if n == unroll:
            carry = step(0, carry)
        else:
            carry = lax.fori_loop(0, n // unroll, step, carry)
    return carry


def degrid_kernel(
    n, cap, taps,
    base_ref, recv_ref, sky_ref, out_ref, w_ref,
    held_re, held_im, w_s, turn_s, blocks, sem,
):
    halves = (held_re, held_im)
    facets = held_re.shape[1]
    planes = 4 * facets
    copies = []
    for x, held in enumerate(halves):
        mine = []
        for f in range(facets):
            i = x * facets + f
            copy = pltpu.make_async_copy(sky_ref.at[i], held.at[:, f], sem.at[i])
            copy.start()
            mine.append(copy)
        copies.append(mine)
    per_block = LANES // n
    block_count = cap // per_block
    fields = turn_fields(n, cap, taps + 1, recv_ref, turn_s)
    line = iota((2 * LANES, LANES), 0).astype(f32)
    for jb in range(block_count):
        place = line - fields[taps][jb : jb + 1, :]
        w = jnp.zeros((2 * LANES, LANES), f32)
        for k in range(taps):
            w = jnp.where(place == float(k), fields[k][jb : jb + 1, :], w)
        w_s[jb * LANES : (jb + 1) * LANES, :] = w.T
    save = pltpu.make_async_copy(w_s, w_ref, sem.at[2 * facets])
    save.start()
    lane3 = iota((2, facets, LANES), 2)
    for x, held in enumerate(halves):
        for copy in copies[x]:
            copy.wait()

        def visit(acc, j, src, u, first):
            w = w_s[pl.ds(j * n + src, 1), :]
            window = held[pl.ds(base_ref[j, src], 4)]
            prod = window[0:2] * w[:, :LANES] + window[2:4] * w[:, LANES:]
            return jnp.where(
                lane3 == first + u, jnp.sum(prod, axis=2, keepdims=True), acc
            )

        def block(jb, carry):
            acc = each_slot(n, visit, jnp.zeros((2, facets, LANES), f32), jb)
            for t in range(2):
                blocks[jb, pl.ds((2 * t + x) * facets, facets), :] = acc[t]
            return carry

        lax.fori_loop(0, block_count, block, 0)
    turned = [blocks[jb].T for jb in range(block_count)]
    pieces = []
    for j in range(cap):
        jb, lo = j * n // LANES, j * n % LANES
        pieces.append(turned[jb][lo : lo + n, :planes])
    per_line = LANES // planes
    per = cap // per_line
    for i in range(per):
        wide_line = jnp.concatenate(pieces[i * per_line : (i + 1) * per_line], axis=1)
        out_ref[pl.ds(i, n, stride=per), :] = wide_line
    save.wait()


def rows_kernel(
    n, cap, group_count,
    rows_ref, cols_ref, vis_ref, back_ref, *rest,
):
    gain_refs = rest[:group_count]
    out_refs = rest[group_count : 2 * group_count]
    send_ref = rest[2 * group_count]
    gains, spec, a_s, b_s, m_s, e_s, glr_hi, glr_lo, gm_hi, gm_lo = rest[
        2 * group_count + 1 :
    ]
    facets, _, group, channels = gain_refs[0].shape
    rows = cols_ref.shape[0]
    stations = group * group_count
    planes = 4 * facets
    pairs = 2 * facets
    half = m_s.shape[2] // 2
    wide = 2 * half
    cols = cols_ref[...]
    owner_col, rank_col = cols[:, 0:1].astype(i32), cols[:, 1:2].astype(i32)
    first_col, second_col = cols[:, 2:3].astype(i32), cols[:, 3:4].astype(i32)

    gains[...] = jnp.zeros(gains.shape, f32)
    for k in range(group_count):
        for f in range(facets):
            for x in range(2):
                gains[f, k * group : (k + 1) * group, x * half : x * half + channels] = (
                    gain_refs[k][f, x]
                )

    owner3 = as_bf16(mod(iota((1, 3 * n), 1), n) == owner_col)
    per_line = LANES // planes
    line_count = cap // per_line
    slot_of = div(iota((1, LANES), 1), planes) - rank_col
    degrid = jnp.zeros((rows, LANES), f32)
    for i in range(line_count):
        line = jnp.concatenate(split(back_ref[pl.ds(i, n, stride=line_count), :], 3), axis=0)
        degrid = degrid + jnp.where(slot_of == -i * per_line, mm(owner3, line), 0.0)
    fold = as_bf16(mod(iota((3 * LANES, planes), 0), planes) == iota((3 * LANES, planes), 1))
    degrid = mm(jnp.concatenate(split(degrid, 3), axis=1), fold)
    term_scale = jnp.where(iota((1, planes), 1) >= pairs, 1.0 / (channels - 1), 1.0)
    d3 = jnp.concatenate(split(degrid * term_scale, 3), axis=1)

    lane_st = mod(iota((1, 3 * stations), 1), stations)
    first3 = as_bf16(lane_st == first_col)
    second3 = as_bf16(lane_st == second_col)
    plane = mod(iota((3 * planes, wide), 0), planes)
    lane_w = iota((3 * planes, wide), 1)
    chan = jnp.where(lane_w >= half, lane_w - half, lane_w)
    side = jnp.where(lane_w >= half, 1, 0)
    value = jnp.where(plane >= pairs, 2 * chan - (channels - 1), 1).astype(f32)
    live = (chan < channels) & (div(mod(plane, pairs), facets) == side)
    value = jnp.where(live, value, 0.0)
    facet_of = mod(plane, facets)
    chunks = [pl.ds(i * CHUNK, CHUNK) for i in range(rows // CHUNK)]

    def gather(f):
        table = jnp.concatenate(split(gains[f], 3), axis=0)
        spec[f] = jnp.where(facet_of == f, value, 0.0).astype(bf16)
        a_s[f] = mm(first3, table)
        b_s[f] = mm(second3, table)
        m_s[f] = mm(d3, spec[f])

    def load(f, at):
        return (
            a_s[f, at, :half], a_s[f, at, half:],
            b_s[f, at, :half], b_s[f, at, half:],
            m_s[f, at, :half], m_s[f, at, half:],
        )

    def predict(f):
        for at in chunks:
            a_re, a_im, b_re, b_im, m_re, m_im = load(f, at)
            p_re = a_re * b_re + a_im * b_im
            p_im = a_im * b_re - a_re * b_im
            e_s[at, :half] += p_re * m_re - p_im * m_im
            e_s[at, half:] += p_re * m_im + p_im * m_re

    e_s[...] = -vis_ref[...].astype(f32)
    gather(0)

    def forward(f, carry):
        gather(f + 1)
        predict(f)
        return carry

    lax.fori_loop(0, facets - 1, forward, 0)
    predict(facets - 1)
    e_s[...] = e_s[...] * cols[:, 4:5]

    block = min(rows, 128)
    block_count = rows // block
    station_row = iota((stations, rows), 0)
    to_first = as_bf16(station_row == rows_ref[2:3, :].astype(i32))
    to_second = as_bf16(station_row == rows_ref[3:4, :].astype(i32))
    to_station = []
    for c in range(block_count):
        part = slice(c * block, (c + 1) * block)
        to_station.append(jnp.concatenate([to_first[:, part], to_second[:, part]], axis=1))

    def put(hi_ref, lo_ref, at, lanes, value):
        hi = value.astype(bf16)
        hi_ref[at, lanes] = hi
        lo_ref[at, lanes] = (value - hi.astype(f32)).astype(bf16)

    re_lanes, im_lanes = slice(0, half), slice(half, wide)

    def grads(f, grad_degrid):
        summed = jnp.zeros((stations, wide), f32)
        table = spec[f, :planes, :]
        parts = []
        for c in range(block_count):
            for i in range(block // CHUNK):
                at = pl.ds(c * block + i * CHUNK, CHUNK)
                left = pl.ds(2 * c * block + i * CHUNK, CHUNK)
                right = pl.ds((2 * c + 1) * block + i * CHUNK, CHUNK)
                e_re, e_im = e_s[at, :half], e_s[at, half:]
                a_re, a_im, b_re, b_im, m_re, m_im = load(f, at)
                t_re = e_re * m_re + e_im * m_im
                t_im = e_im * m_re - e_re * m_im
                p_re = a_re * b_re + a_im * b_im
                p_im = a_im * b_re - a_re * b_im
                put(glr_hi, glr_lo, left, re_lanes, t_re * b_re - t_im * b_im)
                put(glr_hi, glr_lo, left, im_lanes, t_re * b_im + t_im * b_re)
                put(glr_hi, glr_lo, right, re_lanes, t_re * a_re + t_im * a_im)
                put(glr_hi, glr_lo, right, im_lanes, t_re * a_im - t_im * a_re)
                put(gm_hi, gm_lo, at, re_lanes, e_re * p_re + e_im * p_im)
                put(gm_hi, gm_lo, at, im_lanes, e_im * p_re - e_re * p_im)
            both = pl.ds(2 * c * block, 2 * block)
            here = pl.ds(c * block, block)
            summed = summed + (
                mm(to_station[c], glr_hi[both, :]) + mm(to_station[c], glr_lo[both, :])
            )
            parts.append(mm_nt(gm_hi[here, :], table) + mm_nt(gm_lo[here, :], table))
        for k in range(group_count):
            for x in range(2):
                out_refs[k][f, x] = summed[
                    k * group : (k + 1) * group, x * half : x * half + channels
                ]
        return grad_degrid + jnp.concatenate(parts, axis=0)

    grad_degrid = lax.fori_loop(0, facets, grads, jnp.zeros((rows, planes), f32))
    grad3 = jnp.concatenate(split(grad_degrid * term_scale, 3), axis=1)
    spread = as_bf16(
        mod(iota((3 * planes, LANES), 0), planes) == mod(iota((3 * planes, LANES), 1), planes)
    )
    heads = [h.astype(f32) for h in split(mm(grad3, spread), 2)]
    owner_rows = as_bf16(iota((n, rows), 0) == rows_ref[0:1, :].astype(i32))
    for i in range(line_count):
        here = slot_of == -i * per_line
        placed = jnp.concatenate(
            [jnp.where(here, h, 0.0).astype(bf16) for h in heads], axis=1
        )
        total = mm(owner_rows, placed)
        send_ref[pl.ds(i, n, stride=line_count), :] = total[:, :LANES] + total[:, LANES:]


def scatter_kernel(
    n, cap, base_ref, grad_ref, w_ref, out_ref, held_re, held_im, blocks, sem
):
    halves = (held_re, held_im)
    facets = held_re.shape[1]
    planes = 4 * facets
    fill = 64

    def clear(i, carry):
        for held in halves:
            held[pl.ds(i * fill, fill)] = jnp.zeros((fill, facets, LANES), f32)
        return carry

    lax.fori_loop(0, held_re.shape[0] // fill, clear, 0)
    per_line = LANES // planes
    per = cap // per_line
    pieces = []
    for i in range(per):
        line = grad_ref[pl.ds(i, n, stride=per), :]
        for q in range(per_line):
            pieces.append(line[:, q * planes : (q + 1) * planes])
    per_block = LANES // n
    block_count = cap // per_block
    for jb in range(block_count):
        mine = pieces[jb * per_block : (jb + 1) * per_block]
        joined = mine[0] if per_block == 1 else jnp.concatenate(mine, axis=0)
        blocks[jb] = joined.T
    lane3 = iota((2, facets, LANES), 2)
    copies = []
    for x, held in enumerate(halves):

        def block(jb, carry):
            values = jnp.stack(
                [blocks[jb, pl.ds((2 * t + x) * facets, facets), :] for t in range(2)]
            )

            def visit(inner, j, src, u, first):
                at = pl.ds(base_ref[j, src], 4)
                w = w_ref[pl.ds(j * n + src, 1), :]
                value = jnp.sum(
                    jnp.where(lane3 == first + u, values, 0.0), axis=2, keepdims=True
                )
                held[at] = held[at] + jnp.concatenate(
                    [value * w[:, :LANES], value * w[:, LANES:]], axis=0
                )
                return inner

            return each_slot(n, visit, carry, jb)

        lax.fori_loop(0, block_count, block, 0)
        for f in range(facets):
            i = x * facets + f
            copy = pltpu.make_async_copy(held.at[:, f], out_ref.at[i], sem.at[i])
            copy.start()
            copies.append(copy)
    for copy in copies:
        copy.wait()


def body(
    visibilities,
    noise_weight,
    keep_flag,
    station_pairs,
    tile_owner,
    tile_offset,
    kernel_taps,
    gain_field,
    sky_grid,
):
    rows, _, channels = visibilities.shape
    taps = kernel_taps.shape[0]
    time_count = lax.axis_size("tm")
    group_count = lax.axis_size("bl")
    n = time_count * group_count
    cap = max(2, 2 * rows // n)
    _, facets, terms, cells = sky_grid.shape
    pairs = 2 * facets
    planes = pairs * terms
    tiles = cells // LANES
    group = gain_field.shape[1]
    stations = group * group_count
    both = ("tm", "bl")
    half = -(-channels // LANES) * LANES
    wide = 2 * half

    gain_turned = gain_field[0].transpose(1, 2, 0, 3)
    fields = taps + 2
    lines = 1 << (-(-fields * cap // LANES) - 1).bit_length()
    shift = jnp.full((1,), lax.axis_index("bl"), i32)
    send, row_table, col_table = pl.pallas_call(
        functools.partial(slots_kernel, n, cap, tiles, group, group_count),
        out_shape=(
            jax.ShapeDtypeStruct((n * lines, LANES), f32),
            jax.ShapeDtypeStruct((8, rows), f32),
            jax.ShapeDtypeStruct((rows, 8), f32),
        ),
        in_specs=[SMEM] + [VMEM] * 6,
        out_specs=(VMEM,) * 3,
        compiler_params=params(),
        cost_estimate=cost(10**9, 10**6),
        name="slots",
    )(
        shift,
        tile_owner.reshape(1, rows),
        tile_offset.reshape(1, rows),
        kernel_taps,
        station_pairs,
        noise_weight.reshape(1, rows),
        keep_flag.reshape(1, rows),
    )

    def exchange(x):
        x = x.reshape(n, -1, LANES)
        x = lax.all_to_all(x, both, split_axis=0, concat_axis=0, tiled=True)
        return x.reshape(-1, LANES)

    sky = (
        sky_grid.reshape(pairs, terms, tiles, LANES)
        .transpose(0, 2, 1, 3)
        .reshape(pairs, terms * tiles, LANES)
    )
    send, gain_turned = lax.optimization_barrier((send, gain_turned))
    received = exchange(send)
    gathered = [gain_turned]
    for k in range(1, group_count):
        gathered.append(
            lax.ppermute(
                gain_turned, "bl", [(i, (i + k) % group_count) for i in range(group_count)]
            )
        )
    base = received.reshape(n, lines * LANES)[:, (taps + 1) * cap : (taps + 2) * cap]
    base = jnp.clip(base.T.astype(i32), 0, tiles - 2) * terms
    slot_lines = n * cap * planes // LANES
    block_count = n * cap // LANES
    values, weights = pl.pallas_call(
        functools.partial(degrid_kernel, n, cap, taps),
        out_shape=(
            jax.ShapeDtypeStruct((slot_lines, LANES), f32),
            jax.ShapeDtypeStruct((n * cap, 2 * LANES), f32),
        ),
        in_specs=[SMEM, VMEM, ANY],
        out_specs=(VMEM, ANY),
        scratch_shapes=[
            pltpu.VMEM((terms * tiles, facets, LANES), f32),
            pltpu.VMEM((terms * tiles, facets, LANES), f32),
            pltpu.VMEM((n * cap, 2 * LANES), f32),
            pltpu.VMEM((lines * LANES, n), f32),
            pltpu.VMEM((block_count, planes, LANES), f32),
            pltpu.SemaphoreType.DMA((pairs + 1,)),
        ],
        compiler_params=params(),
        cost_estimate=cost(10**8, 7 * 10**7),
        name="degrid",
    )(base, received, sky)
    values, *gathered = lax.optimization_barrier((values, *gathered))
    values, gain_here = lax.optimization_barrier((values, gain_field))
    back = exchange(values)
    below = lax.ppermute(gain_here, "tm", [(i, i + 1) for i in range(time_count - 1)])
    above = lax.ppermute(gain_here, "tm", [(i + 1, i) for i in range(time_count - 1)])

    vis_wide = jnp.pad(visibilities, ((0, 0), (0, 0), (0, half - channels))).reshape(
        rows, wide
    )
    partial_shape = jax.ShapeDtypeStruct((facets, 2, group, channels), f32)
    outs = pl.pallas_call(
        functools.partial(rows_kernel, n, cap, group_count),
        out_shape=(partial_shape,) * group_count
        + (jax.ShapeDtypeStruct((slot_lines, LANES), f32),),
        in_specs=[VMEM] * (4 + group_count),
        out_specs=(VMEM,) * (group_count + 1),
        scratch_shapes=[
            pltpu.VMEM((facets, stations, wide), f32),
            pltpu.VMEM((facets, 3 * planes, wide), bf16),
            pltpu.VMEM((facets, rows, wide), f32),
            pltpu.VMEM((facets, rows, wide), f32),
            pltpu.VMEM((facets, rows, wide), f32),
            pltpu.VMEM((rows, wide), f32),
            pltpu.VMEM((2 * rows, wide), bf16),
            pltpu.VMEM((2 * rows, wide), bf16),
            pltpu.VMEM((rows, wide), bf16),
            pltpu.VMEM((rows, wide), bf16),
        ],
        compiler_params=params(),
        cost_estimate=cost(2 * 10**10, 10**7),
        name="rowgrads",
    )(row_table, col_table, vis_wide, back, *gathered)

    *parts, send_grad = outs
    send_grad, below, above = lax.optimization_barrier((send_grad, below, above))
    got = exchange(send_grad)
    for k in range(1, group_count):
        parts[k] = lax.ppermute(
            parts[k], "bl", [(i, (i - k) % group_count) for i in range(group_count)]
        )
    grid = pl.pallas_call(
        functools.partial(scatter_kernel, n, cap),
        out_shape=jax.ShapeDtypeStruct((pairs, terms * tiles, LANES), f32),
        in_specs=[SMEM, VMEM, VMEM],
        out_specs=ANY,
        scratch_shapes=[
            pltpu.VMEM((terms * tiles, facets, LANES), f32),
            pltpu.VMEM((terms * tiles, facets, LANES), f32),
            pltpu.VMEM((block_count, planes, LANES), f32),
            pltpu.SemaphoreType.DMA((pairs,)),
        ],
        compiler_params=params(),
        cost_estimate=cost(10**8, 10**8),
        name="scatter",
    )(base, got, weights)
    grid, *parts = lax.optimization_barrier((grid, *parts))
    total = parts[0]
    for part in parts[1:]:
        total = total + part
    grid_gradient = (
        grid.reshape(pairs, tiles, terms, LANES)
        .transpose(0, 2, 1, 3)
        .reshape(sky_grid.shape)
    )
    when = lax.axis_index("tm")
    prior = jnp.where(when > 0, gain_field - below, 0.0)
    prior = prior - jnp.where(when < time_count - 1, above - gain_field, 0.0)
    gain_gradient = total.transpose(2, 0, 1, 3)[None] + smoothness * prior
    return (gain_gradient, grid_gradient)


def solution(mesh):
    return jax.shard_map(
        body,
        mesh=mesh,
        in_specs=(
            P(("tm", "bl"), None, None),
            P(("tm", "bl")),
            P(("tm", "bl")),
            P(None, ("tm", "bl")),
            P(("tm", "bl"), None),
            P(("tm", "bl")),
            P(None, ("tm", "bl")),
            P("tm", "bl", None, None, None),
            P(None, None, None, ("tm", "bl")),
        ),
        out_specs=(P("tm", "bl", None, None, None), P(None, None, None, ("tm", "bl"))),
        check_vma=False,
    )
```

```python
import functools

import jax
import jax.numpy as jnp
from jax import lax
from jax.experimental import pallas as pl
from jax.experimental.pallas import tpu as pltpu
from jax.sharding import PartitionSpec as P

smoothness = 4.0
LANES = 128
f32 = jnp.float32
bf16 = jnp.bfloat16
i32 = jnp.int32
VMEM = pl.BlockSpec(memory_space=pltpu.VMEM)
SMEM = pl.BlockSpec(memory_space=pltpu.SMEM)
ANY = pl.BlockSpec(memory_space=pl.ANY)
CHUNK = 16
PAIR = 2


def iota(shape, dim):
    return lax.broadcasted_iota(i32, shape, dim)


def as_bf16(mask):
    return jnp.where(mask, 1.0, 0.0).astype(bf16)


def split(x, pieces):
    out = []
    for _ in range(pieces - 1):
        head = x.astype(bf16)
        out.append(head)
        x = x - head.astype(f32)
    out.append(x.astype(bf16))
    return out


def mm(a, b):
    return jnp.dot(a, b, preferred_element_type=f32)


def mm_nt(a, b):
    return lax.dot_general(a, b, (((1,), (1,)), ((), ())), preferred_element_type=f32)


def div(x, k):
    return x >> (k.bit_length() - 1) if k & (k - 1) == 0 else x // k


def mod(x, k):
    return x & (k - 1) if k & (k - 1) == 0 else x - x // k * k


def params(mib=60):
    return pltpu.CompilerParams(vmem_limit_bytes=mib << 20)


def cost(flops, byte_count):
    return pl.CostEstimate(flops=flops, bytes_accessed=byte_count, transcendentals=0)


def read_wide(ref, count):
    per = ref.shape[0] // count
    return jnp.concatenate(
        [ref[pl.ds(i, count, stride=per), :] for i in range(per)], axis=1
    )


def write_wide(ref, value):
    count = value.shape[0]
    per = ref.shape[0] // count
    for i in range(per):
        ref[pl.ds(i, count, stride=per), :] = value[:, i * LANES : (i + 1) * LANES]


def slots_kernel(
    n, cap, tiles, group, group_count,
    shift_ref, owner_ref, offset_ref, taps_ref, pairs_ref, noise_ref, keep_ref,
    send_ref, rows_ref, cols_ref,
):
    rows = owner_ref.shape[1]
    taps = taps_ref.shape[0]
    width = send_ref.shape[0] // n * LANES
    owner = owner_ref[...]
    hit = iota((n, rows), 0) == owner
    onehot = as_bf16(hit)
    earlier = as_bf16(iota((rows, rows), 0) < iota((rows, rows), 1))
    before = mm(onehot, earlier)
    rank = jnp.sum(jnp.where(hit, before, 0.0), axis=0, keepdims=True)
    at_rank = iota((cap, rows), 0) == rank.astype(i32)
    offset = offset_ref[...]
    base = jnp.minimum(offset // LANES, tiles - 2)
    low = offset - base * LANES
    fields = [taps_ref[k : k + 1, :] for k in range(taps)]
    fields += [low.astype(f32), base.astype(f32)]
    parts = [jnp.where(at_rank, v, 0.0) for v in fields]
    spare = width - len(parts) * cap
    if spare:
        parts.append(jnp.zeros((spare, rows), f32))
    total = None
    for piece in split(jnp.concatenate(parts, axis=0), 3):
        term = mm_nt(onehot, piece)
        total = term if total is None else total + term
    write_wide(send_ref, total)
    station = pairs_ref[...]
    turn = shift_ref[0] - station // group + group_count
    turn = jnp.where(turn >= group_count, turn - group_count, turn)
    local = (turn * group + (station - station // group * group)).astype(f32)
    scale = noise_ref[...] * keep_ref[...].astype(f32)
    table = jnp.concatenate(
        [owner.astype(f32), rank, local, scale, jnp.zeros((3, rows), f32)], axis=0
    )
    rows_ref[...] = table
    cols_ref[...] = table.T


def turn_fields(n, cap, count, recv_ref, turn_s):
    per_block = LANES // n
    turn_s[...] = read_wide(recv_ref, n).T
    return [
        jnp.concatenate(
            [
                turn_s[pl.ds(k * cap + q, cap // per_block, stride=per_block), :]
                for q in range(per_block)
            ],
            axis=1,
        )
        for k in range(count)
    ]


def each_slot(n, visit, carry, jb, group):
    per_block = LANES // n
    unroll = min(n, 32)
    for q in range(per_block):
        j = jb * per_block + q

        def step(g, inner):
            first = g * unroll
            for u in range(0, unroll, group):
                slots = [(j, first + v, q * n + first + v) for v in range(u, u + group)]
                inner = visit(inner, slots)
            return inner

        if n == unroll:
            carry = step(0, carry)
        else:
            carry = lax.fori_loop(0, n // unroll, step, carry)
    return carry


def degrid_kernel(
    n, cap, taps,
    base_ref, recv_ref, sky_ref, out_ref, w_ref,
    held_re, held_im, w_s, turn_s, blocks, sem,
):
    halves = (held_re, held_im)
    facets = held_re.shape[1]
    planes = 4 * facets
    copies = []
    for x, held in enumerate(halves):
        mine = []
        for f in range(facets):
            i = x * facets + f
            copy = pltpu.make_async_copy(sky_ref.at[i], held.at[:, f], sem.at[i])
            copy.start()
            mine.append(copy)
        copies.append(mine)
    per_block = LANES // n
    block_count = cap // per_block
    fields = turn_fields(n, cap, taps + 1, recv_ref, turn_s)
    line = iota((2 * LANES, LANES), 0).astype(f32)
    for jb in range(block_count):
        place = line - fields[taps][jb : jb + 1, :]
        w = jnp.zeros((2 * LANES, LANES), f32)
        for k in range(taps):
            w = jnp.where(place == float(k), fields[k][jb : jb + 1, :], w)
        w_s[jb * LANES : (jb + 1) * LANES, :] = w.T
    save = pltpu.make_async_copy(w_s, w_ref, sem.at[2 * facets])
    save.start()
    lane3 = iota((2, facets, LANES), 2)
    for x, held in enumerate(halves):
        for copy in copies[x]:
            copy.wait()

        def visit(acc, slots):
            ((j, src, lane),) = slots
            w = w_s[pl.ds(j * n + src, 1), :]
            window = held[pl.ds(base_ref[j, src], 4)]
            prod = window[0:2] * w[:, :LANES] + window[2:4] * w[:, LANES:]
            return jnp.where(
                lane3 == lane, jnp.sum(prod, axis=2, keepdims=True), acc
            )

        def block(jb, carry):
            acc = each_slot(n, visit, jnp.zeros((2, facets, LANES), f32), jb, 1)
            for t in range(2):
                blocks[jb, pl.ds((2 * t + x) * facets, facets), :] = acc[t]
            return carry

        lax.fori_loop(0, block_count, block, 0)
    turned = [blocks[jb].T for jb in range(block_count)]
    pieces = []
    for j in range(cap):
        jb, lo = j * n // LANES, j * n % LANES
        pieces.append(turned[jb][lo : lo + n, :planes])
    per_line = LANES // planes
    per = cap // per_line
    for i in range(per):
        wide_line = jnp.concatenate(pieces[i * per_line : (i + 1) * per_line], axis=1)
        out_ref[pl.ds(i, n, stride=per), :] = wide_line
    save.wait()


def rows_kernel(
    n, cap, group_count,
    rows_ref, cols_ref, vis_ref, back_ref, *rest,
):
    gain_refs = rest[:group_count]
    out_refs = rest[group_count : 2 * group_count]
    send_ref = rest[2 * group_count]
    gains, spec, a_s, b_s, m_s, p_s, e_s, glr_hi, glr_lo, gm_hi, gm_lo = rest[
        2 * group_count + 1 :
    ]
    facets, _, group, channels = gain_refs[0].shape
    rows = cols_ref.shape[0]
    stations = group * group_count
    planes = 4 * facets
    pairs = 2 * facets
    half = m_s.shape[2] // 2
    wide = 2 * half
    cols = cols_ref[...]
    owner_col, rank_col = cols[:, 0:1].astype(i32), cols[:, 1:2].astype(i32)
    first_col, second_col = cols[:, 2:3].astype(i32), cols[:, 3:4].astype(i32)

    gains[...] = jnp.zeros(gains.shape, f32)
    for k in range(group_count):
        for f in range(facets):
            for x in range(2):
                gains[f, k * group : (k + 1) * group, x * half : x * half + channels] = (
                    gain_refs[k][f, x]
                )

    owner3 = as_bf16(mod(iota((1, 3 * n), 1), n) == owner_col)
    per_line = LANES // planes
    line_count = cap // per_line
    slot_of = div(iota((1, LANES), 1), planes) - rank_col
    degrid = jnp.zeros((rows, LANES), f32)
    for i in range(line_count):
        line = jnp.concatenate(split(back_ref[pl.ds(i, n, stride=line_count), :], 3), axis=0)
        degrid = degrid + jnp.where(slot_of == -i * per_line, mm(owner3, line), 0.0)
    fold = as_bf16(mod(iota((3 * LANES, planes), 0), planes) == iota((3 * LANES, planes), 1))
    degrid = mm(jnp.concatenate(split(degrid, 3), axis=1), fold)
    term_scale = jnp.where(iota((1, planes), 1) >= pairs, 1.0 / (channels - 1), 1.0)
    d3 = jnp.concatenate(split(degrid * term_scale, 3), axis=1)

    lane_st = mod(iota((1, 3 * stations), 1), stations)
    first3 = as_bf16(lane_st == first_col)
    second3 = as_bf16(lane_st == second_col)
    plane = mod(iota((3 * planes, wide), 0), planes)
    lane_w = iota((3 * planes, wide), 1)
    chan = jnp.where(lane_w >= half, lane_w - half, lane_w)
    side = jnp.where(lane_w >= half, 1, 0)
    value = jnp.where(plane >= pairs, 2 * chan - (channels - 1), 1).astype(f32)
    live = (chan < channels) & (div(mod(plane, pairs), facets) == side)
    value = jnp.where(live, value, 0.0)
    facet_of = mod(plane, facets)
    chunks = [pl.ds(i * CHUNK, CHUNK) for i in range(rows // CHUNK)]

    def gather(f):
        table = jnp.concatenate(split(gains[f], 3), axis=0)
        spec[f] = jnp.where(facet_of == f, value, 0.0).astype(bf16)
        a_s[f] = mm(first3, table)
        b_s[f] = mm(second3, table)
        m_s[f] = mm(d3, spec[f])

    def load(f, at):
        return (
            a_s[f, at, :half], a_s[f, at, half:],
            b_s[f, at, :half], b_s[f, at, half:],
            m_s[f, at, :half], m_s[f, at, half:],
        )

    def predict(f):
        for at in chunks:
            a_re, a_im, b_re, b_im, m_re, m_im = load(f, at)
            p_re = a_re * b_re + a_im * b_im
            p_im = a_im * b_re - a_re * b_im
            p_s[f, at, :half] = p_re
            p_s[f, at, half:] = p_im
            e_s[at, :half] += p_re * m_re - p_im * m_im
            e_s[at, half:] += p_re * m_im + p_im * m_re

    e_s[...] = -vis_ref[...].astype(f32)
    gather(0)

    for f in range(facets):
        if f + 1 < facets:
            gather(f + 1)
        predict(f)
    e_s[...] = e_s[...] * cols[:, 4:5]

    block = min(rows, 128)
    block_count = rows // block
    station_row = iota((stations, rows), 0)
    to_first = as_bf16(station_row == rows_ref[2:3, :].astype(i32))
    to_second = as_bf16(station_row == rows_ref[3:4, :].astype(i32))
    to_station = []
    for c in range(block_count):
        part = slice(c * block, (c + 1) * block)
        to_station.append(jnp.concatenate([to_first[:, part], to_second[:, part]], axis=1))

    def put(hi_ref, lo_ref, at, lanes, value):
        hi = value.astype(bf16)
        hi_ref[at, lanes] = hi
        lo_ref[at, lanes] = (value - hi.astype(f32)).astype(bf16)

    re_lanes, im_lanes = slice(0, half), slice(half, wide)

    def vector_part(f, c, i):
        at = pl.ds(c * block + i * CHUNK, CHUNK)
        left = pl.ds(2 * c * block + i * CHUNK, CHUNK)
        right = pl.ds((2 * c + 1) * block + i * CHUNK, CHUNK)
        e_re, e_im = e_s[at, :half], e_s[at, half:]
        a_re, a_im, b_re, b_im, m_re, m_im = load(f, at)
        p_re, p_im = p_s[f, at, :half], p_s[f, at, half:]
        t_re = e_re * m_re + e_im * m_im
        t_im = e_im * m_re - e_re * m_im
        put(glr_hi, glr_lo, left, re_lanes, t_re * b_re - t_im * b_im)
        put(glr_hi, glr_lo, left, im_lanes, t_re * b_im + t_im * b_re)
        put(glr_hi, glr_lo, right, re_lanes, t_re * a_re + t_im * a_im)
        put(glr_hi, glr_lo, right, im_lanes, t_re * a_im - t_im * a_re)
        put(gm_hi, gm_lo, at, re_lanes, e_re * p_re + e_im * p_im)
        put(gm_hi, gm_lo, at, im_lanes, e_im * p_re - e_re * p_im)

    def matmul_parts(f, c, sums, parts):
        both = pl.ds(2 * c * block, 2 * block)
        here = pl.ds(c * block, block)

        def station(x, ref):
            def run():
                term = mm(to_station[c], ref[both, x * half : (x + 1) * half])
                sums[x] = term if sums[x] is None else sums[x] + term

            return run

        def plane_sum(ref):
            def run():
                term = mm_nt(ref[here, :], spec[f, :planes, :])
                parts[c] = term if parts[c] is None else parts[c] + term

            return run

        return [
            station(0, glr_hi), station(1, glr_hi), station(0, glr_lo),
            station(1, glr_lo), plane_sum(gm_hi), plane_sum(gm_lo),
        ]

    def grads(f, grad_degrid):
        sums, parts, waiting = [None, None], [None] * block_count, []
        for c in range(block_count):
            for i in range(block // CHUNK):
                vector_part(f, c, i)
                if waiting:
                    waiting.pop(0)()
            for run in waiting:
                run()
            waiting = matmul_parts(f, c, sums, parts)
        for run in waiting:
            run()
        for k in range(group_count):
            for x in range(2):
                out_refs[k][f, x] = sums[x][k * group : (k + 1) * group, :channels]
        return grad_degrid + jnp.concatenate(parts, axis=0)

    grad_degrid = lax.fori_loop(0, facets, grads, jnp.zeros((rows, planes), f32))
    grad3 = jnp.concatenate(split(grad_degrid * term_scale, 3), axis=1)
    spread = as_bf16(
        mod(iota((3 * planes, LANES), 0), planes) == mod(iota((3 * planes, LANES), 1), planes)
    )
    heads = [h.astype(f32) for h in split(mm(grad3, spread), 2)]
    owner_rows = as_bf16(iota((n, rows), 0) == rows_ref[0:1, :].astype(i32))
    for i in range(line_count):
        here = slot_of == -i * per_line
        placed = jnp.concatenate(
            [jnp.where(here, h, 0.0).astype(bf16) for h in heads], axis=1
        )
        total = mm(owner_rows, placed)
        send_ref[pl.ds(i, n, stride=line_count), :] = total[:, :LANES] + total[:, LANES:]


def scatter_kernel(
    n, cap, base_ref, grad_ref, w_ref, out_ref, held_re, held_im, blocks, sem
):
    halves = (held_re, held_im)
    facets = held_re.shape[1]
    planes = 4 * facets
    fill = 64

    def clear(i, carry):
        for held in halves:
            held[pl.ds(i * fill, fill)] = jnp.zeros((fill, facets, LANES), f32)
        return carry

    lax.fori_loop(0, held_re.shape[0] // fill, clear, 0)
    per_line = LANES // planes
    per = cap // per_line
    pieces = []
    for i in range(per):
        line = grad_ref[pl.ds(i, n, stride=per), :]
        for q in range(per_line):
            pieces.append(line[:, q * planes : (q + 1) * planes])
    per_block = LANES // n
    block_count = cap // per_block
    for jb in range(block_count):
        mine = pieces[jb * per_block : (jb + 1) * per_block]
        joined = mine[0] if per_block == 1 else jnp.concatenate(mine, axis=0)
        blocks[jb] = joined.T
    lane3 = iota((2, facets, LANES), 2)
    copies = []
    for x, held in enumerate(halves):

        def block(jb, carry):
            values = jnp.stack(
                [blocks[jb, pl.ds((2 * t + x) * facets, facets), :] for t in range(2)]
            )

            def visit(inner, slots):
                starts, windows, adds = [], [], []
                for j, src, lane in slots:
                    starts.append(base_ref[j, src])
                    windows.append(held[pl.ds(starts[-1], 4)])
                for at, (j, src, lane) in enumerate(slots):
                    w = w_ref[pl.ds(j * n + src, 1), :]
                    low, high = w[:, :LANES], w[:, LANES:]
                    value = jnp.sum(
                        jnp.where(lane3 == lane, values, 0.0), axis=2, keepdims=True
                    )
                    window = windows[at] + jnp.concatenate(
                        [value * low, value * high], axis=0
                    )
                    for start, early_value, early_low, early_high in adds:
                        same = jnp.where(start == starts[at], 1.0, 0.0)
                        after = jnp.where(start + 2 == starts[at], 1.0, 0.0)
                        before = jnp.where(start == starts[at] + 2, 1.0, 0.0)
                        shared_low = early_low * same + early_high * after
                        shared_high = early_high * same + early_low * before
                        window = window + jnp.concatenate(
                            [early_value * shared_low, early_value * shared_high], axis=0
                        )
                    windows[at] = window
                    adds.append((starts[at], value, low, high))
                for start, window in zip(starts, windows):
                    held[pl.ds(start, 4)] = window
                return inner

            return each_slot(n, visit, carry, jb, PAIR)

        lax.fori_loop(0, block_count, block, 0)
        for f in range(facets):
            i = x * facets + f
            copy = pltpu.make_async_copy(held.at[:, f], out_ref.at[i], sem.at[i])
            copy.start()
            copies.append(copy)
    for copy in copies:
        copy.wait()


def body(
    visibilities,
    noise_weight,
    keep_flag,
    station_pairs,
    tile_owner,
    tile_offset,
    kernel_taps,
    gain_field,
    sky_grid,
):
    rows, _, channels = visibilities.shape
    taps = kernel_taps.shape[0]
    time_count = lax.axis_size("tm")
    group_count = lax.axis_size("bl")
    n = time_count * group_count
    cap = max(2, 2 * rows // n)
    _, facets, terms, cells = sky_grid.shape
    pairs = 2 * facets
    planes = pairs * terms
    tiles = cells // LANES
    group = gain_field.shape[1]
    stations = group * group_count
    both = ("tm", "bl")
    half = -(-channels // LANES) * LANES
    wide = 2 * half

    gain_turned = gain_field[0].transpose(1, 2, 0, 3)
    fields = taps + 2
    lines = 1 << (-(-fields * cap // LANES) - 1).bit_length()
    shift = jnp.full((1,), lax.axis_index("bl"), i32)
    send, row_table, col_table = pl.pallas_call(
        functools.partial(slots_kernel, n, cap, tiles, group, group_count),
        out_shape=(
            jax.ShapeDtypeStruct((n * lines, LANES), f32),
            jax.ShapeDtypeStruct((8, rows), f32),
            jax.ShapeDtypeStruct((rows, 8), f32),
        ),
        in_specs=[SMEM] + [VMEM] * 6,
        out_specs=(VMEM,) * 3,
        compiler_params=params(),
        cost_estimate=cost(10**9, 10**6),
        name="slots",
    )(
        shift,
        tile_owner.reshape(1, rows),
        tile_offset.reshape(1, rows),
        kernel_taps,
        station_pairs,
        noise_weight.reshape(1, rows),
        keep_flag.reshape(1, rows),
    )

    def exchange(x):
        x = x.reshape(n, -1, LANES)
        x = lax.all_to_all(x, both, split_axis=0, concat_axis=0, tiled=True)
        return x.reshape(-1, LANES)

    sky = (
        sky_grid.reshape(pairs, terms, tiles, LANES)
        .transpose(0, 2, 1, 3)
        .reshape(pairs, terms * tiles, LANES)
    )
    def turn_gains(x, k):
        return lax.ppermute(
            x, "bl", [(i, (i + k) % group_count) for i in range(group_count)]
        )

    near = range(1, group_count // 2 + 1)
    far = range(group_count // 2 + 1, group_count)
    send, gain_turned, gain_here = lax.optimization_barrier(
        (send, gain_turned, gain_field)
    )
    received = exchange(send)
    early = [turn_gains(gain_turned, k) for k in near]
    early.append(lax.ppermute(gain_here, "tm", [(i, i + 1) for i in range(time_count - 1)]))
    early.append(lax.ppermute(gain_here, "tm", [(i + 1, i) for i in range(time_count - 1)]))
    base = received.reshape(n, lines * LANES)[:, (taps + 1) * cap : (taps + 2) * cap]
    base = jnp.clip(base.T.astype(i32), 0, tiles - 2) * terms
    slot_lines = n * cap * planes // LANES
    block_count = n * cap // LANES
    values, weights = pl.pallas_call(
        functools.partial(degrid_kernel, n, cap, taps),
        out_shape=(
            jax.ShapeDtypeStruct((slot_lines, LANES), f32),
            jax.ShapeDtypeStruct((n * cap, 2 * LANES), f32),
        ),
        in_specs=[SMEM, VMEM, ANY],
        out_specs=(VMEM, ANY),
        scratch_shapes=[
            pltpu.VMEM((terms * tiles, facets, LANES), f32),
            pltpu.VMEM((terms * tiles, facets, LANES), f32),
            pltpu.VMEM((n * cap, 2 * LANES), f32),
            pltpu.VMEM((lines * LANES, n), f32),
            pltpu.VMEM((block_count, planes, LANES), f32),
            pltpu.SemaphoreType.DMA((pairs + 1,)),
        ],
        compiler_params=params(),
        cost_estimate=cost(10**8, 7 * 10**7),
        name="degrid",
    )(base, received, sky)
    values, gain_turned, *early = lax.optimization_barrier((values, gain_turned, *early))
    *early, below, above = early
    back = exchange(values)
    gathered = [gain_turned, *early, *(turn_gains(gain_turned, k) for k in far)]

    vis_wide = jnp.pad(visibilities, ((0, 0), (0, 0), (0, half - channels))).reshape(
        rows, wide
    )
    partial_shape = jax.ShapeDtypeStruct((facets, 2, group, channels), f32)
    outs = pl.pallas_call(
        functools.partial(rows_kernel, n, cap, group_count),
        out_shape=(partial_shape,) * group_count
        + (jax.ShapeDtypeStruct((slot_lines, LANES), f32),),
        in_specs=[VMEM] * (4 + group_count),
        out_specs=(VMEM,) * (group_count + 1),
        scratch_shapes=[
            pltpu.VMEM((facets, stations, wide), f32),
            pltpu.VMEM((facets, 3 * planes, wide), bf16),
            pltpu.VMEM((facets, rows, wide), f32),
            pltpu.VMEM((facets, rows, wide), f32),
            pltpu.VMEM((facets, rows, wide), f32),
            pltpu.VMEM((facets, rows, wide), f32),
            pltpu.VMEM((rows, wide), f32),
            pltpu.VMEM((2 * rows, wide), bf16),
            pltpu.VMEM((2 * rows, wide), bf16),
            pltpu.VMEM((rows, wide), bf16),
            pltpu.VMEM((rows, wide), bf16),
        ],
        compiler_params=params(),
        cost_estimate=cost(2 * 10**10, 10**7),
        name="rowgrads",
    )(row_table, col_table, vis_wide, back, *gathered)

    *parts, send_grad = outs
    got = exchange(send_grad)
    for k in range(1, group_count):
        parts[k] = lax.ppermute(
            parts[k], "bl", [(i, (i - k) % group_count) for i in range(group_count)]
        )
    grid = pl.pallas_call(
        functools.partial(scatter_kernel, n, cap),
        out_shape=jax.ShapeDtypeStruct((pairs, terms * tiles, LANES), f32),
        in_specs=[SMEM, VMEM, VMEM],
        out_specs=ANY,
        scratch_shapes=[
            pltpu.VMEM((terms * tiles, facets, LANES), f32),
            pltpu.VMEM((terms * tiles, facets, LANES), f32),
            pltpu.VMEM((block_count, planes, LANES), f32),
            pltpu.SemaphoreType.DMA((pairs,)),
        ],
        compiler_params=params(),
        cost_estimate=cost(10**8, 10**8),
        name="scatter",
    )(base, got, weights)
    grid, *parts = lax.optimization_barrier((grid, *parts))
    total = parts[0]
    for part in parts[1:]:
        total = total + part
    grid_gradient = (
        grid.reshape(pairs, tiles, terms, LANES)
        .transpose(0, 2, 1, 3)
        .reshape(sky_grid.shape)
    )
    when = lax.axis_index("tm")
    prior = jnp.where(when > 0, gain_field - below, 0.0)
    prior = prior - jnp.where(when < time_count - 1, above - gain_field, 0.0)
    gain_gradient = total.transpose(2, 0, 1, 3)[None] + smoothness * prior
    return (gain_gradient, grid_gradient)


def solution(mesh):
    return jax.shard_map(
        body,
        mesh=mesh,
        in_specs=(
            P(("tm", "bl"), None, None),
            P(("tm", "bl")),
            P(("tm", "bl")),
            P(None, ("tm", "bl")),
            P(("tm", "bl"), None),
            P(("tm", "bl")),
            P(None, ("tm", "bl")),
            P("tm", "bl", None, None, None),
            P(None, None, None, ("tm", "bl")),
        ),
        out_specs=(P("tm", "bl", None, None, None), P(None, None, None, ("tm", "bl"))),
        check_vma=False,
    )
```

```python
import functools

import jax
import jax.numpy as jnp
from jax import lax
from jax.experimental import pallas as pl
from jax.experimental.pallas import tpu as pltpu
from jax.sharding import PartitionSpec as P

smoothness = 4.0
LANES = 128
f32 = jnp.float32
bf16 = jnp.bfloat16
i32 = jnp.int32
VMEM = pl.BlockSpec(memory_space=pltpu.VMEM)
SMEM = pl.BlockSpec(memory_space=pltpu.SMEM)
ANY = pl.BlockSpec(memory_space=pl.ANY)
CHUNK = 16
PAIR = 2


def iota(shape, dim):
    return lax.broadcasted_iota(i32, shape, dim)


def as_bf16(mask):
    return jnp.where(mask, 1.0, 0.0).astype(bf16)


def split(x, pieces):
    out = []
    for _ in range(pieces - 1):
        head = x.astype(bf16)
        out.append(head)
        x = x - head.astype(f32)
    out.append(x.astype(bf16))
    return out


def mm(a, b):
    return jnp.dot(a, b, preferred_element_type=f32)


def mm_nt(a, b):
    return lax.dot_general(a, b, (((1,), (1,)), ((), ())), preferred_element_type=f32)


def div(x, k):
    return x >> (k.bit_length() - 1) if k & (k - 1) == 0 else x // k


def mod(x, k):
    return x & (k - 1) if k & (k - 1) == 0 else x - x // k * k


def params(mib=60):
    return pltpu.CompilerParams(vmem_limit_bytes=mib << 20)


def cost(flops, byte_count):
    return pl.CostEstimate(flops=flops, bytes_accessed=byte_count, transcendentals=0)


def read_wide(ref, count):
    per = ref.shape[0] // count
    return jnp.concatenate(
        [ref[pl.ds(i, count, stride=per), :] for i in range(per)], axis=1
    )


def write_wide(ref, value):
    count = value.shape[0]
    per = ref.shape[0] // count
    for i in range(per):
        ref[pl.ds(i, count, stride=per), :] = value[:, i * LANES : (i + 1) * LANES]


def slots_kernel(
    n, cap, tiles, group, group_count,
    shift_ref, owner_ref, offset_ref, taps_ref, pairs_ref, noise_ref, keep_ref,
    send_ref, rows_ref, cols_ref,
):
    rows = owner_ref.shape[1]
    taps = taps_ref.shape[0]
    width = send_ref.shape[0] // n * LANES
    owner = owner_ref[...]
    hit = iota((n, rows), 0) == owner
    onehot = as_bf16(hit)
    earlier = as_bf16(iota((rows, rows), 0) < iota((rows, rows), 1))
    before = mm(onehot, earlier)
    rank = jnp.sum(jnp.where(hit, before, 0.0), axis=0, keepdims=True)
    at_rank = iota((cap, rows), 0) == rank.astype(i32)
    offset = offset_ref[...]
    base = jnp.minimum(offset // LANES, tiles - 2)
    low = offset - base * LANES
    fields = [taps_ref[k : k + 1, :] for k in range(taps)]
    fields += [low.astype(f32), base.astype(f32)]
    parts = [jnp.where(at_rank, v, 0.0) for v in fields]
    spare = width - len(parts) * cap
    if spare:
        parts.append(jnp.zeros((spare, rows), f32))
    total = None
    for piece in split(jnp.concatenate(parts, axis=0), 3):
        term = mm_nt(onehot, piece)
        total = term if total is None else total + term
    write_wide(send_ref, total)
    station = pairs_ref[...]
    turn = shift_ref[0] - station // group + group_count
    turn = jnp.where(turn >= group_count, turn - group_count, turn)
    local = (turn * group + (station - station // group * group)).astype(f32)
    scale = noise_ref[...] * keep_ref[...].astype(f32)
    table = jnp.concatenate(
        [owner.astype(f32), rank, local, scale, jnp.zeros((3, rows), f32)], axis=0
    )
    rows_ref[...] = table
    cols_ref[...] = table.T


def turn_fields(n, cap, count, recv_ref, turn_s):
    per_block = LANES // n
    turn_s[...] = read_wide(recv_ref, n).T
    return [
        jnp.concatenate(
            [
                turn_s[pl.ds(k * cap + q, cap // per_block, stride=per_block), :]
                for q in range(per_block)
            ],
            axis=1,
        )
        for k in range(count)
    ]


def each_slot(n, visit, carry, jb, group):
    per_block = LANES // n
    unroll = min(n, 32)
    for q in range(per_block):
        j = jb * per_block + q

        def step(g, inner):
            first = g * unroll
            for u in range(0, unroll, group):
                slots = [(j, first + v, q * n + first + v) for v in range(u, u + group)]
                inner = visit(inner, slots)
            return inner

        if n == unroll:
            carry = step(0, carry)
        else:
            carry = lax.fori_loop(0, n // unroll, step, carry)
    return carry


def degrid_kernel(
    n, cap, taps,
    base_ref, recv_ref, sky_ref, out_ref, w_ref,
    held_re, held_im, w_s, turn_s, blocks, sem,
):
    halves = (held_re, held_im)
    facets = held_re.shape[1]
    planes = 4 * facets
    copies = []
    for x, held in enumerate(halves):
        mine = []
        for f in range(facets):
            i = x * facets + f
            copy = pltpu.make_async_copy(sky_ref.at[i], held.at[:, f], sem.at[i])
            copy.start()
            mine.append(copy)
        copies.append(mine)
    per_block = LANES // n
    block_count = cap // per_block
    fields = turn_fields(n, cap, taps + 1, recv_ref, turn_s)
    line = iota((2 * LANES, LANES), 0).astype(f32)
    for jb in range(block_count):
        place = line - fields[taps][jb : jb + 1, :]
        w = jnp.zeros((2 * LANES, LANES), f32)
        for k in range(taps):
            w = jnp.where(place == float(k), fields[k][jb : jb + 1, :], w)
        w_s[jb * LANES : (jb + 1) * LANES, :] = w.T
    save = pltpu.make_async_copy(w_s, w_ref, sem.at[2 * facets])
    save.start()
    lane3 = iota((2, facets, LANES), 2)
    for x, held in enumerate(halves):
        for copy in copies[x]:
            copy.wait()
        rows_of = []

        def visit(acc, slots):
            ((j, src, lane),) = slots
            w = rows_of[0][pl.ds(lane, 1), :]
            window = held[pl.ds(base_ref[j, src], 4)]
            prod = window[0:2] * w[:, :LANES] + window[2:4] * w[:, LANES:]
            return jnp.where(
                lane3 == lane, jnp.sum(prod, axis=2, keepdims=True), acc
            )

        def block(jb, carry):
            rows_of[:] = [w_s.at[pl.ds(pl.multiple_of(jb * LANES, LANES), LANES), :]]
            acc = each_slot(n, visit, jnp.zeros((2, facets, LANES), f32), jb, 1)
            for t in range(2):
                blocks[jb, pl.ds((2 * t + x) * facets, facets), :] = acc[t]
            return carry

        lax.fori_loop(0, block_count, block, 0)
    turned = [blocks[jb].T for jb in range(block_count)]
    pieces = []
    for j in range(cap):
        jb, lo = j * n // LANES, j * n % LANES
        pieces.append(turned[jb][lo : lo + n, :planes])
    per_line = LANES // planes
    per = cap // per_line
    for i in range(per):
        wide_line = jnp.concatenate(pieces[i * per_line : (i + 1) * per_line], axis=1)
        out_ref[pl.ds(i, n, stride=per), :] = wide_line
    save.wait()


def rows_kernel(
    n, cap, group_count,
    rows_ref, cols_ref, vis_ref, back_ref, *rest,
):
    gain_refs = rest[:group_count]
    out_refs = rest[group_count : 2 * group_count]
    send_ref = rest[2 * group_count]
    gains, spec, a_s, b_s, m_s, p_s, e_s, glr_hi, glr_lo, gm_hi, gm_lo = rest[
        2 * group_count + 1 :
    ]
    facets, _, group, channels = gain_refs[0].shape
    rows = cols_ref.shape[0]
    stations = group * group_count
    planes = 4 * facets
    pairs = 2 * facets
    half = m_s.shape[2] // 2
    wide = 2 * half
    cols = cols_ref[...]
    owner_col, rank_col = cols[:, 0:1].astype(i32), cols[:, 1:2].astype(i32)
    first_col, second_col = cols[:, 2:3].astype(i32), cols[:, 3:4].astype(i32)

    gains[...] = jnp.zeros(gains.shape, f32)
    for k in range(group_count):
        for f in range(facets):
            for x in range(2):
                gains[f, k * group : (k + 1) * group, x * half : x * half + channels] = (
                    gain_refs[k][f, x]
                )

    owner3 = as_bf16(mod(iota((1, 3 * n), 1), n) == owner_col)
    per_line = LANES // planes
    line_count = cap // per_line
    slot_of = div(iota((1, LANES), 1), planes) - rank_col
    degrid = jnp.zeros((rows, LANES), f32)
    for i in range(line_count):
        line = jnp.concatenate(split(back_ref[pl.ds(i, n, stride=line_count), :], 3), axis=0)
        degrid = degrid + jnp.where(slot_of == -i * per_line, mm(owner3, line), 0.0)
    fold = as_bf16(mod(iota((3 * LANES, planes), 0), planes) == iota((3 * LANES, planes), 1))
    degrid = mm(jnp.concatenate(split(degrid, 3), axis=1), fold)
    term_scale = jnp.where(iota((1, planes), 1) >= pairs, 1.0 / (channels - 1), 1.0)
    d3 = jnp.concatenate(split(degrid * term_scale, 3), axis=1)

    lane_st = mod(iota((1, 3 * stations), 1), stations)
    first3 = as_bf16(lane_st == first_col)
    second3 = as_bf16(lane_st == second_col)
    plane = mod(iota((3 * planes, wide), 0), planes)
    lane_w = iota((3 * planes, wide), 1)
    chan = jnp.where(lane_w >= half, lane_w - half, lane_w)
    side = jnp.where(lane_w >= half, 1, 0)
    value = jnp.where(plane >= pairs, 2 * chan - (channels - 1), 1).astype(f32)
    live = (chan < channels) & (div(mod(plane, pairs), facets) == side)
    value = jnp.where(live, value, 0.0)
    facet_of = mod(plane, facets)
    chunks = [pl.ds(i * CHUNK, CHUNK) for i in range(rows // CHUNK)]

    def gather(f):
        table = jnp.concatenate(split(gains[f], 3), axis=0)
        spec[f] = jnp.where(facet_of == f, value, 0.0).astype(bf16)
        a_s[f] = mm(first3, table)
        b_s[f] = mm(second3, table)
        m_s[f] = mm(d3, spec[f])

    def load(f, at):
        return (
            a_s[f, at, :half], a_s[f, at, half:],
            b_s[f, at, :half], b_s[f, at, half:],
            m_s[f, at, :half], m_s[f, at, half:],
        )

    def predict(f):
        for at in chunks:
            a_re, a_im, b_re, b_im, m_re, m_im = load(f, at)
            p_re = a_re * b_re + a_im * b_im
            p_im = a_im * b_re - a_re * b_im
            p_s[f, at, :half] = p_re
            p_s[f, at, half:] = p_im
            e_s[at, :half] += p_re * m_re - p_im * m_im
            e_s[at, half:] += p_re * m_im + p_im * m_re

    e_s[...] = -vis_ref[...].astype(f32)
    gather(0)

    for f in range(facets):
        if f + 1 < facets:
            gather(f + 1)
        predict(f)
    e_s[...] = e_s[...] * cols[:, 4:5]

    block = min(rows, 128)
    block_count = rows // block
    station_row = iota((stations, rows), 0)
    to_first = as_bf16(station_row == rows_ref[2:3, :].astype(i32))
    to_second = as_bf16(station_row == rows_ref[3:4, :].astype(i32))
    to_station = []
    for c in range(block_count):
        part = slice(c * block, (c + 1) * block)
        to_station.append(jnp.concatenate([to_first[:, part], to_second[:, part]], axis=1))

    def put(hi_ref, lo_ref, at, lanes, value):
        hi = value.astype(bf16)
        hi_ref[at, lanes] = hi
        lo_ref[at, lanes] = (value - hi.astype(f32)).astype(bf16)

    re_lanes, im_lanes = slice(0, half), slice(half, wide)

    def vector_part(f, c, i):
        at = pl.ds(c * block + i * CHUNK, CHUNK)
        left = pl.ds(2 * c * block + i * CHUNK, CHUNK)
        right = pl.ds((2 * c + 1) * block + i * CHUNK, CHUNK)
        e_re, e_im = e_s[at, :half], e_s[at, half:]
        a_re, a_im, b_re, b_im, m_re, m_im = load(f, at)
        p_re, p_im = p_s[f, at, :half], p_s[f, at, half:]
        t_re = e_re * m_re + e_im * m_im
        t_im = e_im * m_re - e_re * m_im
        put(glr_hi, glr_lo, left, re_lanes, t_re * b_re - t_im * b_im)
        put(glr_hi, glr_lo, left, im_lanes, t_re * b_im + t_im * b_re)
        put(glr_hi, glr_lo, right, re_lanes, t_re * a_re + t_im * a_im)
        put(glr_hi, glr_lo, right, im_lanes, t_re * a_im - t_im * a_re)
        put(gm_hi, gm_lo, at, re_lanes, e_re * p_re + e_im * p_im)
        put(gm_hi, gm_lo, at, im_lanes, e_im * p_re - e_re * p_im)

    def matmul_parts(f, c, sums, parts):
        both = pl.ds(2 * c * block, 2 * block)
        here = pl.ds(c * block, block)

        def station(x, ref):
            def run():
                term = mm(to_station[c], ref[both, x * half : (x + 1) * half])
                sums[x] = term if sums[x] is None else sums[x] + term

            return run

        def plane_sum(ref):
            def run():
                term = mm_nt(ref[here, :], spec[f, :planes, :])
                parts[c] = term if parts[c] is None else parts[c] + term

            return run

        return [
            station(0, glr_hi), station(1, glr_hi), station(0, glr_lo),
            station(1, glr_lo), plane_sum(gm_hi), plane_sum(gm_lo),
        ]

    def grads(f, grad_degrid):
        sums, parts, waiting = [None, None], [None] * block_count, []
        for c in range(block_count):
            for i in range(block // CHUNK):
                vector_part(f, c, i)
                if waiting:
                    waiting.pop(0)()
            for run in waiting:
                run()
            waiting = matmul_parts(f, c, sums, parts)
        for run in waiting:
            run()
        for k in range(group_count):
            for x in range(2):
                out_refs[k][f, x] = sums[x][k * group : (k + 1) * group, :channels]
        return grad_degrid + jnp.concatenate(parts, axis=0)

    grad_degrid = lax.fori_loop(0, facets, grads, jnp.zeros((rows, planes), f32))
    grad3 = jnp.concatenate(split(grad_degrid * term_scale, 3), axis=1)
    spread = as_bf16(
        mod(iota((3 * planes, LANES), 0), planes) == mod(iota((3 * planes, LANES), 1), planes)
    )
    heads = [h.astype(f32) for h in split(mm(grad3, spread), 2)]
    owner_rows = as_bf16(iota((n, rows), 0) == rows_ref[0:1, :].astype(i32))
    for i in range(line_count):
        here = slot_of == -i * per_line
        placed = jnp.concatenate(
            [jnp.where(here, h, 0.0).astype(bf16) for h in heads], axis=1
        )
        total = mm(owner_rows, placed)
        send_ref[pl.ds(i, n, stride=line_count), :] = total[:, :LANES] + total[:, LANES:]


def scatter_kernel(
    n, cap, base_ref, grad_ref, w_ref, out_ref, held_re, held_im, blocks, sem
):
    halves = (held_re, held_im)
    facets = held_re.shape[1]
    planes = 4 * facets
    fill = 64

    def clear(i, carry):
        for held in halves:
            held[pl.ds(i * fill, fill)] = jnp.zeros((fill, facets, LANES), f32)
        return carry

    lax.fori_loop(0, held_re.shape[0] // fill, clear, 0)
    per_line = LANES // planes
    per = cap // per_line
    pieces = []
    for i in range(per):
        line = grad_ref[pl.ds(i, n, stride=per), :]
        for q in range(per_line):
            pieces.append(line[:, q * planes : (q + 1) * planes])
    per_block = LANES // n
    block_count = cap // per_block
    for jb in range(block_count):
        mine = pieces[jb * per_block : (jb + 1) * per_block]
        joined = mine[0] if per_block == 1 else jnp.concatenate(mine, axis=0)
        blocks[jb] = joined.T
    lane3 = iota((2, facets, LANES), 2)
    copies = []
    for x, held in enumerate(halves):

        def block(jb, carry):
            w_rows = w_ref.at[pl.ds(pl.multiple_of(jb * LANES, LANES), LANES), :]
            values = jnp.stack(
                [blocks[jb, pl.ds((2 * t + x) * facets, facets), :] for t in range(2)]
            )

            def visit(inner, slots):
                starts, windows, adds = [], [], []
                for j, src, lane in slots:
                    starts.append(base_ref[j, src])
                    windows.append(held[pl.ds(starts[-1], 4)])
                for at, (j, src, lane) in enumerate(slots):
                    w = w_rows[pl.ds(lane, 1), :]
                    low, high = w[:, :LANES], w[:, LANES:]
                    value = jnp.sum(
                        jnp.where(lane3 == lane, values, 0.0), axis=2, keepdims=True
                    )
                    window = windows[at] + jnp.concatenate(
                        [value * low, value * high], axis=0
                    )
                    for start, early_value, early_low, early_high in adds:
                        same = jnp.where(start == starts[at], 1.0, 0.0)
                        after = jnp.where(start + 2 == starts[at], 1.0, 0.0)
                        before = jnp.where(start == starts[at] + 2, 1.0, 0.0)
                        shared_low = early_low * same + early_high * after
                        shared_high = early_high * same + early_low * before
                        window = window + jnp.concatenate(
                            [early_value * shared_low, early_value * shared_high], axis=0
                        )
                    windows[at] = window
                    adds.append((starts[at], value, low, high))
                for start, window in zip(starts, windows):
                    held[pl.ds(start, 4)] = window
                return inner

            return each_slot(n, visit, carry, jb, PAIR)

        lax.fori_loop(0, block_count, block, 0)
        for f in range(facets):
            i = x * facets + f
            copy = pltpu.make_async_copy(held.at[:, f], out_ref.at[i], sem.at[i])
            copy.start()
            copies.append(copy)
    for copy in copies:
        copy.wait()


def body(
    visibilities,
    noise_weight,
    keep_flag,
    station_pairs,
    tile_owner,
    tile_offset,
    kernel_taps,
    gain_field,
    sky_grid,
):
    rows, _, channels = visibilities.shape
    taps = kernel_taps.shape[0]
    time_count = lax.axis_size("tm")
    group_count = lax.axis_size("bl")
    n = time_count * group_count
    cap = max(2, 2 * rows // n)
    _, facets, terms, cells = sky_grid.shape
    pairs = 2 * facets
    planes = pairs * terms
    tiles = cells // LANES
    group = gain_field.shape[1]
    stations = group * group_count
    both = ("tm", "bl")
    half = -(-channels // LANES) * LANES
    wide = 2 * half

    gain_turned = gain_field[0].transpose(1, 2, 0, 3)
    fields = taps + 2
    lines = 1 << (-(-fields * cap // LANES) - 1).bit_length()
    shift = jnp.full((1,), lax.axis_index("bl"), i32)
    send, row_table, col_table = pl.pallas_call(
        functools.partial(slots_kernel, n, cap, tiles, group, group_count),
        out_shape=(
            jax.ShapeDtypeStruct((n * lines, LANES), f32),
            jax.ShapeDtypeStruct((8, rows), f32),
            jax.ShapeDtypeStruct((rows, 8), f32),
        ),
        in_specs=[SMEM] + [VMEM] * 6,
        out_specs=(VMEM,) * 3,
        compiler_params=params(),
        cost_estimate=cost(10**9, 10**6),
        name="slots",
    )(
        shift,
        tile_owner.reshape(1, rows),
        tile_offset.reshape(1, rows),
        kernel_taps,
        station_pairs,
        noise_weight.reshape(1, rows),
        keep_flag.reshape(1, rows),
    )

    def exchange(x):
        x = x.reshape(n, -1, LANES)
        x = lax.all_to_all(x, both, split_axis=0, concat_axis=0, tiled=True)
        return x.reshape(-1, LANES)

    sky = (
        sky_grid.reshape(pairs, terms, tiles, LANES)
        .transpose(0, 2, 1, 3)
        .reshape(pairs, terms * tiles, LANES)
    )
    def turn_gains(x, k):
        return lax.ppermute(
            x, "bl", [(i, (i + k) % group_count) for i in range(group_count)]
        )

    send, gain_first = lax.optimization_barrier((send, gain_turned))
    received = exchange(send)
    gathered = [turn_gains(gain_first, k) for k in range(1, group_count)]
    base = received.reshape(n, lines * LANES)[:, (taps + 1) * cap : (taps + 2) * cap]
    base = jnp.clip(base.T.astype(i32), 0, tiles - 2) * terms
    slot_lines = n * cap * planes // LANES
    block_count = n * cap // LANES
    values, weights = pl.pallas_call(
        functools.partial(degrid_kernel, n, cap, taps),
        out_shape=(
            jax.ShapeDtypeStruct((slot_lines, LANES), f32),
            jax.ShapeDtypeStruct((n * cap, 2 * LANES), f32),
        ),
        in_specs=[SMEM, VMEM, ANY],
        out_specs=(VMEM, ANY),
        scratch_shapes=[
            pltpu.VMEM((terms * tiles, facets, LANES), f32),
            pltpu.VMEM((terms * tiles, facets, LANES), f32),
            pltpu.VMEM((n * cap, 2 * LANES), f32),
            pltpu.VMEM((lines * LANES, n), f32),
            pltpu.VMEM((block_count, planes, LANES), f32),
            pltpu.SemaphoreType.DMA((pairs + 1,)),
        ],
        compiler_params=params(),
        cost_estimate=cost(10**8, 7 * 10**7),
        name="degrid",
    )(base, received, sky)
    values, gain_here = lax.optimization_barrier((values, gain_turned))
    back = exchange(values)
    below = lax.ppermute(gain_here, "tm", [(i, i + 1) for i in range(time_count - 1)])
    above = lax.ppermute(gain_here, "tm", [(i + 1, i) for i in range(time_count - 1)])
    visibilities, *gathered = lax.optimization_barrier((visibilities, *gathered))

    vis_wide = jnp.pad(visibilities, ((0, 0), (0, 0), (0, half - channels))).reshape(
        rows, wide
    )
    partial_shape = jax.ShapeDtypeStruct((facets, 2, group, channels), f32)
    outs = pl.pallas_call(
        functools.partial(rows_kernel, n, cap, group_count),
        out_shape=(partial_shape,) * group_count
        + (jax.ShapeDtypeStruct((slot_lines, LANES), f32),),
        in_specs=[VMEM] * (4 + group_count),
        out_specs=(VMEM,) * (group_count + 1),
        scratch_shapes=[
            pltpu.VMEM((facets, stations, wide), f32),
            pltpu.VMEM((facets, 3 * planes, wide), bf16),
            pltpu.VMEM((facets, rows, wide), f32),
            pltpu.VMEM((facets, rows, wide), f32),
            pltpu.VMEM((facets, rows, wide), f32),
            pltpu.VMEM((facets, rows, wide), f32),
            pltpu.VMEM((rows, wide), f32),
            pltpu.VMEM((2 * rows, wide), bf16),
            pltpu.VMEM((2 * rows, wide), bf16),
            pltpu.VMEM((rows, wide), bf16),
            pltpu.VMEM((rows, wide), bf16),
        ],
        compiler_params=params(52),
        cost_estimate=cost(2 * 10**10, 10**7),
        name="rowgrads",
    )(row_table, col_table, vis_wide, back, gain_turned, *gathered)

    own, *parts, send_grad = outs
    when = lax.axis_index("tm")
    prior = jnp.where(when > 0, gain_turned - below, 0.0)
    prior = prior - jnp.where(when < time_count - 1, above - gain_turned, 0.0)
    own = own + smoothness * prior
    got, own = lax.optimization_barrier((exchange(send_grad), own))
    parts = [turn_gains(part, -k) for k, part in enumerate(parts, 1)]
    grid = pl.pallas_call(
        functools.partial(scatter_kernel, n, cap),
        out_shape=jax.ShapeDtypeStruct((pairs, terms * tiles, LANES), f32),
        in_specs=[SMEM, VMEM, VMEM],
        out_specs=ANY,
        scratch_shapes=[
            pltpu.VMEM((terms * tiles, facets, LANES), f32),
            pltpu.VMEM((terms * tiles, facets, LANES), f32),
            pltpu.VMEM((block_count, planes, LANES), f32),
            pltpu.SemaphoreType.DMA((pairs,)),
        ],
        compiler_params=params(40),
        cost_estimate=cost(0, 10**5),
        name="scatter",
    )(base, got, weights)
    grid, *parts = lax.optimization_barrier((grid, *parts))
    for part in parts:
        own = own + part
    grid_gradient = (
        grid.reshape(pairs, tiles, terms, LANES)
        .transpose(0, 2, 1, 3)
        .reshape(sky_grid.shape)
    )
    gain_gradient = own.transpose(2, 0, 1, 3)[None]
    return (gain_gradient, grid_gradient)


def solution(mesh):
    return jax.shard_map(
        body,
        mesh=mesh,
        in_specs=(
            P(("tm", "bl"), None, None),
            P(("tm", "bl")),
            P(("tm", "bl")),
            P(None, ("tm", "bl")),
            P(("tm", "bl"), None),
            P(("tm", "bl")),
            P(None, ("tm", "bl")),
            P("tm", "bl", None, None, None),
            P(None, None, None, ("tm", "bl")),
        ),
        out_specs=(P("tm", "bl", None, None, None), P(None, None, None, ("tm", "bl"))),
        check_vma=False,
    )
```

```python
import functools

import jax
import jax.numpy as jnp
from jax import lax
from jax.experimental import pallas as pl
from jax.experimental.pallas import tpu as pltpu
from jax.sharding import PartitionSpec as P

smoothness = 4.0
LANES = 128
f32 = jnp.float32
bf16 = jnp.bfloat16
i32 = jnp.int32
VMEM = pl.BlockSpec(memory_space=pltpu.VMEM)
SMEM = pl.BlockSpec(memory_space=pltpu.SMEM)
ANY = pl.BlockSpec(memory_space=pl.ANY)
CHUNK = 16
PAIR = 2


def iota(shape, dim):
    return lax.broadcasted_iota(i32, shape, dim)


def as_bf16(mask):
    return jnp.where(mask, 1.0, 0.0).astype(bf16)


def split(x, pieces):
    out = []
    for _ in range(pieces - 1):
        head = x.astype(bf16)
        out.append(head)
        x = x - head.astype(f32)
    out.append(x.astype(bf16))
    return out


def mm(a, b):
    return jnp.dot(a, b, preferred_element_type=f32)


def mm_nt(a, b):
    return lax.dot_general(a, b, (((1,), (1,)), ((), ())), preferred_element_type=f32)


def div(x, k):
    return x >> (k.bit_length() - 1) if k & (k - 1) == 0 else x // k


def mod(x, k):
    return x & (k - 1) if k & (k - 1) == 0 else x - x // k * k


def params(mib=60):
    return pltpu.CompilerParams(vmem_limit_bytes=mib << 20)


def cost(flops, byte_count):
    return pl.CostEstimate(flops=flops, bytes_accessed=byte_count, transcendentals=0)


def read_wide(ref, count):
    per = ref.shape[0] // count
    return jnp.concatenate(
        [ref[pl.ds(i, count, stride=per), :] for i in range(per)], axis=1
    )


def write_wide(ref, value):
    count = value.shape[0]
    per = ref.shape[0] // count
    for i in range(per):
        ref[pl.ds(i, count, stride=per), :] = value[:, i * LANES : (i + 1) * LANES]


def slots_kernel(
    n, cap, tiles, group, group_count,
    shift_ref, owner_ref, offset_ref, taps_ref, pairs_ref, noise_ref, keep_ref,
    send_ref, rows_ref, cols_ref,
):
    rows = owner_ref.shape[1]
    taps = taps_ref.shape[0]
    width = send_ref.shape[0] // n * LANES
    owner = owner_ref[...]
    hit = iota((n, rows), 0) == owner
    onehot = as_bf16(hit)
    earlier = as_bf16(iota((rows, rows), 0) < iota((rows, rows), 1))
    before = mm(onehot, earlier)
    rank = jnp.sum(jnp.where(hit, before, 0.0), axis=0, keepdims=True)
    at_rank = iota((cap, rows), 0) == rank.astype(i32)
    offset = offset_ref[...]
    base = jnp.minimum(offset // LANES, tiles - 2)
    low = offset - base * LANES
    fields = [taps_ref[k : k + 1, :] for k in range(taps)]
    fields += [low.astype(f32), base.astype(f32)]
    parts = [jnp.where(at_rank, v, 0.0) for v in fields]
    spare = width - len(parts) * cap
    if spare:
        parts.append(jnp.zeros((spare, rows), f32))
    total = None
    for piece in split(jnp.concatenate(parts, axis=0), 3):
        term = mm_nt(onehot, piece)
        total = term if total is None else total + term
    write_wide(send_ref, total)
    station = pairs_ref[...]
    turn = shift_ref[0] - station // group + group_count
    turn = jnp.where(turn >= group_count, turn - group_count, turn)
    local = (turn * group + (station - station // group * group)).astype(f32)
    scale = noise_ref[...] * keep_ref[...].astype(f32)
    table = jnp.concatenate(
        [owner.astype(f32), rank, local, scale, jnp.zeros((3, rows), f32)], axis=0
    )
    rows_ref[...] = table
    cols_ref[...] = table.T


def turn_fields(n, cap, count, recv_ref, turn_s):
    per_block = LANES // n
    turn_s[...] = read_wide(recv_ref, n).T
    return [
        jnp.concatenate(
            [
                turn_s[pl.ds(k * cap + q, cap // per_block, stride=per_block), :]
                for q in range(per_block)
            ],
            axis=1,
        )
        for k in range(count)
    ]


def each_slot(n, visit, carry, jb, group):
    per_block = LANES // n
    unroll = min(n, 32)
    for q in range(per_block):
        j = jb * per_block + q

        def step(g, inner):
            first = g * unroll
            for u in range(0, unroll, group):
                slots = [(j, first + v, q * n + first + v) for v in range(u, u + group)]
                inner = visit(inner, slots)
            return inner

        if n == unroll:
            carry = step(0, carry)
        else:
            carry = lax.fori_loop(0, n // unroll, step, carry)
    return carry


def degrid_kernel(
    n, cap, taps,
    base_ref, recv_ref, sky_ref, out_ref, w_ref,
    held_re, held_im, w_s, turn_s, blocks, sem,
):
    halves = (held_re, held_im)
    facets = held_re.shape[1]
    planes = 4 * facets
    copies = []
    for x, held in enumerate(halves):
        mine = []
        for f in range(facets):
            i = x * facets + f
            copy = pltpu.make_async_copy(sky_ref.at[i], held.at[:, f], sem.at[i])
            copy.start()
            mine.append(copy)
        copies.append(mine)
    per_block = LANES // n
    block_count = cap // per_block
    fields = turn_fields(n, cap, taps + 1, recv_ref, turn_s)
    line = iota((2 * LANES, LANES), 0).astype(f32)
    for jb in range(block_count):
        place = line - fields[taps][jb : jb + 1, :]
        w = jnp.zeros((2 * LANES, LANES), f32)
        for k in range(taps):
            w = jnp.where(place == float(k), fields[k][jb : jb + 1, :], w)
        w_s[jb * LANES : (jb + 1) * LANES, :] = w.T
    save = pltpu.make_async_copy(w_s, w_ref, sem.at[2 * facets])
    save.start()
    lane3 = iota((2, facets, LANES), 2)
    for x, held in enumerate(halves):
        for copy in copies[x]:
            copy.wait()
        rows_of = []

        def visit(acc, slots):
            ((j, src, lane),) = slots
            w = rows_of[0][pl.ds(lane, 1), :]
            window = held[pl.ds(base_ref[j, src], 4)]
            prod = window[0:2] * w[:, :LANES] + window[2:4] * w[:, LANES:]
            return jnp.where(
                lane3 == lane, jnp.sum(prod, axis=2, keepdims=True), acc
            )

        def block(jb, carry):
            rows_of[:] = [w_s.at[pl.ds(pl.multiple_of(jb * LANES, LANES), LANES), :]]
            acc = each_slot(n, visit, jnp.zeros((2, facets, LANES), f32), jb, 1)
            for t in range(2):
                blocks[jb, pl.ds((2 * t + x) * facets, facets), :] = acc[t]
            return carry

        lax.fori_loop(0, block_count, block, 0)
    turned = [blocks[jb].T for jb in range(block_count)]
    pieces = []
    for j in range(cap):
        jb, lo = j * n // LANES, j * n % LANES
        pieces.append(turned[jb][lo : lo + n, :planes])
    per_line = LANES // planes
    per = cap // per_line
    for i in range(per):
        wide_line = jnp.concatenate(pieces[i * per_line : (i + 1) * per_line], axis=1)
        out_ref[pl.ds(i, n, stride=per), :] = wide_line
    save.wait()


def rows_kernel(
    n, cap, group_count,
    rows_ref, cols_ref, vis_ref, back_ref, *rest,
):
    far = group_count - group_count // 2 - 1
    gain_refs, rest = rest[: group_count + far], rest[group_count + far :]
    out_refs, send_ref, rest = rest[:group_count], rest[group_count], rest[group_count + 1 :]
    gains, spec, a_s, b_s, m_s, p_s, e_s, glr_hi, glr_lo, gm_hi, gm_lo = rest
    facets, _, group, channels = gain_refs[0].shape
    rows = cols_ref.shape[0]
    stations = group * group_count
    planes = 4 * facets
    pairs = 2 * facets
    half = m_s.shape[2] // 2
    wide = 2 * half
    cols = cols_ref[...]
    owner_col, rank_col = cols[:, 0:1].astype(i32), cols[:, 1:2].astype(i32)
    first_col, second_col = cols[:, 2:3].astype(i32), cols[:, 3:4].astype(i32)

    gains[...] = jnp.zeros(gains.shape, f32)
    for k in range(group_count):
        mine = slice(k * group, (k + 1) * group)
        for f in range(facets):
            ref, at = gain_refs[k], f
            if f >= ref.shape[0]:
                ref, at = gain_refs[k + far], f - ref.shape[0]
            for x in range(2):
                gains[f, mine, x * half : x * half + channels] = ref[at, x]

    owner3 = as_bf16(mod(iota((1, 3 * n), 1), n) == owner_col)
    per_line = LANES // planes
    line_count = cap // per_line
    slot_of = div(iota((1, LANES), 1), planes) - rank_col
    degrid = jnp.zeros((rows, LANES), f32)
    for i in range(line_count):
        line = jnp.concatenate(split(back_ref[pl.ds(i, n, stride=line_count), :], 3), axis=0)
        degrid = degrid + jnp.where(slot_of == -i * per_line, mm(owner3, line), 0.0)
    fold = as_bf16(mod(iota((3 * LANES, planes), 0), planes) == iota((3 * LANES, planes), 1))
    degrid = mm(jnp.concatenate(split(degrid, 3), axis=1), fold)
    term_scale = jnp.where(iota((1, planes), 1) >= pairs, 1.0 / (channels - 1), 1.0)
    d3 = jnp.concatenate(split(degrid * term_scale, 3), axis=1)

    lane_st = mod(iota((1, 3 * stations), 1), stations)
    first3 = as_bf16(lane_st == first_col)
    second3 = as_bf16(lane_st == second_col)
    plane = mod(iota((3 * planes, wide), 0), planes)
    lane_w = iota((3 * planes, wide), 1)
    chan = jnp.where(lane_w >= half, lane_w - half, lane_w)
    side = jnp.where(lane_w >= half, 1, 0)
    value = jnp.where(plane >= pairs, 2 * chan - (channels - 1), 1).astype(f32)
    live = (chan < channels) & (div(mod(plane, pairs), facets) == side)
    value = jnp.where(live, value, 0.0)
    facet_of = mod(plane, facets)
    chunks = [pl.ds(i * CHUNK, CHUNK) for i in range(rows // CHUNK)]

    def gather(f):
        table = jnp.concatenate(split(gains[f], 3), axis=0)
        spec[f] = jnp.where(facet_of == f, value, 0.0).astype(bf16)
        a_s[f] = mm(first3, table)
        b_s[f] = mm(second3, table)
        m_s[f] = mm(d3, spec[f])

    def load(f, at):
        return (
            a_s[f, at, :half], a_s[f, at, half:],
            b_s[f, at, :half], b_s[f, at, half:],
            m_s[f, at, :half], m_s[f, at, half:],
        )

    def predict(f):
        for at in chunks:
            a_re, a_im, b_re, b_im, m_re, m_im = load(f, at)
            p_re = a_re * b_re + a_im * b_im
            p_im = a_im * b_re - a_re * b_im
            p_s[f, at, :half] = p_re
            p_s[f, at, half:] = p_im
            e_s[at, :half] += p_re * m_re - p_im * m_im
            e_s[at, half:] += p_re * m_im + p_im * m_re

    e_s[...] = -vis_ref[...].astype(f32)
    gather(0)

    for f in range(facets):
        if f + 1 < facets:
            gather(f + 1)
        predict(f)
    e_s[...] = e_s[...] * cols[:, 4:5]

    block = min(rows, 128)
    block_count = rows // block
    station_row = iota((stations, rows), 0)
    to_first = as_bf16(station_row == rows_ref[2:3, :].astype(i32))
    to_second = as_bf16(station_row == rows_ref[3:4, :].astype(i32))
    to_station = []
    for c in range(block_count):
        part = slice(c * block, (c + 1) * block)
        to_station.append(jnp.concatenate([to_first[:, part], to_second[:, part]], axis=1))

    def put(hi_ref, lo_ref, at, lanes, value):
        hi = value.astype(bf16)
        hi_ref[at, lanes] = hi
        lo_ref[at, lanes] = (value - hi.astype(f32)).astype(bf16)

    re_lanes, im_lanes = slice(0, half), slice(half, wide)

    def vector_part(f, c, i):
        at = pl.ds(c * block + i * CHUNK, CHUNK)
        left = pl.ds(2 * c * block + i * CHUNK, CHUNK)
        right = pl.ds((2 * c + 1) * block + i * CHUNK, CHUNK)
        e_re, e_im = e_s[at, :half], e_s[at, half:]
        a_re, a_im, b_re, b_im, m_re, m_im = load(f, at)
        p_re, p_im = p_s[f, at, :half], p_s[f, at, half:]
        t_re = e_re * m_re + e_im * m_im
        t_im = e_im * m_re - e_re * m_im
        put(glr_hi, glr_lo, left, re_lanes, t_re * b_re - t_im * b_im)
        put(glr_hi, glr_lo, left, im_lanes, t_re * b_im + t_im * b_re)
        put(glr_hi, glr_lo, right, re_lanes, t_re * a_re + t_im * a_im)
        put(glr_hi, glr_lo, right, im_lanes, t_re * a_im - t_im * a_re)
        put(gm_hi, gm_lo, at, re_lanes, e_re * p_re + e_im * p_im)
        put(gm_hi, gm_lo, at, im_lanes, e_im * p_re - e_re * p_im)

    def matmul_parts(f, c, sums, parts):
        both = pl.ds(2 * c * block, 2 * block)
        here = pl.ds(c * block, block)

        def station(x, ref):
            def run():
                term = mm(to_station[c], ref[both, x * half : (x + 1) * half])
                sums[x] = term if sums[x] is None else sums[x] + term

            return run

        def plane_sum(ref):
            def run():
                term = mm_nt(ref[here, :], spec[f, :planes, :])
                parts[c] = term if parts[c] is None else parts[c] + term

            return run

        return [
            station(0, glr_hi), station(1, glr_hi), station(0, glr_lo),
            station(1, glr_lo), plane_sum(gm_hi), plane_sum(gm_lo),
        ]

    def grads(f, grad_degrid):
        sums, parts, waiting = [None, None], [None] * block_count, []
        for c in range(block_count):
            for i in range(block // CHUNK):
                vector_part(f, c, i)
                if waiting:
                    waiting.pop(0)()
            for run in waiting:
                run()
            waiting = matmul_parts(f, c, sums, parts)
        for run in waiting:
            run()
        for k in range(group_count):
            for x in range(2):
                out_refs[k][f, x] = sums[x][k * group : (k + 1) * group, :channels]
        return grad_degrid + jnp.concatenate(parts, axis=0)

    grad_degrid = lax.fori_loop(0, facets, grads, jnp.zeros((rows, planes), f32))
    grad3 = jnp.concatenate(split(grad_degrid * term_scale, 3), axis=1)
    spread = as_bf16(
        mod(iota((3 * planes, LANES), 0), planes) == mod(iota((3 * planes, LANES), 1), planes)
    )
    heads = [h.astype(f32) for h in split(mm(grad3, spread), 2)]
    owner_rows = as_bf16(iota((n, rows), 0) == rows_ref[0:1, :].astype(i32))
    for i in range(line_count):
        here = slot_of == -i * per_line
        placed = jnp.concatenate(
            [jnp.where(here, h, 0.0).astype(bf16) for h in heads], axis=1
        )
        total = mm(owner_rows, placed)
        send_ref[pl.ds(i, n, stride=line_count), :] = total[:, :LANES] + total[:, LANES:]


def scatter_kernel(
    n, cap, base_ref, grad_ref, w_ref, out_ref, held_re, held_im, blocks, sem
):
    halves = (held_re, held_im)
    facets = held_re.shape[1]
    planes = 4 * facets
    fill = 64

    def clear(i, carry):
        for held in halves:
            held[pl.ds(i * fill, fill)] = jnp.zeros((fill, facets, LANES), f32)
        return carry

    lax.fori_loop(0, held_re.shape[0] // fill, clear, 0)
    per_line = LANES // planes
    per = cap // per_line
    pieces = []
    for i in range(per):
        line = grad_ref[pl.ds(i, n, stride=per), :]
        for q in range(per_line):
            pieces.append(line[:, q * planes : (q + 1) * planes])
    per_block = LANES // n
    block_count = cap // per_block
    for jb in range(block_count):
        mine = pieces[jb * per_block : (jb + 1) * per_block]
        joined = mine[0] if per_block == 1 else jnp.concatenate(mine, axis=0)
        blocks[jb] = joined.T
    lane3 = iota((2, facets, LANES), 2)
    copies = []
    for x, held in enumerate(halves):

        def block(jb, carry):
            w_rows = w_ref.at[pl.ds(pl.multiple_of(jb * LANES, LANES), LANES), :]
            values = jnp.stack(
                [blocks[jb, pl.ds((2 * t + x) * facets, facets), :] for t in range(2)]
            )

            def visit(inner, slots):
                starts, windows, adds = [], [], []
                for j, src, lane in slots:
                    starts.append(base_ref[j, src])
                    windows.append(held[pl.ds(starts[-1], 4)])
                for at, (j, src, lane) in enumerate(slots):
                    w = w_rows[pl.ds(lane, 1), :]
                    low, high = w[:, :LANES], w[:, LANES:]
                    value = jnp.sum(
                        jnp.where(lane3 == lane, values, 0.0), axis=2, keepdims=True
                    )
                    window = windows[at] + jnp.concatenate(
                        [value * low, value * high], axis=0
                    )
                    for start, early_value, early_low, early_high in adds:
                        same = jnp.where(start == starts[at], 1.0, 0.0)
                        after = jnp.where(start + 2 == starts[at], 1.0, 0.0)
                        before = jnp.where(start == starts[at] + 2, 1.0, 0.0)
                        shared_low = early_low * same + early_high * after
                        shared_high = early_high * same + early_low * before
                        window = window + jnp.concatenate(
                            [early_value * shared_low, early_value * shared_high], axis=0
                        )
                    windows[at] = window
                    adds.append((starts[at], value, low, high))
                for start, window in zip(starts, windows):
                    held[pl.ds(start, 4)] = window
                return inner

            return each_slot(n, visit, carry, jb, PAIR)

        lax.fori_loop(0, block_count, block, 0)
        for f in range(facets):
            i = x * facets + f
            copy = pltpu.make_async_copy(held.at[:, f], out_ref.at[i], sem.at[i])
            copy.start()
            copies.append(copy)
    for copy in copies:
        copy.wait()


def body(
    visibilities,
    noise_weight,
    keep_flag,
    station_pairs,
    tile_owner,
    tile_offset,
    kernel_taps,
    gain_field,
    sky_grid,
):
    rows, _, channels = visibilities.shape
    taps = kernel_taps.shape[0]
    time_count = lax.axis_size("tm")
    group_count = lax.axis_size("bl")
    n = time_count * group_count
    cap = max(2, 2 * rows // n)
    _, facets, terms, cells = sky_grid.shape
    pairs = 2 * facets
    planes = pairs * terms
    tiles = cells // LANES
    group = gain_field.shape[1]
    stations = group * group_count
    both = ("tm", "bl")
    half = -(-channels // LANES) * LANES
    wide = 2 * half

    gain_turned = gain_field[0].transpose(1, 2, 0, 3)
    fields = taps + 2
    lines = 1 << (-(-fields * cap // LANES) - 1).bit_length()
    shift = jnp.full((1,), lax.axis_index("bl"), i32)
    send, row_table, col_table = pl.pallas_call(
        functools.partial(slots_kernel, n, cap, tiles, group, group_count),
        out_shape=(
            jax.ShapeDtypeStruct((n * lines, LANES), f32),
            jax.ShapeDtypeStruct((8, rows), f32),
            jax.ShapeDtypeStruct((rows, 8), f32),
        ),
        in_specs=[SMEM] + [VMEM] * 6,
        out_specs=(VMEM,) * 3,
        compiler_params=params(),
        cost_estimate=cost(10**9, 10**6),
        name="slots",
    )(
        shift,
        tile_owner.reshape(1, rows),
        tile_offset.reshape(1, rows),
        kernel_taps,
        station_pairs,
        noise_weight.reshape(1, rows),
        keep_flag.reshape(1, rows),
    )

    def exchange(x):
        x = x.reshape(n, -1, LANES)
        x = lax.all_to_all(x, both, split_axis=0, concat_axis=0, tiled=True)
        return x.reshape(-1, LANES)

    sky = (
        sky_grid.reshape(pairs, terms, tiles, LANES)
        .transpose(0, 2, 1, 3)
        .reshape(pairs, terms * tiles, LANES)
    )
    def turn_gains(x, k):
        return lax.ppermute(
            x, "bl", [(i, (i + k) % group_count) for i in range(group_count)]
        )

    send, gain_first = lax.optimization_barrier((send, gain_turned))
    received = exchange(send)
    near = range(1, group_count // 2 + 1)
    far = range(group_count // 2 + 1, group_count)
    part = facets // 2
    early = [turn_gains(gain_first, k) for k in near]
    early += [turn_gains(gain_first[:part], k) for k in far]
    base = received.reshape(n, lines * LANES)[:, (taps + 1) * cap : (taps + 2) * cap]
    base = jnp.clip(base.T.astype(i32), 0, tiles - 2) * terms
    slot_lines = n * cap * planes // LANES
    block_count = n * cap // LANES
    values, weights = pl.pallas_call(
        functools.partial(degrid_kernel, n, cap, taps),
        out_shape=(
            jax.ShapeDtypeStruct((slot_lines, LANES), f32),
            jax.ShapeDtypeStruct((n * cap, 2 * LANES), f32),
        ),
        in_specs=[SMEM, VMEM, ANY],
        out_specs=(VMEM, ANY),
        scratch_shapes=[
            pltpu.VMEM((terms * tiles, facets, LANES), f32),
            pltpu.VMEM((terms * tiles, facets, LANES), f32),
            pltpu.VMEM((n * cap, 2 * LANES), f32),
            pltpu.VMEM((lines * LANES, n), f32),
            pltpu.VMEM((block_count, planes, LANES), f32),
            pltpu.SemaphoreType.DMA((pairs + 1,)),
        ],
        compiler_params=params(),
        cost_estimate=cost(10**8, 7 * 10**7),
        name="degrid",
    )(base, received, sky)
    values, gain_here, *early = lax.optimization_barrier((values, gain_turned, *early))
    back = exchange(values)
    below = lax.ppermute(gain_here, "tm", [(i, i + 1) for i in range(time_count - 1)])
    above = lax.ppermute(gain_here, "tm", [(i + 1, i) for i in range(time_count - 1)])
    late = [turn_gains(gain_here[part:], k) for k in far]
    gathered = [gain_turned, *early, *late]

    vis_wide = jnp.pad(visibilities, ((0, 0), (0, 0), (0, half - channels))).reshape(
        rows, wide
    )
    partial_shape = jax.ShapeDtypeStruct((facets, 2, group, channels), f32)
    outs = pl.pallas_call(
        functools.partial(rows_kernel, n, cap, group_count),
        out_shape=(partial_shape,) * group_count
        + (jax.ShapeDtypeStruct((slot_lines, LANES), f32),),
        in_specs=[VMEM] * (4 + len(gathered)),
        out_specs=(VMEM,) * (group_count + 1),
        scratch_shapes=[
            pltpu.VMEM((facets, stations, wide), f32),
            pltpu.VMEM((facets, 3 * planes, wide), bf16),
            pltpu.VMEM((facets, rows, wide), f32),
            pltpu.VMEM((facets, rows, wide), f32),
            pltpu.VMEM((facets, rows, wide), f32),
            pltpu.VMEM((facets, rows, wide), f32),
            pltpu.VMEM((rows, wide), f32),
            pltpu.VMEM((2 * rows, wide), bf16),
            pltpu.VMEM((2 * rows, wide), bf16),
            pltpu.VMEM((rows, wide), bf16),
            pltpu.VMEM((rows, wide), bf16),
        ],
        compiler_params=params(52),
        cost_estimate=cost(2 * 10**10, 10**7),
        name="rowgrads",
    )(row_table, col_table, vis_wide, back, *gathered)

    own, *parts, send_grad = outs
    when = lax.axis_index("tm")
    prior = jnp.where(when > 0, gain_turned - below, 0.0)
    prior = prior - jnp.where(when < time_count - 1, above - gain_turned, 0.0)
    own = own + smoothness * prior
    got, own = lax.optimization_barrier((exchange(send_grad), own))
    parts = [turn_gains(part, -k) for k, part in enumerate(parts, 1)]
    grid = pl.pallas_call(
        functools.partial(scatter_kernel, n, cap),
        out_shape=jax.ShapeDtypeStruct((pairs, terms * tiles, LANES), f32),
        in_specs=[SMEM, VMEM, VMEM],
        out_specs=ANY,
        scratch_shapes=[
            pltpu.VMEM((terms * tiles, facets, LANES), f32),
            pltpu.VMEM((terms * tiles, facets, LANES), f32),
            pltpu.VMEM((block_count, planes, LANES), f32),
            pltpu.SemaphoreType.DMA((pairs,)),
        ],
        compiler_params=params(40),
        cost_estimate=cost(0, 10**5),
        name="scatter",
    )(base, got, weights)
    grid, *parts = lax.optimization_barrier((grid, *parts))
    for part in parts:
        own = own + part
    grid_gradient = (
        grid.reshape(pairs, tiles, terms, LANES)
        .transpose(0, 2, 1, 3)
        .reshape(sky_grid.shape)
    )
    gain_gradient = own.transpose(2, 0, 1, 3)[None]
    return (gain_gradient, grid_gradient)


def solution(mesh):
    return jax.shard_map(
        body,
        mesh=mesh,
        in_specs=(
            P(("tm", "bl"), None, None),
            P(("tm", "bl")),
            P(("tm", "bl")),
            P(None, ("tm", "bl")),
            P(("tm", "bl"), None),
            P(("tm", "bl")),
            P(None, ("tm", "bl")),
            P("tm", "bl", None, None, None),
            P(None, None, None, ("tm", "bl")),
        ),
        out_specs=(P("tm", "bl", None, None, None), P(None, None, None, ("tm", "bl"))),
        check_vma=False,
    )
```

```python
import functools

import jax
import jax.numpy as jnp
from jax import lax
from jax.experimental import pallas as pl
from jax.experimental.pallas import tpu as pltpu
from jax.sharding import PartitionSpec as P

smoothness = 4.0
LANES = 128
f32 = jnp.float32
bf16 = jnp.bfloat16
i32 = jnp.int32
VMEM = pl.BlockSpec(memory_space=pltpu.VMEM)
SMEM = pl.BlockSpec(memory_space=pltpu.SMEM)
ANY = pl.BlockSpec(memory_space=pl.ANY)
CHUNK = 16
PAIR = 2


def iota(shape, dim):
    return lax.broadcasted_iota(i32, shape, dim)


def as_bf16(mask):
    return jnp.where(mask, 1.0, 0.0).astype(bf16)


def split(x, pieces):
    out = []
    for _ in range(pieces - 1):
        head = x.astype(bf16)
        out.append(head)
        x = x - head.astype(f32)
    out.append(x.astype(bf16))
    return out


def mm(a, b):
    return jnp.dot(a, b, preferred_element_type=f32)


def mm_nt(a, b):
    return lax.dot_general(a, b, (((1,), (1,)), ((), ())), preferred_element_type=f32)


def div(x, k):
    return x >> (k.bit_length() - 1) if k & (k - 1) == 0 else x // k


def mod(x, k):
    return x & (k - 1) if k & (k - 1) == 0 else x - x // k * k


def params(mib=60):
    return pltpu.CompilerParams(vmem_limit_bytes=mib << 20)


def cost(flops, byte_count):
    return pl.CostEstimate(flops=flops, bytes_accessed=byte_count, transcendentals=0)


def read_wide(ref, count):
    per = ref.shape[0] // count
    return jnp.concatenate(
        [ref[pl.ds(i, count, stride=per), :] for i in range(per)], axis=1
    )


def write_wide(ref, value):
    count = value.shape[0]
    per = ref.shape[0] // count
    for i in range(per):
        ref[pl.ds(i, count, stride=per), :] = value[:, i * LANES : (i + 1) * LANES]


def slots_kernel(
    n, cap, tiles, group, group_count,
    shift_ref, owner_ref, offset_ref, taps_ref, pairs_ref, noise_ref, keep_ref,
    send_ref, rows_ref, cols_ref,
):
    rows = owner_ref.shape[1]
    taps = taps_ref.shape[0]
    width = send_ref.shape[0] // n * LANES
    owner = owner_ref[...]
    hit = iota((n, rows), 0) == owner
    onehot = as_bf16(hit)
    earlier = as_bf16(iota((rows, rows), 0) < iota((rows, rows), 1))
    before = mm(onehot, earlier)
    rank = jnp.sum(jnp.where(hit, before, 0.0), axis=0, keepdims=True)
    at_rank = iota((cap, rows), 0) == rank.astype(i32)
    offset = offset_ref[...]
    base = jnp.minimum(offset // LANES, tiles - 2)
    low = offset - base * LANES
    fields = [taps_ref[k : k + 1, :] for k in range(taps)]
    fields += [low.astype(f32), base.astype(f32)]
    parts = [jnp.where(at_rank, v, 0.0) for v in fields]
    spare = width - len(parts) * cap
    if spare:
        parts.append(jnp.zeros((spare, rows), f32))
    total = None
    for piece in split(jnp.concatenate(parts, axis=0), 3):
        term = mm_nt(onehot, piece)
        total = term if total is None else total + term
    write_wide(send_ref, total)
    station = pairs_ref[...]
    turn = shift_ref[0] - station // group + group_count
    turn = jnp.where(turn >= group_count, turn - group_count, turn)
    local = (turn * group + (station - station // group * group)).astype(f32)
    scale = noise_ref[...] * keep_ref[...].astype(f32)
    table = jnp.concatenate(
        [owner.astype(f32), rank, local, scale, jnp.zeros((3, rows), f32)], axis=0
    )
    rows_ref[...] = table
    cols_ref[...] = table.T


def turn_fields(n, cap, count, recv_ref, turn_s):
    per_block = LANES // n
    turn_s[...] = read_wide(recv_ref, n).T
    return [
        jnp.concatenate(
            [
                turn_s[pl.ds(k * cap + q, cap // per_block, stride=per_block), :]
                for q in range(per_block)
            ],
            axis=1,
        )
        for k in range(count)
    ]


def each_slot(n, visit, carry, jb, group):
    per_block = LANES // n
    unroll = min(n, 32)
    for q in range(per_block):
        j = jb * per_block + q

        def step(g, inner):
            first = g * unroll
            for u in range(0, unroll, group):
                slots = [(j, first + v, q * n + first + v) for v in range(u, u + group)]
                inner = visit(inner, slots)
            return inner

        if n == unroll:
            carry = step(0, carry)
        else:
            carry = lax.fori_loop(0, n // unroll, step, carry)
    return carry


def degrid_kernel(
    n, cap, taps,
    base_ref, recv_ref, sky_ref, out_ref, w_ref,
    held_re, held_im, w_s, turn_s, blocks, sem,
):
    halves = (held_re, held_im)
    facets = held_re.shape[1]
    planes = 4 * facets
    copies = []
    for x, held in enumerate(halves):
        mine = []
        for f in range(facets):
            i = x * facets + f
            copy = pltpu.make_async_copy(sky_ref.at[i], held.at[:, f], sem.at[i])
            copy.start()
            mine.append(copy)
        copies.append(mine)
    per_block = LANES // n
    block_count = cap // per_block
    fields = turn_fields(n, cap, taps + 1, recv_ref, turn_s)
    line = iota((2 * LANES, LANES), 0).astype(f32)
    for jb in range(block_count):
        place = line - fields[taps][jb : jb + 1, :]
        w = jnp.zeros((2 * LANES, LANES), f32)
        for k in range(taps):
            w = jnp.where(place == float(k), fields[k][jb : jb + 1, :], w)
        w_s[jb * LANES : (jb + 1) * LANES, :] = w.T
    save = pltpu.make_async_copy(w_s, w_ref, sem.at[2 * facets])
    save.start()
    lane3 = iota((2, facets, LANES), 2)
    for x, held in enumerate(halves):
        for copy in copies[x]:
            copy.wait()
        rows_of = []

        def visit(acc, slots):
            ((j, src, lane),) = slots
            w = rows_of[0][pl.ds(lane, 1), :]
            window = held[pl.ds(base_ref[j, src], 4)]
            prod = window[0:2] * w[:, :LANES] + window[2:4] * w[:, LANES:]
            return jnp.where(
                lane3 == lane, jnp.sum(prod, axis=2, keepdims=True), acc
            )

        def block(jb, carry):
            rows_of[:] = [w_s.at[pl.ds(pl.multiple_of(jb * LANES, LANES), LANES), :]]
            acc = each_slot(n, visit, jnp.zeros((2, facets, LANES), f32), jb, 1)
            for t in range(2):
                blocks[jb, pl.ds((2 * t + x) * facets, facets), :] = acc[t]
            return carry

        lax.fori_loop(0, block_count, block, 0)
    turned = [blocks[jb].T for jb in range(block_count)]
    pieces = []
    for j in range(cap):
        jb, lo = j * n // LANES, j * n % LANES
        pieces.append(turned[jb][lo : lo + n, :planes])
    per_line = LANES // planes
    per = cap // per_line
    for i in range(per):
        wide_line = jnp.concatenate(pieces[i * per_line : (i + 1) * per_line], axis=1)
        out_ref[pl.ds(i, n, stride=per), :] = wide_line
    save.wait()


def rows_kernel(
    n, cap, group_count,
    rows_ref, cols_ref, vis_ref, back_ref, *rest,
):
    far = group_count - group_count // 2 - 1
    gain_refs, rest = rest[: group_count + far], rest[group_count + far :]
    out_refs, send_ref, rest = rest[:group_count], rest[group_count], rest[group_count + 1 :]
    gains, spec, a_s, b_s, m_s, p_s, e_s, glr_hi, glr_lo, gm_hi, gm_lo = rest
    facets, _, group, channels = gain_refs[0].shape
    rows = cols_ref.shape[0]
    stations = group * group_count
    planes = 4 * facets
    pairs = 2 * facets
    half = m_s.shape[2] // 2
    wide = 2 * half
    cols = cols_ref[...]
    owner_col, rank_col = cols[:, 0:1].astype(i32), cols[:, 1:2].astype(i32)
    first_col, second_col = cols[:, 2:3].astype(i32), cols[:, 3:4].astype(i32)

    gains[...] = jnp.zeros(gains.shape, f32)
    for k in range(group_count):
        mine = slice(k * group, (k + 1) * group)
        for f in range(facets):
            ref, at = gain_refs[k], f
            if f >= ref.shape[0]:
                ref, at = gain_refs[k + far], f - ref.shape[0]
            for x in range(2):
                gains[f, mine, x * half : x * half + channels] = ref[at, x]

    owner3 = as_bf16(mod(iota((1, 3 * n), 1), n) == owner_col)
    per_line = LANES // planes
    line_count = cap // per_line
    slot_of = div(iota((1, LANES), 1), planes) - rank_col
    degrid = jnp.zeros((rows, LANES), f32)
    for i in range(line_count):
        line = jnp.concatenate(split(back_ref[pl.ds(i, n, stride=line_count), :], 3), axis=0)
        degrid = degrid + jnp.where(slot_of == -i * per_line, mm(owner3, line), 0.0)
    fold = as_bf16(mod(iota((3 * LANES, planes), 0), planes) == iota((3 * LANES, planes), 1))
    degrid = mm(jnp.concatenate(split(degrid, 3), axis=1), fold)
    term_scale = jnp.where(iota((1, planes), 1) >= pairs, 1.0 / (channels - 1), 1.0)
    d3 = jnp.concatenate(split(degrid * term_scale, 3), axis=1)

    lane_st = mod(iota((1, 3 * stations), 1), stations)
    first3 = as_bf16(lane_st == first_col)
    second3 = as_bf16(lane_st == second_col)
    plane = mod(iota((3 * planes, wide), 0), planes)
    lane_w = iota((3 * planes, wide), 1)
    chan = jnp.where(lane_w >= half, lane_w - half, lane_w)
    side = jnp.where(lane_w >= half, 1, 0)
    value = jnp.where(plane >= pairs, 2 * chan - (channels - 1), 1).astype(f32)
    live = (chan < channels) & (div(mod(plane, pairs), facets) == side)
    value = jnp.where(live, value, 0.0)
    facet_of = mod(plane, facets)
    chunks = [pl.ds(i * CHUNK, CHUNK) for i in range(rows // CHUNK)]

    def gather(f):
        tables = {}

        def prepare():
            tables["gains"] = jnp.concatenate(split(gains[f], 3), axis=0)
            spec[f] = jnp.where(facet_of == f, value, 0.0).astype(bf16)

        def product(ref, left, lanes):
            def run():
                right = spec[f, :, lanes] if left is d3 else tables["gains"][:, lanes]
                ref[f, :, lanes] = mm(left, right)

            return run

        pieces = [prepare]
        for ref, left in ((a_s, first3), (b_s, second3), (m_s, d3)):
            for lanes in (slice(0, half), slice(half, wide)):
                pieces.append(product(ref, left, lanes))
        return pieces

    def load(f, at):
        return (
            a_s[f, at, :half], a_s[f, at, half:],
            b_s[f, at, :half], b_s[f, at, half:],
            m_s[f, at, :half], m_s[f, at, half:],
        )

    def predict(f, waiting):
        for i, at in enumerate(chunks):
            if waiting and i % 4 == 0:
                waiting.pop(0)()
            a_re, a_im, b_re, b_im, m_re, m_im = load(f, at)
            p_re = a_re * b_re + a_im * b_im
            p_im = a_im * b_re - a_re * b_im
            p_s[f, at, :half] = p_re
            p_s[f, at, half:] = p_im
            e_s[at, :half] += p_re * m_re - p_im * m_im
            e_s[at, half:] += p_re * m_im + p_im * m_re

    e_s[...] = -vis_ref[...].astype(f32)
    for run in gather(0):
        run()
    for f in range(facets):
        waiting = gather(f + 1) if f + 1 < facets else []
        predict(f, waiting)
        for run in waiting:
            run()
    e_s[...] = e_s[...] * cols[:, 4:5]

    block = min(rows, 128)
    block_count = rows // block
    station_row = iota((stations, rows), 0)
    to_first = as_bf16(station_row == rows_ref[2:3, :].astype(i32))
    to_second = as_bf16(station_row == rows_ref[3:4, :].astype(i32))
    to_station = []
    for c in range(block_count):
        part = slice(c * block, (c + 1) * block)
        to_station.append(jnp.concatenate([to_first[:, part], to_second[:, part]], axis=1))

    def put(hi_ref, lo_ref, at, lanes, value):
        hi = value.astype(bf16)
        hi_ref[at, lanes] = hi
        lo_ref[at, lanes] = (value - hi.astype(f32)).astype(bf16)

    re_lanes, im_lanes = slice(0, half), slice(half, wide)

    def vector_part(f, c, i):
        at = pl.ds(c * block + i * CHUNK, CHUNK)
        left = pl.ds(2 * c * block + i * CHUNK, CHUNK)
        right = pl.ds((2 * c + 1) * block + i * CHUNK, CHUNK)
        e_re, e_im = e_s[at, :half], e_s[at, half:]
        a_re, a_im, b_re, b_im, m_re, m_im = load(f, at)
        p_re, p_im = p_s[f, at, :half], p_s[f, at, half:]
        t_re = e_re * m_re + e_im * m_im
        t_im = e_im * m_re - e_re * m_im
        put(glr_hi, glr_lo, left, re_lanes, t_re * b_re - t_im * b_im)
        put(glr_hi, glr_lo, left, im_lanes, t_re * b_im + t_im * b_re)
        put(glr_hi, glr_lo, right, re_lanes, t_re * a_re + t_im * a_im)
        put(glr_hi, glr_lo, right, im_lanes, t_re * a_im - t_im * a_re)
        put(gm_hi, gm_lo, at, re_lanes, e_re * p_re + e_im * p_im)
        put(gm_hi, gm_lo, at, im_lanes, e_im * p_re - e_re * p_im)

    def matmul_parts(f, c, sums, parts):
        both = pl.ds(2 * c * block, 2 * block)
        here = pl.ds(c * block, block)

        def station(x, ref):
            def run():
                term = mm(to_station[c], ref[both, x * half : (x + 1) * half])
                sums[x] = term if sums[x] is None else sums[x] + term

            return run

        def plane_sum(ref):
            def run():
                parts[c] = parts[c] + mm_nt(ref[here, :], spec[f, :planes, :])

            return run

        return [
            station(0, glr_hi), station(1, glr_hi), station(0, glr_lo),
            station(1, glr_lo), plane_sum(gm_hi), plane_sum(gm_lo),
        ]

    def put_out(f, sums):
        for k in range(group_count):
            for x in range(2):
                out_refs[k][f, x] = sums[x][k * group : (k + 1) * group, :channels]

    last = block_count - 1

    def grads(f, carry):
        old_sums, parts = list(carry[0]), list(carry[1])
        before = jnp.maximum(f - 1, 0)
        sums = [None, None]
        waiting = matmul_parts(before, last, old_sums, parts)
        for c in range(block_count):
            for i in range(block // CHUNK):
                vector_part(f, c, i)
                if c == 0 and i == 0:
                    continue
                if waiting:
                    waiting.pop(0)()
            for run in waiting:
                run()
            if c == 0:
                put_out(before, old_sums)
            waiting = matmul_parts(f, c, sums, parts) if c < last else []
        return tuple(sums), tuple(parts)

    tail_wide, tail = pl.ds(2 * last * block, 2 * block), pl.ds(last * block, block)
    for ref in (glr_hi, glr_lo):
        ref[tail_wide, :] = jnp.zeros((2 * block, wide), bf16)
    for ref in (gm_hi, gm_lo):
        ref[tail, :] = jnp.zeros((block, wide), bf16)
    no_sum = jnp.zeros((stations, half), f32)
    no_part = jnp.zeros((block, planes), f32)
    sums, parts = lax.fori_loop(
        0, facets, grads, ((no_sum, no_sum), (no_part,) * block_count)
    )
    sums, parts = list(sums), list(parts)
    for run in matmul_parts(facets - 1, last, sums, parts):
        run()
    put_out(facets - 1, sums)
    grad_degrid = jnp.concatenate(parts, axis=0)
    grad3 = jnp.concatenate(split(grad_degrid * term_scale, 3), axis=1)
    spread = as_bf16(
        mod(iota((3 * planes, LANES), 0), planes) == mod(iota((3 * planes, LANES), 1), planes)
    )
    heads = [h.astype(f32) for h in split(mm(grad3, spread), 2)]
    owner_rows = as_bf16(iota((n, rows), 0) == rows_ref[0:1, :].astype(i32))
    for i in range(line_count):
        here = slot_of == -i * per_line
        placed = jnp.concatenate(
            [jnp.where(here, h, 0.0).astype(bf16) for h in heads], axis=1
        )
        total = mm(owner_rows, placed)
        send_ref[pl.ds(i, n, stride=line_count), :] = total[:, :LANES] + total[:, LANES:]


def scatter_kernel(
    n, cap, base_ref, grad_ref, w_ref, out_ref, held_re, held_im, blocks, sem
):
    halves = (held_re, held_im)
    facets = held_re.shape[1]
    planes = 4 * facets
    fill = 64

    def clear(i, carry):
        for held in halves:
            held[pl.ds(i * fill, fill)] = jnp.zeros((fill, facets, LANES), f32)
        return carry

    lax.fori_loop(0, held_re.shape[0] // fill, clear, 0)
    per_line = LANES // planes
    per = cap // per_line
    pieces = []
    for i in range(per):
        line = grad_ref[pl.ds(i, n, stride=per), :]
        for q in range(per_line):
            pieces.append(line[:, q * planes : (q + 1) * planes])
    per_block = LANES // n
    block_count = cap // per_block
    for jb in range(block_count):
        mine = pieces[jb * per_block : (jb + 1) * per_block]
        joined = mine[0] if per_block == 1 else jnp.concatenate(mine, axis=0)
        blocks[jb] = joined.T
    lane3 = iota((2, facets, LANES), 2)
    copies = []
    for x, held in enumerate(halves):

        def block(jb, carry):
            w_rows = w_ref.at[pl.ds(pl.multiple_of(jb * LANES, LANES), LANES), :]
            values = jnp.stack(
                [blocks[jb, pl.ds((2 * t + x) * facets, facets), :] for t in range(2)]
            )

            def visit(inner, slots):
                starts, windows, adds = [], [], []
                for j, src, lane in slots:
                    starts.append(base_ref[j, src])
                    windows.append(held[pl.ds(starts[-1], 4)])
                for at, (j, src, lane) in enumerate(slots):
                    w = w_rows[pl.ds(lane, 1), :]
                    low, high = w[:, :LANES], w[:, LANES:]
                    value = jnp.sum(
                        jnp.where(lane3 == lane, values, 0.0), axis=2, keepdims=True
                    )
                    window = windows[at] + jnp.concatenate(
                        [value * low, value * high], axis=0
                    )
                    for start, early_value, early_low, early_high in adds:
                        same = jnp.where(start == starts[at], 1.0, 0.0)
                        after = jnp.where(start + 2 == starts[at], 1.0, 0.0)
                        before = jnp.where(start == starts[at] + 2, 1.0, 0.0)
                        shared_low = early_low * same + early_high * after
                        shared_high = early_high * same + early_low * before
                        window = window + jnp.concatenate(
                            [early_value * shared_low, early_value * shared_high], axis=0
                        )
                    windows[at] = window
                    adds.append((starts[at], value, low, high))
                for start, window in zip(starts, windows):
                    held[pl.ds(start, 4)] = window
                return inner

            return each_slot(n, visit, carry, jb, PAIR)

        lax.fori_loop(0, block_count, block, 0)
        for f in range(facets):
            i = x * facets + f
            copy = pltpu.make_async_copy(held.at[:, f], out_ref.at[i], sem.at[i])
            copy.start()
            copies.append(copy)
    for copy in copies:
        copy.wait()


def body(
    visibilities,
    noise_weight,
    keep_flag,
    station_pairs,
    tile_owner,
    tile_offset,
    kernel_taps,
    gain_field,
    sky_grid,
):
    rows, _, channels = visibilities.shape
    taps = kernel_taps.shape[0]
    time_count = lax.axis_size("tm")
    group_count = lax.axis_size("bl")
    n = time_count * group_count
    cap = max(2, 2 * rows // n)
    _, facets, terms, cells = sky_grid.shape
    pairs = 2 * facets
    planes = pairs * terms
    tiles = cells // LANES
    group = gain_field.shape[1]
    stations = group * group_count
    both = ("tm", "bl")
    half = -(-channels // LANES) * LANES
    wide = 2 * half

    gain_turned = gain_field[0].transpose(1, 2, 0, 3)
    fields = taps + 2
    lines = 1 << (-(-fields * cap // LANES) - 1).bit_length()
    shift = jnp.full((1,), lax.axis_index("bl"), i32)
    send, row_table, col_table = pl.pallas_call(
        functools.partial(slots_kernel, n, cap, tiles, group, group_count),
        out_shape=(
            jax.ShapeDtypeStruct((n * lines, LANES), f32),
            jax.ShapeDtypeStruct((8, rows), f32),
            jax.ShapeDtypeStruct((rows, 8), f32),
        ),
        in_specs=[SMEM] + [VMEM] * 6,
        out_specs=(VMEM,) * 3,
        compiler_params=params(),
        cost_estimate=cost(10**9, 10**6),
        name="slots",
    )(
        shift,
        tile_owner.reshape(1, rows),
        tile_offset.reshape(1, rows),
        kernel_taps,
        station_pairs,
        noise_weight.reshape(1, rows),
        keep_flag.reshape(1, rows),
    )

    def exchange(x):
        x = x.reshape(n, -1, LANES)
        x = lax.all_to_all(x, both, split_axis=0, concat_axis=0, tiled=True)
        return x.reshape(-1, LANES)

    sky = (
        sky_grid.reshape(pairs, terms, tiles, LANES)
        .transpose(0, 2, 1, 3)
        .reshape(pairs, terms * tiles, LANES)
    )
    def turn_gains(x, k):
        return lax.ppermute(
            x, "bl", [(i, (i + k) % group_count) for i in range(group_count)]
        )

    send, gain_first = lax.optimization_barrier((send, gain_turned))
    received = exchange(send)
    near = range(1, group_count // 2 + 1)
    far = range(group_count // 2 + 1, group_count)
    part = facets // 2
    early = [turn_gains(gain_first, k) for k in near]
    early += [turn_gains(gain_first[:part], k) for k in far]
    below = lax.ppermute(gain_first, "tm", [(i, i + 1) for i in range(time_count - 1)])
    base = received.reshape(n, lines * LANES)[:, (taps + 1) * cap : (taps + 2) * cap]
    base = jnp.clip(base.T.astype(i32), 0, tiles - 2) * terms
    slot_lines = n * cap * planes // LANES
    block_count = n * cap // LANES
    values, weights = pl.pallas_call(
        functools.partial(degrid_kernel, n, cap, taps),
        out_shape=(
            jax.ShapeDtypeStruct((slot_lines, LANES), f32),
            jax.ShapeDtypeStruct((n * cap, 2 * LANES), f32),
        ),
        in_specs=[SMEM, VMEM, ANY],
        out_specs=(VMEM, ANY),
        scratch_shapes=[
            pltpu.VMEM((terms * tiles, facets, LANES), f32),
            pltpu.VMEM((terms * tiles, facets, LANES), f32),
            pltpu.VMEM((n * cap, 2 * LANES), f32),
            pltpu.VMEM((lines * LANES, n), f32),
            pltpu.VMEM((block_count, planes, LANES), f32),
            pltpu.SemaphoreType.DMA((pairs + 1,)),
        ],
        compiler_params=params(),
        cost_estimate=cost(10**8, 7 * 10**7),
        name="degrid",
    )(base, received, sky)
    values, gain_here, below, *early = lax.optimization_barrier(
        (values, gain_turned, below, *early)
    )
    back = exchange(values)
    above = lax.ppermute(gain_here, "tm", [(i + 1, i) for i in range(time_count - 1)])
    late = [turn_gains(gain_here[part:], k) for k in far]
    gathered = [gain_turned, *early, *late]

    vis_wide = jnp.pad(visibilities, ((0, 0), (0, 0), (0, half - channels))).reshape(
        rows, wide
    )
    partial_shape = jax.ShapeDtypeStruct((facets, 2, group, channels), f32)
    outs = pl.pallas_call(
        functools.partial(rows_kernel, n, cap, group_count),
        out_shape=(partial_shape,) * group_count
        + (jax.ShapeDtypeStruct((slot_lines, LANES), f32),),
        in_specs=[VMEM] * (4 + len(gathered)),
        out_specs=(VMEM,) * (group_count + 1),
        scratch_shapes=[
            pltpu.VMEM((facets, stations, wide), f32),
            pltpu.VMEM((facets, 3 * planes, wide), bf16),
            pltpu.VMEM((facets, rows, wide), f32),
            pltpu.VMEM((facets, rows, wide), f32),
            pltpu.VMEM((facets, rows, wide), f32),
            pltpu.VMEM((facets, rows, wide), f32),
            pltpu.VMEM((rows, wide), f32),
            pltpu.VMEM((2 * rows, wide), bf16),
            pltpu.VMEM((2 * rows, wide), bf16),
            pltpu.VMEM((rows, wide), bf16),
            pltpu.VMEM((rows, wide), bf16),
        ],
        compiler_params=params(52),
        cost_estimate=cost(2 * 10**10, 10**7),
        name="rowgrads",
    )(row_table, col_table, vis_wide, back, *gathered)

    own, *parts, send_grad = outs
    when = lax.axis_index("tm")
    prior = jnp.where(when > 0, gain_turned - below, 0.0)
    prior = prior - jnp.where(when < time_count - 1, above - gain_turned, 0.0)
    own = own + smoothness * prior
    got, own = lax.optimization_barrier((exchange(send_grad), own))
    parts = [turn_gains(part, -k) for k, part in enumerate(parts, 1)]
    grid = pl.pallas_call(
        functools.partial(scatter_kernel, n, cap),
        out_shape=jax.ShapeDtypeStruct((pairs, terms * tiles, LANES), f32),
        in_specs=[SMEM, VMEM, VMEM],
        out_specs=ANY,
        scratch_shapes=[
            pltpu.VMEM((terms * tiles, facets, LANES), f32),
            pltpu.VMEM((terms * tiles, facets, LANES), f32),
            pltpu.VMEM((block_count, planes, LANES), f32),
            pltpu.SemaphoreType.DMA((pairs,)),
        ],
        compiler_params=params(40),
        cost_estimate=cost(0, 10**5),
        name="scatter",
    )(base, got, weights)
    grid, *parts = lax.optimization_barrier((grid, *parts))
    for part in parts:
        own = own + part
    grid_gradient = (
        grid.reshape(pairs, tiles, terms, LANES)
        .transpose(0, 2, 1, 3)
        .reshape(sky_grid.shape)
    )
    gain_gradient = own.transpose(2, 0, 1, 3)[None]
    return (gain_gradient, grid_gradient)


def solution(mesh):
    return jax.shard_map(
        body,
        mesh=mesh,
        in_specs=(
            P(("tm", "bl"), None, None),
            P(("tm", "bl")),
            P(("tm", "bl")),
            P(None, ("tm", "bl")),
            P(("tm", "bl"), None),
            P(("tm", "bl")),
            P(None, ("tm", "bl")),
            P("tm", "bl", None, None, None),
            P(None, None, None, ("tm", "bl")),
        ),
        out_specs=(P("tm", "bl", None, None, None), P(None, None, None, ("tm", "bl"))),
        check_vma=False,
    )
```

```python
import functools

import jax
import jax.numpy as jnp
from jax import lax
from jax.experimental import pallas as pl
from jax.experimental.pallas import tpu as pltpu
from jax.sharding import PartitionSpec as P

smoothness = 4.0
LANES = 128
f32 = jnp.float32
bf16 = jnp.bfloat16
i32 = jnp.int32
VMEM = pl.BlockSpec(memory_space=pltpu.VMEM)
SMEM = pl.BlockSpec(memory_space=pltpu.SMEM)
ANY = pl.BlockSpec(memory_space=pl.ANY)
CHUNK = 16
PAIR = 2


def iota(shape, dim):
    return lax.broadcasted_iota(i32, shape, dim)


def as_bf16(mask):
    return jnp.where(mask, 1.0, 0.0).astype(bf16)


def split(x, pieces):
    out = []
    for _ in range(pieces - 1):
        head = x.astype(bf16)
        out.append(head)
        x = x - head.astype(f32)
    out.append(x.astype(bf16))
    return out


def mm(a, b):
    return jnp.dot(a, b, preferred_element_type=f32)


def mm_nt(a, b):
    return lax.dot_general(a, b, (((1,), (1,)), ((), ())), preferred_element_type=f32)


def div(x, k):
    return x >> (k.bit_length() - 1) if k & (k - 1) == 0 else x // k


def mod(x, k):
    return x & (k - 1) if k & (k - 1) == 0 else x - x // k * k


def params(mib=60):
    return pltpu.CompilerParams(vmem_limit_bytes=mib << 20)


def cost(flops, byte_count):
    return pl.CostEstimate(flops=flops, bytes_accessed=byte_count, transcendentals=0)


def read_wide(ref, count):
    per = ref.shape[0] // count
    return jnp.concatenate(
        [ref[pl.ds(i, count, stride=per), :] for i in range(per)], axis=1
    )


def write_wide(ref, value):
    count = value.shape[0]
    per = ref.shape[0] // count
    for i in range(per):
        ref[pl.ds(i, count, stride=per), :] = value[:, i * LANES : (i + 1) * LANES]


def slots_kernel(
    n, cap, tiles, group, group_count,
    shift_ref, owner_ref, offset_ref, taps_ref, pairs_ref, noise_ref, keep_ref,
    send_ref, rows_ref, cols_ref,
):
    rows = owner_ref.shape[1]
    taps = taps_ref.shape[0]
    width = send_ref.shape[0] // n * LANES
    owner = owner_ref[...]
    hit = iota((n, rows), 0) == owner
    onehot = as_bf16(hit)
    earlier = as_bf16(iota((rows, rows), 0) < iota((rows, rows), 1))
    before = mm(onehot, earlier)
    rank = jnp.sum(jnp.where(hit, before, 0.0), axis=0, keepdims=True)
    at_rank = iota((cap, rows), 0) == rank.astype(i32)
    offset = offset_ref[...]
    base = jnp.minimum(offset // LANES, tiles - 2)
    low = offset - base * LANES
    fields = [taps_ref[k : k + 1, :] for k in range(taps)]
    fields += [low.astype(f32), base.astype(f32)]
    parts = [jnp.where(at_rank, v, 0.0) for v in fields]
    spare = width - len(parts) * cap
    if spare:
        parts.append(jnp.zeros((spare, rows), f32))
    total = None
    for piece in split(jnp.concatenate(parts, axis=0), 3):
        term = mm_nt(onehot, piece)
        total = term if total is None else total + term
    write_wide(send_ref, total)
    station = pairs_ref[...]
    turn = shift_ref[0] - station // group + group_count
    turn = jnp.where(turn >= group_count, turn - group_count, turn)
    local = (turn * group + (station - station // group * group)).astype(f32)
    scale = noise_ref[...] * keep_ref[...].astype(f32)
    table = jnp.concatenate(
        [owner.astype(f32), rank, local, scale, jnp.zeros((3, rows), f32)], axis=0
    )
    rows_ref[...] = table
    cols_ref[...] = table.T


def turn_fields(n, cap, count, recv_ref, turn_s):
    per_block = LANES // n
    turn_s[...] = read_wide(recv_ref, n).T
    return [
        jnp.concatenate(
            [
                turn_s[pl.ds(k * cap + q, cap // per_block, stride=per_block), :]
                for q in range(per_block)
            ],
            axis=1,
        )
        for k in range(count)
    ]


def each_slot(n, visit, carry, jb, group):
    per_block = LANES // n
    unroll = min(n, 32)
    for q in range(per_block):
        j = jb * per_block + q

        def step(g, inner):
            first = g * unroll
            for u in range(0, unroll, group):
                slots = [(j, first + v, q * n + first + v) for v in range(u, u + group)]
                inner = visit(inner, slots)
            return inner

        if n == unroll:
            carry = step(0, carry)
        else:
            carry = lax.fori_loop(0, n // unroll, step, carry)
    return carry


def degrid_kernel(
    n, cap, taps,
    base_ref, recv_ref, sky_ref, out_ref, w_ref,
    held_re, held_im, w_s, turn_s, blocks, sem,
):
    halves = (held_re, held_im)
    facets = held_re.shape[1]
    planes = 4 * facets
    copies = []
    for x, held in enumerate(halves):
        mine = []
        for f in range(facets):
            i = x * facets + f
            copy = pltpu.make_async_copy(sky_ref.at[i], held.at[:, f], sem.at[i])
            copy.start()
            mine.append(copy)
        copies.append(mine)
    per_block = LANES // n
    block_count = cap // per_block
    fields = turn_fields(n, cap, taps + 1, recv_ref, turn_s)
    line = iota((2 * LANES, LANES), 0).astype(f32)
    for jb in range(block_count):
        place = line - fields[taps][jb : jb + 1, :]
        w = jnp.zeros((2 * LANES, LANES), f32)
        for k in range(taps):
            w = jnp.where(place == float(k), fields[k][jb : jb + 1, :], w)
        w_s[jb * LANES : (jb + 1) * LANES, :] = w.T
    save = pltpu.make_async_copy(w_s, w_ref, sem.at[2 * facets])
    save.start()
    lane3 = iota((2, facets, LANES), 2)
    for x, held in enumerate(halves):
        for copy in copies[x]:
            copy.wait()
        rows_of = []

        def visit(acc, slots):
            ((j, src, lane),) = slots
            w = rows_of[0][pl.ds(lane, 1), :]
            window = held[pl.ds(base_ref[j, src], 4)]
            prod = window[0:2] * w[:, :LANES] + window[2:4] * w[:, LANES:]
            return jnp.where(
                lane3 == lane, jnp.sum(prod, axis=2, keepdims=True), acc
            )

        def block(jb, carry):
            rows_of[:] = [w_s.at[pl.ds(pl.multiple_of(jb * LANES, LANES), LANES), :]]
            acc = each_slot(n, visit, jnp.zeros((2, facets, LANES), f32), jb, 1)
            for t in range(2):
                blocks[jb, pl.ds((2 * t + x) * facets, facets), :] = acc[t]
            return carry

        lax.fori_loop(0, block_count, block, 0)
    turned = [blocks[jb].T for jb in range(block_count)]
    pieces = []
    for j in range(cap):
        jb, lo = j * n // LANES, j * n % LANES
        pieces.append(turned[jb][lo : lo + n, :planes])
    per_line = LANES // planes
    per = cap // per_line
    for i in range(per):
        wide_line = jnp.concatenate(pieces[i * per_line : (i + 1) * per_line], axis=1)
        out_ref[pl.ds(i, n, stride=per), :] = wide_line
    save.wait()


def rows_kernel(
    n, cap, group_count,
    rows_ref, cols_ref, vis_ref, back_ref, *rest,
):
    far = group_count - group_count // 2 - 1
    gain_refs, rest = rest[: group_count + far], rest[group_count + far :]
    out_refs, send_ref, rest = rest[:group_count], rest[group_count], rest[group_count + 1 :]
    gains, spec, a_s, b_s, m_s, p_s, e_s, glr_hi, glr_lo, gm_hi, gm_lo = rest
    facets, _, group, channels = gain_refs[0].shape
    rows = cols_ref.shape[0]
    stations = group * group_count
    planes = 4 * facets
    pairs = 2 * facets
    half = m_s.shape[2] // 2
    wide = 2 * half
    cols = cols_ref[...]
    owner_col, rank_col = cols[:, 0:1].astype(i32), cols[:, 1:2].astype(i32)
    first_col, second_col = cols[:, 2:3].astype(i32), cols[:, 3:4].astype(i32)

    gains[...] = jnp.zeros(gains.shape, f32)
    for k in range(group_count):
        mine = slice(k * group, (k + 1) * group)
        for f in range(facets):
            ref, at = gain_refs[k], f
            if f >= ref.shape[0]:
                ref, at = gain_refs[k + far], f - ref.shape[0]
            for x in range(2):
                gains[f, mine, x * half : x * half + channels] = ref[at, x]

    owner3 = as_bf16(mod(iota((1, 3 * n), 1), n) == owner_col)
    per_line = LANES // planes
    line_count = cap // per_line
    slot_of = div(iota((1, LANES), 1), planes) - rank_col
    degrid = jnp.zeros((rows, LANES), f32)
    for i in range(line_count):
        line = jnp.concatenate(split(back_ref[pl.ds(i, n, stride=line_count), :], 3), axis=0)
        degrid = degrid + jnp.where(slot_of == -i * per_line, mm(owner3, line), 0.0)
    fold = as_bf16(mod(iota((3 * LANES, planes), 0), planes) == iota((3 * LANES, planes), 1))
    degrid = mm(jnp.concatenate(split(degrid, 3), axis=1), fold)
    term_scale = jnp.where(iota((1, planes), 1) >= pairs, 1.0 / (channels - 1), 1.0)
    d3 = jnp.concatenate(split(degrid * term_scale, 3), axis=1)

    lane_st = mod(iota((1, 3 * stations), 1), stations)
    first3 = as_bf16(lane_st == first_col)
    second3 = as_bf16(lane_st == second_col)
    plane = mod(iota((3 * planes, wide), 0), planes)
    lane_w = iota((3 * planes, wide), 1)
    chan = jnp.where(lane_w >= half, lane_w - half, lane_w)
    side = jnp.where(lane_w >= half, 1, 0)
    value = jnp.where(plane >= pairs, 2 * chan - (channels - 1), 1).astype(f32)
    live = (chan < channels) & (div(mod(plane, pairs), facets) == side)
    value = jnp.where(live, value, 0.0)
    facet_of = mod(plane, facets)
    chunks = [pl.ds(i * CHUNK, CHUNK) for i in range(rows // CHUNK)]

    def gather(f):
        table = jnp.concatenate(split(gains[f], 3), axis=0)
        spec[f] = jnp.where(facet_of == f, value, 0.0).astype(bf16)
        a_s[f] = mm(first3, table)
        b_s[f] = mm(second3, table)
        m_s[f] = mm(d3, spec[f])

    def load(f, at):
        return (
            a_s[f, at, :half], a_s[f, at, half:],
            b_s[f, at, :half], b_s[f, at, half:],
            m_s[f, at, :half], m_s[f, at, half:],
        )

    def predict(f):
        for at in chunks:
            a_re, a_im, b_re, b_im, m_re, m_im = load(f, at)
            p_re = a_re * b_re + a_im * b_im
            p_im = a_im * b_re - a_re * b_im
            p_s[f, at, :half] = p_re
            p_s[f, at, half:] = p_im
            e_s[at, :half] += p_re * m_re - p_im * m_im
            e_s[at, half:] += p_re * m_im + p_im * m_re

    e_s[...] = -vis_ref[...].astype(f32)
    gather(0)

    for f in range(facets):
        if f + 1 < facets:
            gather(f + 1)
        predict(f)
    e_s[...] = e_s[...] * cols[:, 4:5]

    block = min(rows, 128)
    block_count = rows // block
    station_row = iota((stations, rows), 0)
    to_first = as_bf16(station_row == rows_ref[2:3, :].astype(i32))
    to_second = as_bf16(station_row == rows_ref[3:4, :].astype(i32))
    to_station = []
    for c in range(block_count):
        part = slice(c * block, (c + 1) * block)
        to_station.append(jnp.concatenate([to_first[:, part], to_second[:, part]], axis=1))

    def put(hi_ref, lo_ref, at, lanes, value):
        hi = value.astype(bf16)
        hi_ref[at, lanes] = hi
        lo_ref[at, lanes] = (value - hi.astype(f32)).astype(bf16)

    re_lanes, im_lanes = slice(0, half), slice(half, wide)

    def vector_part(f, c, i):
        at = pl.ds(c * block + i * CHUNK, CHUNK)
        left = pl.ds(2 * c * block + i * CHUNK, CHUNK)
        right = pl.ds((2 * c + 1) * block + i * CHUNK, CHUNK)
        e_re, e_im = e_s[at, :half], e_s[at, half:]
        a_re, a_im, b_re, b_im, m_re, m_im = load(f, at)
        p_re, p_im = p_s[f, at, :half], p_s[f, at, half:]
        t_re = e_re * m_re + e_im * m_im
        t_im = e_im * m_re - e_re * m_im
        put(glr_hi, glr_lo, left, re_lanes, t_re * b_re - t_im * b_im)
        put(glr_hi, glr_lo, left, im_lanes, t_re * b_im + t_im * b_re)
        put(glr_hi, glr_lo, right, re_lanes, t_re * a_re + t_im * a_im)
        put(glr_hi, glr_lo, right, im_lanes, t_re * a_im - t_im * a_re)
        put(gm_hi, gm_lo, at, re_lanes, e_re * p_re + e_im * p_im)
        put(gm_hi, gm_lo, at, im_lanes, e_im * p_re - e_re * p_im)

    def matmul_parts(f, c, sums, parts):
        both = pl.ds(2 * c * block, 2 * block)
        here = pl.ds(c * block, block)

        def station(x, ref):
            def run():
                term = mm(to_station[c], ref[both, x * half : (x + 1) * half])
                sums[x] = term if sums[x] is None else sums[x] + term

            return run

        def plane_sum(ref):
            def run():
                term = mm_nt(ref[here, :], spec[f, :planes, :])
                parts[c] = term if parts[c] is None else parts[c] + term

            return run

        return [
            station(0, glr_hi), station(1, glr_hi), station(0, glr_lo),
            station(1, glr_lo), plane_sum(gm_hi), plane_sum(gm_lo),
        ]

    def grads(f, grad_degrid):
        sums, parts, waiting = [None, None], [None] * block_count, []
        for c in range(block_count):
            for i in range(block // CHUNK):
                vector_part(f, c, i)
                if waiting:
                    waiting.pop(0)()
            for run in waiting:
                run()
            waiting = matmul_parts(f, c, sums, parts)
        for run in waiting:
            run()
        for k in range(group_count):
            for x in range(2):
                out_refs[k][f, x] = sums[x][k * group : (k + 1) * group, :channels]
        return grad_degrid + jnp.concatenate(parts, axis=0)

    grad_degrid = lax.fori_loop(0, facets, grads, jnp.zeros((rows, planes), f32))
    grad3 = jnp.concatenate(split(grad_degrid * term_scale, 3), axis=1)
    spread = as_bf16(
        mod(iota((3 * planes, LANES), 0), planes) == mod(iota((3 * planes, LANES), 1), planes)
    )
    heads = [h.astype(f32) for h in split(mm(grad3, spread), 2)]
    owner_rows = as_bf16(iota((n, rows), 0) == rows_ref[0:1, :].astype(i32))
    for i in range(line_count):
        here = slot_of == -i * per_line
        placed = jnp.concatenate(
            [jnp.where(here, h, 0.0).astype(bf16) for h in heads], axis=1
        )
        total = mm(owner_rows, placed)
        send_ref[pl.ds(i, n, stride=line_count), :] = total[:, :LANES] + total[:, LANES:]


def scatter_kernel(
    n, cap, base_ref, grad_ref, w_ref, out_ref, held_re, held_im, blocks, sem
):
    halves = (held_re, held_im)
    facets = held_re.shape[1]
    planes = 4 * facets
    fill = 64

    def clear(i, carry):
        for held in halves:
            held[pl.ds(i * fill, fill)] = jnp.zeros((fill, facets, LANES), f32)
        return carry

    lax.fori_loop(0, held_re.shape[0] // fill, clear, 0)
    per_line = LANES // planes
    per = cap // per_line
    pieces = []
    for i in range(per):
        line = grad_ref[pl.ds(i, n, stride=per), :]
        for q in range(per_line):
            pieces.append(line[:, q * planes : (q + 1) * planes])
    per_block = LANES // n
    block_count = cap // per_block
    for jb in range(block_count):
        mine = pieces[jb * per_block : (jb + 1) * per_block]
        joined = mine[0] if per_block == 1 else jnp.concatenate(mine, axis=0)
        blocks[jb] = joined.T
    lane3 = iota((2, facets, LANES), 2)
    copies = []
    for x, held in enumerate(halves):

        def block(jb, carry):
            w_rows = w_ref.at[pl.ds(pl.multiple_of(jb * LANES, LANES), LANES), :]
            values = jnp.stack(
                [blocks[jb, pl.ds((2 * t + x) * facets, facets), :] for t in range(2)]
            )

            def visit(inner, slots):
                starts, windows, adds = [], [], []
                for j, src, lane in slots:
                    starts.append(base_ref[j, src])
                    windows.append(held[pl.ds(starts[-1], 4)])
                for at, (j, src, lane) in enumerate(slots):
                    w = w_rows[pl.ds(lane, 1), :]
                    low, high = w[:, :LANES], w[:, LANES:]
                    value = jnp.sum(
                        jnp.where(lane3 == lane, values, 0.0), axis=2, keepdims=True
                    )
                    window = windows[at] + jnp.concatenate(
                        [value * low, value * high], axis=0
                    )
                    for start, early_value, early_low, early_high in adds:
                        same = jnp.where(start == starts[at], 1.0, 0.0)
                        after = jnp.where(start + 2 == starts[at], 1.0, 0.0)
                        before = jnp.where(start == starts[at] + 2, 1.0, 0.0)
                        shared_low = early_low * same + early_high * after
                        shared_high = early_high * same + early_low * before
                        window = window + jnp.concatenate(
                            [early_value * shared_low, early_value * shared_high], axis=0
                        )
                    windows[at] = window
                    adds.append((starts[at], value, low, high))
                for start, window in zip(starts, windows):
                    held[pl.ds(start, 4)] = window
                return inner

            return each_slot(n, visit, carry, jb, PAIR)

        lax.fori_loop(0, block_count, block, 0)
        for f in range(facets):
            i = x * facets + f
            copy = pltpu.make_async_copy(held.at[:, f], out_ref.at[i], sem.at[i])
            copy.start()
            copies.append(copy)
    for copy in copies:
        copy.wait()


def body(
    visibilities,
    noise_weight,
    keep_flag,
    station_pairs,
    tile_owner,
    tile_offset,
    kernel_taps,
    gain_field,
    sky_grid,
):
    rows, _, channels = visibilities.shape
    taps = kernel_taps.shape[0]
    time_count = lax.axis_size("tm")
    group_count = lax.axis_size("bl")
    n = time_count * group_count
    cap = max(2, 2 * rows // n)
    _, facets, terms, cells = sky_grid.shape
    pairs = 2 * facets
    planes = pairs * terms
    tiles = cells // LANES
    group = gain_field.shape[1]
    stations = group * group_count
    both = ("tm", "bl")
    half = -(-channels // LANES) * LANES
    wide = 2 * half

    gain_turned = gain_field[0].transpose(1, 2, 0, 3)
    fields = taps + 2
    lines = 1 << (-(-fields * cap // LANES) - 1).bit_length()
    shift = jnp.full((1,), lax.axis_index("bl"), i32)
    send, row_table, col_table = pl.pallas_call(
        functools.partial(slots_kernel, n, cap, tiles, group, group_count),
        out_shape=(
            jax.ShapeDtypeStruct((n * lines, LANES), f32),
            jax.ShapeDtypeStruct((8, rows), f32),
            jax.ShapeDtypeStruct((rows, 8), f32),
        ),
        in_specs=[SMEM] + [VMEM] * 6,
        out_specs=(VMEM,) * 3,
        compiler_params=params(),
        cost_estimate=cost(10**9, 10**6),
        name="slots",
    )(
        shift,
        tile_owner.reshape(1, rows),
        tile_offset.reshape(1, rows),
        kernel_taps,
        station_pairs,
        noise_weight.reshape(1, rows),
        keep_flag.reshape(1, rows),
    )

    def exchange(x):
        x = x.reshape(n, -1, LANES)
        x = lax.all_to_all(x, both, split_axis=0, concat_axis=0, tiled=True)
        return x.reshape(-1, LANES)

    sky = (
        sky_grid.reshape(pairs, terms, tiles, LANES)
        .transpose(0, 2, 1, 3)
        .reshape(pairs, terms * tiles, LANES)
    )
    def turn_gains(x, k):
        return lax.ppermute(
            x, "bl", [(i, (i + k) % group_count) for i in range(group_count)]
        )

    send, gain_first = lax.optimization_barrier((send, gain_turned))
    received = exchange(send)
    near = range(1, group_count // 2 + 1)
    far = range(group_count // 2 + 1, group_count)
    part = facets * 3 // 4
    early = [turn_gains(gain_first, k) for k in near]
    early += [turn_gains(gain_first[:part], k) for k in far]
    below = lax.ppermute(gain_first, "tm", [(i, i + 1) for i in range(time_count - 1)])
    base = received.reshape(n, lines * LANES)[:, (taps + 1) * cap : (taps + 2) * cap]
    base = jnp.clip(base.T.astype(i32), 0, tiles - 2) * terms
    slot_lines = n * cap * planes // LANES
    block_count = n * cap // LANES
    values, weights = pl.pallas_call(
        functools.partial(degrid_kernel, n, cap, taps),
        out_shape=(
            jax.ShapeDtypeStruct((slot_lines, LANES), f32),
            jax.ShapeDtypeStruct((n * cap, 2 * LANES), f32),
        ),
        in_specs=[SMEM, VMEM, ANY],
        out_specs=(VMEM, ANY),
        scratch_shapes=[
            pltpu.VMEM((terms * tiles, facets, LANES), f32),
            pltpu.VMEM((terms * tiles, facets, LANES), f32),
            pltpu.VMEM((n * cap, 2 * LANES), f32),
            pltpu.VMEM((lines * LANES, n), f32),
            pltpu.VMEM((block_count, planes, LANES), f32),
            pltpu.SemaphoreType.DMA((pairs + 1,)),
        ],
        compiler_params=params(),
        cost_estimate=cost(10**8, 7 * 10**7),
        name="degrid",
    )(base, received, sky)
    back = exchange(values)
    gain_late, below, *early = lax.optimization_barrier((gain_first, below, *early))
    late = [turn_gains(gain_late[part:], k) for k in far]
    above = lax.ppermute(gain_late, "tm", [(i + 1, i) for i in range(time_count - 1)])
    gathered = [gain_turned, *early, *late]

    vis_wide = jnp.pad(visibilities, ((0, 0), (0, 0), (0, half - channels))).reshape(
        rows, wide
    )
    partial_shape = jax.ShapeDtypeStruct((facets, 2, group, channels), f32)
    outs = pl.pallas_call(
        functools.partial(rows_kernel, n, cap, group_count),
        out_shape=(partial_shape,) * group_count
        + (jax.ShapeDtypeStruct((slot_lines, LANES), f32),),
        in_specs=[VMEM] * (4 + len(gathered)),
        out_specs=(VMEM,) * (group_count + 1),
        scratch_shapes=[
            pltpu.VMEM((facets, stations, wide), f32),
            pltpu.VMEM((facets, 3 * planes, wide), bf16),
            pltpu.VMEM((facets, rows, wide), f32),
            pltpu.VMEM((facets, rows, wide), f32),
            pltpu.VMEM((facets, rows, wide), f32),
            pltpu.VMEM((facets, rows, wide), f32),
            pltpu.VMEM((rows, wide), f32),
            pltpu.VMEM((2 * rows, wide), bf16),
            pltpu.VMEM((2 * rows, wide), bf16),
            pltpu.VMEM((rows, wide), bf16),
            pltpu.VMEM((rows, wide), bf16),
        ],
        compiler_params=params(52),
        cost_estimate=cost(2 * 10**10, 10**7),
        name="rowgrads",
    )(row_table, col_table, vis_wide, back, *gathered)

    own, *parts, send_grad = outs
    when = lax.axis_index("tm")
    prior = jnp.where(when > 0, gain_turned - below, 0.0)
    prior = prior - jnp.where(when < time_count - 1, above - gain_turned, 0.0)
    own = own + smoothness * prior
    got, own = lax.optimization_barrier((exchange(send_grad), own))
    parts = [turn_gains(part, -k) for k, part in enumerate(parts, 1)]
    grid = pl.pallas_call(
        functools.partial(scatter_kernel, n, cap),
        out_shape=jax.ShapeDtypeStruct((pairs, terms * tiles, LANES), f32),
        in_specs=[SMEM, VMEM, VMEM],
        out_specs=ANY,
        scratch_shapes=[
            pltpu.VMEM((terms * tiles, facets, LANES), f32),
            pltpu.VMEM((terms * tiles, facets, LANES), f32),
            pltpu.VMEM((block_count, planes, LANES), f32),
            pltpu.SemaphoreType.DMA((pairs,)),
        ],
        compiler_params=params(40),
        cost_estimate=cost(0, 10**5),
        name="scatter",
    )(base, got, weights)
    grid, *parts = lax.optimization_barrier((grid, *parts))
    for part in parts:
        own = own + part
    grid_gradient = (
        grid.reshape(pairs, tiles, terms, LANES)
        .transpose(0, 2, 1, 3)
        .reshape(sky_grid.shape)
    )
    gain_gradient = own.transpose(2, 0, 1, 3)[None]
    return (gain_gradient, grid_gradient)


def solution(mesh):
    return jax.shard_map(
        body,
        mesh=mesh,
        in_specs=(
            P(("tm", "bl"), None, None),
            P(("tm", "bl")),
            P(("tm", "bl")),
            P(None, ("tm", "bl")),
            P(("tm", "bl"), None),
            P(("tm", "bl")),
            P(None, ("tm", "bl")),
            P("tm", "bl", None, None, None),
            P(None, None, None, ("tm", "bl")),
        ),
        out_specs=(P("tm", "bl", None, None, None), P(None, None, None, ("tm", "bl"))),
        check_vma=False,
    )
```

```python
import functools

import jax
import jax.numpy as jnp
from jax import lax
from jax.experimental import pallas as pl
from jax.experimental.pallas import tpu as pltpu
from jax.sharding import PartitionSpec as P

smoothness = 4.0
LANES = 128
f32 = jnp.float32
bf16 = jnp.bfloat16
i32 = jnp.int32
VMEM = pl.BlockSpec(memory_space=pltpu.VMEM)
SMEM = pl.BlockSpec(memory_space=pltpu.SMEM)
ANY = pl.BlockSpec(memory_space=pl.ANY)
CHUNK = 16
PAIR = 2


def iota(shape, dim):
    return lax.broadcasted_iota(i32, shape, dim)


def as_bf16(mask):
    return jnp.where(mask, 1.0, 0.0).astype(bf16)


def split(x, pieces):
    out = []
    for _ in range(pieces - 1):
        head = x.astype(bf16)
        out.append(head)
        x = x - head.astype(f32)
    out.append(x.astype(bf16))
    return out


def mm(a, b):
    return jnp.dot(a, b, preferred_element_type=f32)


def mm_nt(a, b):
    return lax.dot_general(a, b, (((1,), (1,)), ((), ())), preferred_element_type=f32)


def div(x, k):
    return x >> (k.bit_length() - 1) if k & (k - 1) == 0 else x // k


def mod(x, k):
    return x & (k - 1) if k & (k - 1) == 0 else x - x // k * k


def params(mib=60):
    return pltpu.CompilerParams(vmem_limit_bytes=mib << 20)


def cost(flops, byte_count):
    return pl.CostEstimate(flops=flops, bytes_accessed=byte_count, transcendentals=0)


def read_wide(ref, count):
    per = ref.shape[0] // count
    return jnp.concatenate(
        [ref[pl.ds(i, count, stride=per), :] for i in range(per)], axis=1
    )


def write_wide(ref, value):
    count = value.shape[0]
    per = ref.shape[0] // count
    for i in range(per):
        ref[pl.ds(i, count, stride=per), :] = value[:, i * LANES : (i + 1) * LANES]


def slots_kernel(
    n, cap, tiles, group, group_count,
    shift_ref, owner_ref, offset_ref, taps_ref, pairs_ref, noise_ref, keep_ref,
    send_ref, rows_ref, cols_ref,
):
    rows = owner_ref.shape[1]
    taps = taps_ref.shape[0]
    width = send_ref.shape[0] // n * LANES
    owner = owner_ref[...]
    hit = iota((n, rows), 0) == owner
    onehot = as_bf16(hit)
    earlier = as_bf16(iota((rows, rows), 0) < iota((rows, rows), 1))
    before = mm(onehot, earlier)
    rank = jnp.sum(jnp.where(hit, before, 0.0), axis=0, keepdims=True)
    at_rank = iota((cap, rows), 0) == rank.astype(i32)
    offset = offset_ref[...]
    base = jnp.minimum(offset // LANES, tiles - 2)
    low = offset - base * LANES
    fields = [taps_ref[k : k + 1, :] for k in range(taps)]
    fields += [low.astype(f32), base.astype(f32)]
    parts = [jnp.where(at_rank, v, 0.0) for v in fields]
    spare = width - len(parts) * cap
    if spare:
        parts.append(jnp.zeros((spare, rows), f32))
    total = None
    for piece in split(jnp.concatenate(parts, axis=0), 3):
        term = mm_nt(onehot, piece)
        total = term if total is None else total + term
    write_wide(send_ref, total)
    station = pairs_ref[...]
    turn = shift_ref[0] - station // group + group_count
    turn = jnp.where(turn >= group_count, turn - group_count, turn)
    local = (turn * group + (station - station // group * group)).astype(f32)
    scale = noise_ref[...] * keep_ref[...].astype(f32)
    table = jnp.concatenate(
        [owner.astype(f32), rank, local, scale, jnp.zeros((3, rows), f32)], axis=0
    )
    rows_ref[...] = table
    cols_ref[...] = table.T


def turn_fields(n, cap, count, recv_ref, turn_s):
    per_block = LANES // n
    turn_s[...] = read_wide(recv_ref, n).T
    return [
        jnp.concatenate(
            [
                turn_s[pl.ds(k * cap + q, cap // per_block, stride=per_block), :]
                for q in range(per_block)
            ],
            axis=1,
        )
        for k in range(count)
    ]


def each_slot(n, visit, carry, jb, group):
    per_block = LANES // n
    unroll = min(n, 32)
    for q in range(per_block):
        j = jb * per_block + q

        def step(g, inner):
            first = g * unroll
            for u in range(0, unroll, group):
                slots = [(j, first + v, q * n + first + v) for v in range(u, u + group)]
                inner = visit(inner, slots)
            return inner

        if n == unroll:
            carry = step(0, carry)
        else:
            carry = lax.fori_loop(0, n // unroll, step, carry)
    return carry


def degrid_kernel(
    n, cap, taps,
    base_ref, recv_ref, sky_ref, out_ref, w_ref,
    held_re, held_im, w_s, turn_s, blocks, sem,
):
    halves = (held_re, held_im)
    facets = held_re.shape[1]
    planes = 4 * facets
    copies = []
    for x, held in enumerate(halves):
        mine = []
        for f in range(facets):
            i = x * facets + f
            copy = pltpu.make_async_copy(sky_ref.at[i], held.at[:, f], sem.at[i])
            copy.start()
            mine.append(copy)
        copies.append(mine)
    per_block = LANES // n
    block_count = cap // per_block
    fields = turn_fields(n, cap, taps + 1, recv_ref, turn_s)
    line = iota((2 * LANES, LANES), 0).astype(f32)
    for jb in range(block_count):
        place = line - fields[taps][jb : jb + 1, :]
        w = jnp.zeros((2 * LANES, LANES), f32)
        for k in range(taps):
            w = jnp.where(place == float(k), fields[k][jb : jb + 1, :], w)
        w_s[jb * LANES : (jb + 1) * LANES, :] = w.T
    save = pltpu.make_async_copy(w_s, w_ref, sem.at[2 * facets])
    save.start()
    lane3 = iota((2, facets, LANES), 2)
    for x, held in enumerate(halves):
        for copy in copies[x]:
            copy.wait()
        rows_of = []

        def visit(acc, slots):
            ((j, src, lane),) = slots
            w = rows_of[0][pl.ds(lane, 1), :]
            window = held[pl.ds(base_ref[j, src], 4)]
            prod = window[0:2] * w[:, :LANES] + window[2:4] * w[:, LANES:]
            return jnp.where(
                lane3 == lane, jnp.sum(prod, axis=2, keepdims=True), acc
            )

        def block(jb, carry):
            rows_of[:] = [w_s.at[pl.ds(pl.multiple_of(jb * LANES, LANES), LANES), :]]
            acc = each_slot(n, visit, jnp.zeros((2, facets, LANES), f32), jb, 1)
            for t in range(2):
                blocks[jb, pl.ds((2 * t + x) * facets, facets), :] = acc[t]
            return carry

        lax.fori_loop(0, block_count, block, 0)
    turned = [blocks[jb].T for jb in range(block_count)]
    pieces = []
    for j in range(cap):
        jb, lo = j * n // LANES, j * n % LANES
        pieces.append(turned[jb][lo : lo + n, :planes])
    per_line = LANES // planes
    per = cap // per_line
    for i in range(per):
        wide_line = jnp.concatenate(pieces[i * per_line : (i + 1) * per_line], axis=1)
        out_ref[pl.ds(i, n, stride=per), :] = wide_line
    save.wait()


def rows_kernel(
    n, cap, group_count,
    rows_ref, cols_ref, vis_ref, back_ref, *rest,
):
    gain_refs, rest = rest[:group_count], rest[group_count:]
    out_refs, send_ref, rest = rest[:group_count], rest[group_count], rest[group_count + 1 :]
    gains, spec, a_s, b_s, m_s, p_s, e_s, glr_hi, glr_lo, gm_hi, gm_lo = rest
    facets, _, group, channels = gain_refs[0].shape
    rows = cols_ref.shape[0]
    stations = group * group_count
    planes = 4 * facets
    pairs = 2 * facets
    half = m_s.shape[2] // 2
    wide = 2 * half
    cols = cols_ref[...]
    owner_col, rank_col = cols[:, 0:1].astype(i32), cols[:, 1:2].astype(i32)
    first_col, second_col = cols[:, 2:3].astype(i32), cols[:, 3:4].astype(i32)

    gains[...] = jnp.zeros(gains.shape, f32)
    for k in range(group_count):
        mine = slice(k * group, (k + 1) * group)
        for f in range(facets):
            for x in range(2):
                gains[f, mine, x * half : x * half + channels] = gain_refs[k][f, x]

    owner3 = as_bf16(mod(iota((1, 3 * n), 1), n) == owner_col)
    per_line = LANES // planes
    line_count = cap // per_line
    slot_of = div(iota((1, LANES), 1), planes) - rank_col
    degrid = jnp.zeros((rows, LANES), f32)
    for i in range(line_count):
        line = jnp.concatenate(split(back_ref[pl.ds(i, n, stride=line_count), :], 3), axis=0)
        degrid = degrid + jnp.where(slot_of == -i * per_line, mm(owner3, line), 0.0)
    fold = as_bf16(mod(iota((3 * LANES, planes), 0), planes) == iota((3 * LANES, planes), 1))
    degrid = mm(jnp.concatenate(split(degrid, 3), axis=1), fold)
    term_scale = jnp.where(iota((1, planes), 1) >= pairs, 1.0 / (channels - 1), 1.0)
    d3 = jnp.concatenate(split(degrid * term_scale, 3), axis=1)

    lane_st = mod(iota((1, 3 * stations), 1), stations)
    first3 = as_bf16(lane_st == first_col)
    second3 = as_bf16(lane_st == second_col)
    plane = mod(iota((3 * planes, wide), 0), planes)
    lane_w = iota((3 * planes, wide), 1)
    chan = jnp.where(lane_w >= half, lane_w - half, lane_w)
    side = jnp.where(lane_w >= half, 1, 0)
    value = jnp.where(plane >= pairs, 2 * chan - (channels - 1), 1).astype(f32)
    live = (chan < channels) & (div(mod(plane, pairs), facets) == side)
    value = jnp.where(live, value, 0.0)
    facet_of = mod(plane, facets)
    chunks = [pl.ds(i * CHUNK, CHUNK) for i in range(rows // CHUNK)]

    def gather(f):
        table = jnp.concatenate(split(gains[f], 3), axis=0)
        spec[f] = jnp.where(facet_of == f, value, 0.0).astype(bf16)
        a_s[f] = mm(first3, table)
        b_s[f] = mm(second3, table)
        m_s[f] = mm(d3, spec[f])

    def load(f, at):
        return (
            a_s[f, at, :half], a_s[f, at, half:],
            b_s[f, at, :half], b_s[f, at, half:],
            m_s[f, at, :half], m_s[f, at, half:],
        )

    def predict(f):
        for at in chunks:
            a_re, a_im, b_re, b_im, m_re, m_im = load(f, at)
            p_re = a_re * b_re + a_im * b_im
            p_im = a_im * b_re - a_re * b_im
            p_s[f, at, :half] = p_re
            p_s[f, at, half:] = p_im
            e_s[at, :half] += p_re * m_re - p_im * m_im
            e_s[at, half:] += p_re * m_im + p_im * m_re

    e_s[...] = -vis_ref[...].astype(f32)
    gather(0)

    for f in range(facets):
        if f + 1 < facets:
            gather(f + 1)
        predict(f)
    e_s[...] = e_s[...] * cols[:, 4:5]

    block = min(rows, 128)
    block_count = rows // block
    station_row = iota((stations, rows), 0)
    to_first = as_bf16(station_row == rows_ref[2:3, :].astype(i32))
    to_second = as_bf16(station_row == rows_ref[3:4, :].astype(i32))
    to_station = []
    for c in range(block_count):
        part = slice(c * block, (c + 1) * block)
        to_station.append(jnp.concatenate([to_first[:, part], to_second[:, part]], axis=1))

    def put(hi_ref, lo_ref, at, lanes, value):
        hi = value.astype(bf16)
        hi_ref[at, lanes] = hi
        lo_ref[at, lanes] = (value - hi.astype(f32)).astype(bf16)

    re_lanes, im_lanes = slice(0, half), slice(half, wide)

    def vector_part(f, c, i):
        at = pl.ds(c * block + i * CHUNK, CHUNK)
        left = pl.ds(2 * c * block + i * CHUNK, CHUNK)
        right = pl.ds((2 * c + 1) * block + i * CHUNK, CHUNK)
        e_re, e_im = e_s[at, :half], e_s[at, half:]
        a_re, a_im, b_re, b_im, m_re, m_im = load(f, at)
        p_re, p_im = p_s[f, at, :half], p_s[f, at, half:]
        t_re = e_re * m_re + e_im * m_im
        t_im = e_im * m_re - e_re * m_im
        put(glr_hi, glr_lo, left, re_lanes, t_re * b_re - t_im * b_im)
        put(glr_hi, glr_lo, left, im_lanes, t_re * b_im + t_im * b_re)
        put(glr_hi, glr_lo, right, re_lanes, t_re * a_re + t_im * a_im)
        put(glr_hi, glr_lo, right, im_lanes, t_re * a_im - t_im * a_re)
        put(gm_hi, gm_lo, at, re_lanes, e_re * p_re + e_im * p_im)
        put(gm_hi, gm_lo, at, im_lanes, e_im * p_re - e_re * p_im)

    def matmul_parts(f, c, sums, parts):
        both = pl.ds(2 * c * block, 2 * block)
        here = pl.ds(c * block, block)

        def station(x, ref):
            def run():
                term = mm(to_station[c], ref[both, x * half : (x + 1) * half])
                sums[x] = term if sums[x] is None else sums[x] + term

            return run

        def plane_sum(ref):
            def run():
                term = mm_nt(ref[here, :], spec[f, :planes, :])
                parts[c] = term if parts[c] is None else parts[c] + term

            return run

        return [
            station(0, glr_hi), station(1, glr_hi), station(0, glr_lo),
            station(1, glr_lo), plane_sum(gm_hi), plane_sum(gm_lo),
        ]

    def grads(f, grad_degrid):
        sums, parts, waiting = [None, None], [None] * block_count, []
        for c in range(block_count):
            for i in range(block // CHUNK):
                vector_part(f, c, i)
                if waiting:
                    waiting.pop(0)()
            for run in waiting:
                run()
            waiting = matmul_parts(f, c, sums, parts)
        for run in waiting:
            run()
        for k in range(group_count):
            for x in range(2):
                out_refs[k][f, x] = sums[x][k * group : (k + 1) * group, :channels]
        return grad_degrid + jnp.concatenate(parts, axis=0)

    grad_degrid = lax.fori_loop(0, facets, grads, jnp.zeros((rows, planes), f32))
    grad3 = jnp.concatenate(split(grad_degrid * term_scale, 3), axis=1)
    spread = as_bf16(
        mod(iota((3 * planes, LANES), 0), planes) == mod(iota((3 * planes, LANES), 1), planes)
    )
    heads = [h.astype(f32) for h in split(mm(grad3, spread), 2)]
    owner_rows = as_bf16(iota((n, rows), 0) == rows_ref[0:1, :].astype(i32))
    for i in range(line_count):
        here = slot_of == -i * per_line
        placed = jnp.concatenate(
            [jnp.where(here, h, 0.0).astype(bf16) for h in heads], axis=1
        )
        total = mm(owner_rows, placed)
        send_ref[pl.ds(i, n, stride=line_count), :] = total[:, :LANES] + total[:, LANES:]


def scatter_kernel(
    n, cap, base_ref, grad_ref, w_ref, out_ref, held_re, held_im, blocks, sem
):
    halves = (held_re, held_im)
    facets = held_re.shape[1]
    planes = 4 * facets
    fill = 64

    def clear(i, carry):
        for held in halves:
            held[pl.ds(i * fill, fill)] = jnp.zeros((fill, facets, LANES), f32)
        return carry

    lax.fori_loop(0, held_re.shape[0] // fill, clear, 0)
    per_line = LANES // planes
    per = cap // per_line
    pieces = []
    for i in range(per):
        line = grad_ref[pl.ds(i, n, stride=per), :]
        for q in range(per_line):
            pieces.append(line[:, q * planes : (q + 1) * planes])
    per_block = LANES // n
    block_count = cap // per_block
    for jb in range(block_count):
        mine = pieces[jb * per_block : (jb + 1) * per_block]
        joined = mine[0] if per_block == 1 else jnp.concatenate(mine, axis=0)
        blocks[jb] = joined.T
    lane3 = iota((2, facets, LANES), 2)
    copies = []
    for x, held in enumerate(halves):

        def block(jb, carry):
            w_rows = w_ref.at[pl.ds(pl.multiple_of(jb * LANES, LANES), LANES), :]
            values = jnp.stack(
                [blocks[jb, pl.ds((2 * t + x) * facets, facets), :] for t in range(2)]
            )

            def visit(inner, slots):
                starts, windows, adds = [], [], []
                for j, src, lane in slots:
                    starts.append(base_ref[j, src])
                    windows.append(held[pl.ds(starts[-1], 4)])
                for at, (j, src, lane) in enumerate(slots):
                    w = w_rows[pl.ds(lane, 1), :]
                    low, high = w[:, :LANES], w[:, LANES:]
                    value = jnp.sum(
                        jnp.where(lane3 == lane, values, 0.0), axis=2, keepdims=True
                    )
                    window = windows[at] + jnp.concatenate(
                        [value * low, value * high], axis=0
                    )
                    for start, early_value, early_low, early_high in adds:
                        same = jnp.where(start == starts[at], 1.0, 0.0)
                        after = jnp.where(start + 2 == starts[at], 1.0, 0.0)
                        before = jnp.where(start == starts[at] + 2, 1.0, 0.0)
                        shared_low = early_low * same + early_high * after
                        shared_high = early_high * same + early_low * before
                        window = window + jnp.concatenate(
                            [early_value * shared_low, early_value * shared_high], axis=0
                        )
                    windows[at] = window
                    adds.append((starts[at], value, low, high))
                for start, window in zip(starts, windows):
                    held[pl.ds(start, 4)] = window
                return inner

            return each_slot(n, visit, carry, jb, PAIR)

        lax.fori_loop(0, block_count, block, 0)
        for f in range(facets):
            i = x * facets + f
            copy = pltpu.make_async_copy(held.at[:, f], out_ref.at[i], sem.at[i])
            copy.start()
            copies.append(copy)
    for copy in copies:
        copy.wait()


def body(
    visibilities,
    noise_weight,
    keep_flag,
    station_pairs,
    tile_owner,
    tile_offset,
    kernel_taps,
    gain_field,
    sky_grid,
):
    rows, _, channels = visibilities.shape
    taps = kernel_taps.shape[0]
    time_count = lax.axis_size("tm")
    group_count = lax.axis_size("bl")
    n = time_count * group_count
    cap = max(2, 2 * rows // n)
    _, facets, terms, cells = sky_grid.shape
    pairs = 2 * facets
    planes = pairs * terms
    tiles = cells // LANES
    group = gain_field.shape[1]
    stations = group * group_count
    both = ("tm", "bl")
    half = -(-channels // LANES) * LANES
    wide = 2 * half

    gain_turned = gain_field[0].transpose(1, 2, 0, 3)
    fields = taps + 2
    lines = 1 << (-(-fields * cap // LANES) - 1).bit_length()
    shift = jnp.full((1,), lax.axis_index("bl"), i32)
    send, row_table, col_table = pl.pallas_call(
        functools.partial(slots_kernel, n, cap, tiles, group, group_count),
        out_shape=(
            jax.ShapeDtypeStruct((n * lines, LANES), f32),
            jax.ShapeDtypeStruct((8, rows), f32),
            jax.ShapeDtypeStruct((rows, 8), f32),
        ),
        in_specs=[SMEM] + [VMEM] * 6,
        out_specs=(VMEM,) * 3,
        compiler_params=params(),
        cost_estimate=cost(10**9, 10**6),
        name="slots",
    )(
        shift,
        tile_owner.reshape(1, rows),
        tile_offset.reshape(1, rows),
        kernel_taps,
        station_pairs,
        noise_weight.reshape(1, rows),
        keep_flag.reshape(1, rows),
    )

    def exchange(x):
        x = x.reshape(n, -1, LANES)
        x = lax.all_to_all(x, both, split_axis=0, concat_axis=0, tiled=True)
        return x.reshape(-1, LANES)

    sky = (
        sky_grid.reshape(pairs, terms, tiles, LANES)
        .transpose(0, 2, 1, 3)
        .reshape(pairs, terms * tiles, LANES)
    )
    def turn_gains(x, k):
        return lax.ppermute(
            x, "bl", [(i, (i + k) % group_count) for i in range(group_count)]
        )

    send, gain_first = lax.optimization_barrier((send, gain_turned))
    received = exchange(send)
    near = range(1, group_count // 2 + 1)
    far = range(group_count // 2 + 1, group_count)
    early = [turn_gains(gain_first, k) for k in near]
    below = lax.ppermute(gain_first, "tm", [(i, i + 1) for i in range(time_count - 1)])
    base = received.reshape(n, lines * LANES)[:, (taps + 1) * cap : (taps + 2) * cap]
    base = jnp.clip(base.T.astype(i32), 0, tiles - 2) * terms
    slot_lines = n * cap * planes // LANES
    block_count = n * cap // LANES
    values, weights = pl.pallas_call(
        functools.partial(degrid_kernel, n, cap, taps),
        out_shape=(
            jax.ShapeDtypeStruct((slot_lines, LANES), f32),
            jax.ShapeDtypeStruct((n * cap, 2 * LANES), f32),
        ),
        in_specs=[SMEM, VMEM, ANY],
        out_specs=(VMEM, ANY),
        scratch_shapes=[
            pltpu.VMEM((terms * tiles, facets, LANES), f32),
            pltpu.VMEM((terms * tiles, facets, LANES), f32),
            pltpu.VMEM((n * cap, 2 * LANES), f32),
            pltpu.VMEM((lines * LANES, n), f32),
            pltpu.VMEM((block_count, planes, LANES), f32),
            pltpu.SemaphoreType.DMA((pairs + 1,)),
        ],
        compiler_params=params(),
        cost_estimate=cost(10**8, 7 * 10**7),
        name="degrid",
    )(base, received, sky)
    back = exchange(values)
    gain_late, below, *early = lax.optimization_barrier((gain_first, below, *early))
    late = [turn_gains(gain_late, k) for k in far]
    above = lax.ppermute(gain_late, "tm", [(i + 1, i) for i in range(time_count - 1)])
    gathered = [gain_turned, *early, *late]

    vis_wide = jnp.pad(visibilities, ((0, 0), (0, 0), (0, half - channels))).reshape(
        rows, wide
    )
    partial_shape = jax.ShapeDtypeStruct((facets, 2, group, channels), f32)
    outs = pl.pallas_call(
        functools.partial(rows_kernel, n, cap, group_count),
        out_shape=(partial_shape,) * group_count
        + (jax.ShapeDtypeStruct((slot_lines, LANES), f32),),
        in_specs=[VMEM] * (4 + len(gathered)),
        out_specs=(VMEM,) * (group_count + 1),
        scratch_shapes=[
            pltpu.VMEM((facets, stations, wide), f32),
            pltpu.VMEM((facets, 3 * planes, wide), bf16),
            pltpu.VMEM((facets, rows, wide), f32),
            pltpu.VMEM((facets, rows, wide), f32),
            pltpu.VMEM((facets, rows, wide), f32),
            pltpu.VMEM((facets, rows, wide), f32),
            pltpu.VMEM((rows, wide), f32),
            pltpu.VMEM((2 * rows, wide), bf16),
            pltpu.VMEM((2 * rows, wide), bf16),
            pltpu.VMEM((rows, wide), bf16),
            pltpu.VMEM((rows, wide), bf16),
        ],
        compiler_params=params(52),
        cost_estimate=cost(2 * 10**10, 10**7),
        name="rowgrads",
    )(row_table, col_table, vis_wide, back, *gathered)

    own, *parts, send_grad = outs
    when = lax.axis_index("tm")
    prior = jnp.where(when > 0, gain_turned - below, 0.0)
    prior = prior - jnp.where(when < time_count - 1, above - gain_turned, 0.0)
    own = own + smoothness * prior
    got, own = lax.optimization_barrier((exchange(send_grad), own))
    parts = [turn_gains(part, -k) for k, part in enumerate(parts, 1)]
    grid = pl.pallas_call(
        functools.partial(scatter_kernel, n, cap),
        out_shape=jax.ShapeDtypeStruct((pairs, terms * tiles, LANES), f32),
        in_specs=[SMEM, VMEM, VMEM],
        out_specs=ANY,
        scratch_shapes=[
            pltpu.VMEM((terms * tiles, facets, LANES), f32),
            pltpu.VMEM((terms * tiles, facets, LANES), f32),
            pltpu.VMEM((block_count, planes, LANES), f32),
            pltpu.SemaphoreType.DMA((pairs,)),
        ],
        compiler_params=params(40),
        cost_estimate=cost(0, 10**5),
        name="scatter",
    )(base, got, weights)
    grid, *parts = lax.optimization_barrier((grid, *parts))
    for part in parts:
        own = own + part
    grid_gradient = (
        grid.reshape(pairs, tiles, terms, LANES)
        .transpose(0, 2, 1, 3)
        .reshape(sky_grid.shape)
    )
    gain_gradient = own.transpose(2, 0, 1, 3)[None]
    return (gain_gradient, grid_gradient)


def solution(mesh):
    return jax.shard_map(
        body,
        mesh=mesh,
        in_specs=(
            P(("tm", "bl"), None, None),
            P(("tm", "bl")),
            P(("tm", "bl")),
            P(None, ("tm", "bl")),
            P(("tm", "bl"), None),
            P(("tm", "bl")),
            P(None, ("tm", "bl")),
            P("tm", "bl", None, None, None),
            P(None, None, None, ("tm", "bl")),
        ),
        out_specs=(P("tm", "bl", None, None, None), P(None, None, None, ("tm", "bl"))),
        check_vma=False,
    )
```
